32 devices in a mesh: nodes: 32 (over z, y, x, core).
Axes of the slice: x: 2, y: 2, z: 4, core: 2. Of those that a mesh axis runs over, the one named last changes fastest.
Arguments:
- node_table: float32 [307200, 400], P('nodes'), may hold values from -6 to 6
- batch_nodes: int32 [65536], P('nodes'), may hold values from 0 to 307199, as said below
- send_counts: int32 [32, 32], P('nodes'), may hold values from 1 to 64, as said below
- labels: int32 [65536], P('nodes'), may hold values from 0 to 46
- hop_weight: float32 [4, 100, 512], replicated, may hold values from -0.625 to 0.625
- hop_gain: float32 [4, 512], replicated, may hold values from 0.5 to 1.5
- hop_shift: float32 [4, 512], replicated, may hold values from -3 to 3
- hop_slope: float32 [4, 512], replicated, may hold values from 0 to 0.5
- cat_slope: float32 [2048], replicated, may hold values from 0 to 0.5
- mid_weight: float32 [2048, 512], replicated, may hold values from -0.125 to 0.125
- mid_gain: float32 [512], replicated, may hold values from 0.5 to 1.5
- mid_shift: float32 [512], replicated, may hold values from -3 to 3
- mid_slope: float32 [512], replicated, may hold values from 0 to 0.5
- out_weight: float32 [512, 47], replicated, may hold values from -0.5 to 0.5
- out_bias: float32 [47], replicated, may hold values from -3 to 3
Outputs:
- mean_loss: float32 [], replicated
- hop_weight_grad: float32 [4, 100, 512], replicated
- hop_gain_grad: float32 [4, 512], replicated
- hop_shift_grad: float32 [4, 512], replicated
- hop_slope_grad: float32 [4, 512], replicated
- cat_slope_grad: float32 [2048], replicated
- mid_weight_grad: float32 [2048, 512], replicated
- mid_gain_grad: float32 [512], replicated
- mid_shift_grad: float32 [512], replicated
- mid_slope_grad: float32 [512], replicated
- out_weight_grad: float32 [512, 47], replicated
- out_bias_grad: float32 [47], replicated
The draws below stay inside these ranges and needn't reach their ends.
Inputs may be any that keep to these rules, and one draw needn't show every extreme that they name: `batch_nodes`: the slot at position (s * 32 + d) * 64 + k names a node of owner d, between d * 9600 and (d + 1) * 9600 - 1; only slots with k < send_counts[s, d] belong to the batch. `send_counts`: in every draw one owner, drawn from the seed, has 64 live slots from every device.
All inputs are finite; a program needn't handle non-finite values.
Results may differ from the reference program's by a relative error of at most 0.0003.
Values sent between devices are 32-bit elements; how exact they have to be, the bound alone decides.
A program may use at most 192 MiB of HBM per device.

```python
import jax
import jax.numpy as jnp
from jax import lax

F = 100
H = 512
MID = 512
CLASSES = 47
HOPS = 4
NODE_DEV = 9600
CAP = 64
BATCH = 65536
NODES = 307200
N_NODES = 32


def draw_batch_nodes(key, part):
    key = jax.random.fold_in(key, 7)
    slot_index = jnp.arange(BATCH, dtype=jnp.int32)
    owner = slot_index // CAP % N_NODES
    offset = jax.random.randint(key, (BATCH,), 0, NODE_DEV, dtype=jnp.int32)
    offset = offset.at[0].set(0).at[BATCH - 1].set(NODE_DEV - 1)
    return (owner * NODE_DEV + offset).astype(jnp.int32)


def draw_send_counts(key, part):
    key = jax.random.fold_in(key, 11)
    first_key, second_key = jax.random.split(key)
    lowest = max(1, CAP - CAP // 4 - 1)
    drawn = jax.random.randint(first_key, (N_NODES, N_NODES), lowest, CAP + 1, dtype=jnp.int32)
    column = jax.random.randint(second_key, (), 0, N_NODES, dtype=jnp.int32)
    full_column = jnp.arange(N_NODES, dtype=jnp.int32)[None, :] == column
    return jnp.where(full_column, CAP, drawn).astype(jnp.int32)


def place_ends(values, own_key, low, top_value):
    shape = values.shape
    index_at = [jax.random.randint(jax.random.fold_in(own_key, axis), (), 0, shape[axis]) for axis in range(len(shape))]
    values = values.at[tuple(index_at)].set(low)
    longest = shape.index(max(shape))
    index_at[longest] = (index_at[longest] + 1) % shape[longest]
    return values.at[tuple(index_at)].set(top_value)


def level_of(key, shape, cuts, least, top_value):
    gain = 1.0
    for axis_at, parts in cuts:
        steps = jax.random.uniform(jax.random.fold_in(jax.random.fold_in(key, 6), axis_at), (parts,), jnp.float32, least / len(cuts), top_value / len(cuts))
        gain = gain * jnp.repeat(jnp.exp(steps), shape[axis_at] // parts).reshape((-1,) + (1,) * (len(shape) - 1 - axis_at))
    return gain


def normal_values(stream_key, extent, scale, limit, cuts=(), kind=jnp.bfloat16):
    loudness = level_of(stream_key, extent, cuts, -0.22, 0.18) if cuts else 1.0
    result = jax.random.normal(stream_key, extent, jnp.float32) * scale * loudness
    return jnp.minimum(jnp.maximum(result, -limit), limit).astype(kind)


def setup_inputs(seed: int = 0) -> dict:
    splits = jax.random.split(jax.random.key(seed), 16)
    node_table = normal_values(splits[0], (NODES, HOPS * F), 1.0, 6.0, ((0, 32),), jnp.float32)
    batch_nodes = draw_batch_nodes(jax.random.fold_in(splits[15], 71), 0)
    send_counts = draw_send_counts(jax.random.fold_in(splits[15], 71), 0)
    labels = place_ends(jax.random.randint(splits[3], (BATCH,), 0, CLASSES), jax.random.fold_in(splits[3], 1), 0, CLASSES - 1).astype(jnp.int32)
    hop_weight = normal_values(splits[4], (HOPS, F, H), F ** -0.5, 0.625, (), jnp.float32)
    hop_gain = jnp.clip(1.0 + 0.1 * jax.random.normal(splits[5], (HOPS, H), jnp.float32), 0.5, 1.5)
    hop_shift = normal_values(splits[6], (HOPS, H), 0.5, 3.0, (), jnp.float32)
    hop_slope = jnp.clip(jax.random.uniform(splits[7], (HOPS, H), jnp.float32, 0.0, 0.5), 0.0, 0.5)
    cat_slope = jnp.clip(jax.random.uniform(splits[8], (HOPS * H,), jnp.float32, 0.0, 0.5), 0.0, 0.5)
    mid_weight = normal_values(splits[9], (HOPS * H, MID), (HOPS * H) ** -0.5, 0.125, (), jnp.float32)
    mid_gain = jnp.clip(1.0 + 0.1 * jax.random.normal(splits[10], (MID,), jnp.float32), 0.5, 1.5)
    mid_shift = normal_values(splits[11], (MID,), 0.5, 3.0, (), jnp.float32)
    mid_slope = jnp.clip(jax.random.uniform(splits[12], (MID,), jnp.float32, 0.0, 0.5), 0.0, 0.5)
    out_weight = normal_values(splits[13], (MID, CLASSES), (MID // 4) ** -0.5, 0.5, (), jnp.float32)
    out_bias = normal_values(splits[14], (CLASSES,), 0.5, 3.0, (), jnp.float32)
    return dict(node_table=node_table, batch_nodes=batch_nodes, send_counts=send_counts, labels=labels, hop_weight=hop_weight, hop_gain=hop_gain, hop_shift=hop_shift, hop_slope=hop_slope, cat_slope=cat_slope, mid_weight=mid_weight, mid_gain=mid_gain, mid_shift=mid_shift, mid_slope=mid_slope, out_weight=out_weight, out_bias=out_bias)


@jax.custom_vjp
def low(v):
    return lax.optimization_barrier(v.astype(jnp.bfloat16)).astype(jnp.float32)

@jax.custom_vjp
def low_back(v):
    return v

def low_keep(v):
    return (low(v), None)

def low_pass(kept, grad):
    return (grad,)

def back_keep(v):
    return (v, None)

def back_low(kept, grad):
    return (low(grad),)
low.defvjp(low_keep, low_pass)
low_back.defvjp(back_keep, back_low)

def smooth_prelu(values, slope_vec):
    return slope_vec * values + (1.0 - slope_vec) * jax.nn.silu(values)

def batch_norm(values, row_mask, total_rows, gain_vec, shift_vec):
    weights = row_mask[:, None]
    centre = lax.optimization_barrier(jnp.sum(weights * values, axis=0)) / total_rows
    deviation = values - centre
    spread = lax.optimization_barrier(jnp.sum(weights * deviation * deviation, axis=0)) / total_rows
    return deviation * lax.rsqrt(spread + 1e-05) * gain_vec + shift_vec

def reference(node_table, batch_nodes, send_counts, labels, hop_weight, hop_gain, hop_shift, hop_slope, cat_slope, mid_weight, mid_gain, mid_shift, mid_slope, out_weight, out_bias):
    features = jnp.take(node_table, batch_nodes, axis=0).reshape(BATCH, HOPS, F)
    slot_index = jnp.arange(CAP, dtype=jnp.int32)
    row_mask = (slot_index[None, None, :] < send_counts[:, :, None]).astype(jnp.float32).reshape(BATCH)
    total_rows = jnp.sum(row_mask)
    onehot = (labels[:, None] == jnp.arange(CLASSES, dtype=jnp.int32)[None, :]).astype(jnp.float32)

    def forward(hop_weight, hop_gain, hop_shift, hop_slope, cat_slope, mid_weight, mid_gain, mid_shift, mid_slope, out_weight, out_bias):
        hop_pre = jnp.einsum('bhf,hfo->bho', features, hop_weight, precision=lax.Precision.HIGHEST).reshape(BATCH, HOPS * H)
        hop_out = batch_norm(hop_pre, row_mask, total_rows, hop_gain.reshape(-1), hop_shift.reshape(-1))
        hop_act = smooth_prelu(hop_out, hop_slope.reshape(-1))
        cat_act = smooth_prelu(hop_act, cat_slope)
        mid_pre = jnp.dot(cat_act, mid_weight, precision=lax.Precision.HIGHEST)
        mid_act = smooth_prelu(batch_norm(mid_pre, row_mask, total_rows, mid_gain, mid_shift), mid_slope)
        logits = jnp.dot(mid_act, out_weight, precision=lax.Precision.HIGHEST) + out_bias
        log_probs = jax.nn.log_softmax(logits, axis=1)
        return -jnp.sum(row_mask * lax.optimization_barrier(jnp.sum(onehot * log_probs, axis=1))) / total_rows
    mean_loss, pullback = jax.vjp(forward, hop_weight, hop_gain, hop_shift, hop_slope, cat_slope, mid_weight, mid_gain, mid_shift, mid_slope, out_weight, out_bias)
    grad_hw, grad_hg, grad_hs, grad_hl, grad_cl, grad_mw, grad_mg, grad_ms, grad_ml, grad_ow, grad_ob = pullback(jnp.ones((), jnp.float32))
    return (mean_loss, grad_hw, grad_hg, grad_hs, grad_hl, grad_cl, grad_mw, grad_mg, grad_ms, grad_ml, grad_ow, grad_ob)
```

```python
import functools

import jax
import jax.numpy as jnp
from jax import lax
from jax.experimental import pallas as pl
from jax.experimental.pallas import tpu as pltpu
from jax.sharding import PartitionSpec as P

MESH = pl.DeviceIdType.MESH
F32, BF16 = jnp.float32, jnp.bfloat16
NN = (((1,), (0,)), ((), ()))
NT = (((1,), (1,)), ((), ()))
W = 512
WIN = 256


def win_start(hop):
    return max(hop - 1, 0) * 128


def split(values):
    high = values.astype(BF16)
    return high, (values - high.astype(F32)).astype(BF16)


def dot(a, b, dims):
    return lax.dot_general(a, b, dims, preferred_element_type=F32)


def dot3(ah, al, bh, bl, dims=NN):
    return dot(ah, bh, dims) + (dot(al, bh, dims) + dot(ah, bl, dims))


def wide(column):
    return jnp.concatenate([column] * (W // 128), axis=1)


def fold(values):
    out = values[:, 0:128]
    for tile in range(1, W // 128):
        out = out + values[:, tile * 128 : (tile + 1) * 128]
    return out


def lane_sum(values):
    return jnp.broadcast_to(jnp.sum(values, axis=1, keepdims=True), values.shape)


def to_row(column):
    return column.T[0:1, :]


def to_column(row):
    return jnp.broadcast_to(row, (128, row.shape[1])).T


def main_kernel(
    n,
    slots,
    table,
    pack,
    weights,
    mid_weight,
    gain,
    shift,
    slope,
    cat_slope,
    mid_rows,
    out_t,
    bias,
    mid_grad,
    hop_grad,
    gram,
    small,
    mid_norm,
    inv_rows,
    cat_hbm,
    tab,
    x,
    dwm,
    xh,
    xl,
    wmh,
    wml,
    pgh,
    pgl,
    cath,
    catl,
    par,
    mcol,
    acc,
    vec,
    mask,
    lab,
    delta,
    ids,
    got0,
    got1,
    got2,
    got3,
    send_sem,
    recv_sem,
    table_sem,
    load_sem,
    cat_sem,
):
    me = lax.axis_index("nodes")
    rows = slots * n
    blocks = rows // W
    feats, node_rows = table.shape
    hops = 4
    chunk = next(c for c in (512, 384, 256, 128) if node_rows % c == 0)
    chunks = node_rows // chunk
    depth = min(dwm.shape[0] // feats, chunks)

    def peer(k):
        return lax.rem(me + k, n)

    def table_copy(i, slot):
        return pltpu.make_async_copy(
            table.at[:, pl.ds(pl.multiple_of(i * chunk, 128), chunk)],
            dwm.at[pl.ds(pl.multiple_of(slot * feats, 8), feats), 0:chunk],
            table_sem.at[slot],
        )

    def exchange(buf, e, k, out):
        at = me if out else lax.rem(me + n - k, n)
        return pltpu.make_async_remote_copy(
            buf.at[me], buf.at[at], send_sem.at[e, k], recv_sem.at[e, at],
            device_id=(peer(k),), device_id_type=MESH,
        )

    def send_all(buf, e):
        @pl.loop(1, n)
        def _(k):
            exchange(buf, e, k, True).start()

    def wait_all(buf, e):
        @pl.loop(1, n)
        def _(k):
            exchange(buf, e, k, False).wait()

    def ids_copy(k, out):
        at = me if out else lax.rem(me + n - k, n)
        return pltpu.make_async_remote_copy(
            pack.at[peer(k)], got0.at[at], send_sem.at[0, k], recv_sem.at[0, at],
            device_id=(peer(k),), device_id_type=MESH,
        )

    for i in range(depth):
        table_copy(i, i).start()
    weight_load = pltpu.make_async_copy(mid_weight, x, load_sem.at[0])
    weight_load.start()

    barrier = pltpu.get_barrier_semaphore()

    @pl.loop(1, n)
    def _(k):
        pl.semaphore_signal(barrier, inc=1, device_id=(peer(k),), device_id_type=MESH)

    half_lane = lax.broadcasted_iota(jnp.int32, (W, 128), 1)
    for h in range(hops):
        here = slice(h * W, (h + 1) * W)
        par[0, here, :] = to_column(gain[h : h + 1, :])
        par[1, here, :] = to_column(shift[h : h + 1, :])
        par[2, here, :] = to_column(0.5 + 0.5 * slope[h : h + 1, :])
        par[3, here, :] = to_column(0.5 + 0.5 * cat_slope[0:1, here])
    for j in range(3):
        mcol[j] = to_column(mid_rows[j : j + 1, :])

    pl.semaphore_wait(barrier, n - 1)
    got0[me] = pack[me]

    @pl.loop(1, n)
    def _(k):
        ids_copy(k, True).start()

    @pl.loop(0, chunks)
    def _(i):
        slot = lax.rem(i, depth)
        table_copy(i, slot).wait()
        for k in range(chunk // 128):
            tab[pl.ds(pl.multiple_of(i * chunk + k * 128, 128), 128), 0:feats] = dwm[
                pl.ds(pl.multiple_of(slot * feats, 8), feats), k * 128 : (k + 1) * 128
            ].T

        @pl.when(i + depth < chunks)
        def _():
            table_copy(i + depth, slot).start()

    weight_load.wait()
    for h in range(hops):
        high, low = split(x[h * W : (h + 1) * W, :].T)
        wmh[h * W : (h + 1) * W, :] = high
        wml[h * W : (h + 1) * W, :] = low

    @pl.loop(1, n)
    def _(k):
        ids_copy(k, False).wait()

    to_smem = pltpu.make_async_copy(got0, ids, load_sem.at[1])
    to_smem.start()
    to_smem.wait()

    step = min(slots, 16)

    @pl.loop(0, n)
    def _(s):
        @pl.loop(0, slots // step)
        def _(g):
            for k in range(step):
                at = g * step + k
                x[pl.ds(s * slots + at, 1), :] = tab[pl.ds(ids[s, 0, at], 1), :]

    per = 128 // slots
    lane8 = lax.broadcasted_iota(jnp.int32, (8, 128), 1)

    @pl.loop(0, rows // 128)
    def _(j):
        live = jnp.zeros((8, 128), F32)
        names = jnp.zeros((8, 128), jnp.int32)
        for q in range(per):
            s = j * per + q
            mine = (lane8 >= q * slots) & (lane8 < (q + 1) * slots)
            live = live + jnp.where(
                mine & (lane8 < q * slots + ids[s, 1, 127]), 1.0, 0.0
            )
            row = jnp.broadcast_to(got0[s, 1:2, :], (8, 128))
            if q:
                row = pltpu.roll(row, q * slots, 1)
            names = jnp.where(mine, row, names)
        at = pl.ds(pl.multiple_of(j * 128, 128), 128)
        mask[0:1, at] = live[0:1, :]
        lab[0:1, at] = names[0:1, :]

    here_count = jnp.broadcast_to(
        jnp.sum(mask[...], axis=1, keepdims=True), (1, 128)
    )
    acc[0] = jnp.zeros((W, 128), F32)
    top_row = lax.broadcasted_iota(jnp.int32, (128, W), 0)

    @pl.loop(0, blocks)
    def _(b):
        at = pl.ds(pl.multiple_of(b * W, W), W)
        live = mask[0:1, at]
        for f in range(4):
            block = x[at, f * 128 : (f + 1) * 128].T
            if (f + 1) * 128 > feats:
                block = jnp.where(top_row < feats - f * 128, block, 0.0)
            tab[pl.ds(pl.multiple_of(b * W + f * 128, 128), 128), :] = block
            acc[0, f * 128 : (f + 1) * 128, :] += fold(block * live)

    mean_here = lane_sum(acc[0]) / here_count

    @pl.loop(0, blocks)
    def _(b):
        at = pl.ds(pl.multiple_of(b * W, W), W)
        live = mask[0:1, at]
        high, low = split((tab[at, :] - wide(mean_here)) * live)
        xh[:, at] = high
        xl[:, at] = low

    def pre_at(h, b):
        return pl.ds(pl.multiple_of((h * blocks + b) * W, W), W)

    for h in range(hops):
        wh, wl = split(weights[h * W : (h + 1) * W, :])
        window = slice(win_start(h), win_start(h) + WIN)
        acc[h] = jnp.zeros((W, 128), F32)

        @pl.loop(0, blocks)
        def _(b):
            at = pl.ds(pl.multiple_of(b * W, W), W)
            pre = dot3(wh, wl, xh[window, at], xl[window, at])
            tab[pre_at(h, b), :] = pre
            acc[h] += fold(pre * pre)

    for h in range(hops):
        row = to_row(lane_sum(acc[h]))
        if h < 3:
            got1[me, 0:1, h * W : (h + 1) * W] = row
        else:
            got1[me, 1:2, 0:W] = row
    got1[me, 1:2, W : 2 * W] = to_row(mean_here)
    got1[me, 1:2, 2 * W : 3 * W] = wide(here_count)
    send_all(got1, 1)

    for j in range(3):
        window = slice(j * 128, j * 128 + WIN)
        gram[j] = dot3(xh[window, :], xl[window, :], xh[window, :], xl[window, :], NT)

    wait_all(got1, 1)

    vec[...] = jnp.zeros_like(vec)
    delta[...] = jnp.zeros_like(delta)

    @pl.loop(0, n)
    def _(d):
        counts = got1[d, 1:2, 2 * W : 3 * W]
        vec[0:1, :] += counts
        vec[1:2, :] += counts * got1[d, 1:2, W : 2 * W]
        for h in range(3):
            vec[2 + h : 3 + h, :] += got1[d, 0:1, h * W : (h + 1) * W]
        vec[5:6, :] += got1[d, 1:2, 0:W]

    total = vec[0:1, :]
    total_lane = vec[0:1, 0:128]
    mean_row = vec[1:2, :] / total

    @pl.loop(0, n)
    def _(d):
        counts = got1[d, 1:2, 2 * W : 3 * W]
        delta[pl.ds(d, 1), :] = (got1[d, 1:2, W : 2 * W] - mean_row) * jnp.sqrt(counts)

    delta[n : n + 1, :] = got1[me, 1:2, W : 2 * W] - mean_row
    span = delta.shape[0]
    span_lane = lax.broadcasted_iota(jnp.int32, (W, span), 1)
    for h in range(hops):
        here = slice(h * W, (h + 1) * W)
        wh, wl = split(weights[here, :])
        dh, dl = split(delta[:, win_start(h) : win_start(h) + WIN])
        apart = dot3(wh, wl, dh, dl, NT)
        between = jnp.sum(jnp.where(span_lane < n, apart * apart, 0.0), axis=1, keepdims=True)
        offset = jnp.sum(jnp.where(span_lane == n, apart, 0.0), axis=1, keepdims=True)
        spread = to_column(vec[2 + h : 3 + h, :]) + between
        inv = lax.rsqrt(spread / total_lane + 1e-05)
        inv_rows[h : h + 1, :] = to_row(inv)
        scale = 0.5 * par[0, here, :] * inv
        par[1, here, :] = 0.5 * par[1, here, :] + scale * offset
        par[0, here, :] = scale

    def cat_copy(h, b, slot, part):
        ref = (cath, catl)[part]
        return pltpu.make_async_copy(
            ref.at[slot], cat_hbm.at[part, h, b], cat_sem.at[part, slot]
        )

    def cat_load(h, b, slot, part):
        ref = (cath, catl)[part]
        return pltpu.make_async_copy(
            cat_hbm.at[part, h, b], ref.at[slot], cat_sem.at[part, slot]
        )

    def hop_act(h, b, slot):
        for c in range(8):
            sub = slice(c * 64, (c + 1) * 64)
            here = slice(h * W + c * 64, h * W + (c + 1) * 64)
            pre = tab[pl.ds(pl.multiple_of((h * blocks + b) * W + c * 64, 64), 64), :]
            u = pre * wide(par[0, here, :]) + wide(par[1, here, :])
            t = jnp.tanh(u)
            v = u * (t + wide(par[2, here, :]) * (1.0 - t))
            t = jnp.tanh(v)
            high, low = split((v + v) * (t + wide(par[3, here, :]) * (1.0 - t)))
            cath[slot, sub, :] = high
            catl[slot, sub, :] = low

    @pl.loop(0, blocks)
    def _(b):
        at = pl.ds(pl.multiple_of(b * W, W), W)
        for h in range(hops):
            @pl.when(b > 0)
            def _():
                for part in range(2):
                    cat_copy(h, b - 1, h, part).wait()

            hop_act(h, b, h)
            for part in range(2):
                cat_copy(h, b, h, part).start()
            here = slice(h * W, (h + 1) * W)
            part_sum = dot3(wmh[here, :], wml[here, :], cath[h], catl[h])
            if h == 0:
                x[at, :] = part_sum
            else:
                x[at, :] += part_sum

    for h in range(hops):
        for part in range(2):
            cat_copy(h, blocks - 1, h, part).wait()

    dwm[:W, 0:128] = jnp.zeros((W, 128), F32)

    @pl.loop(0, blocks)
    def _(b):
        at = pl.ds(pl.multiple_of(b * W, W), W)
        dwm[:W, 0:128] += fold(x[at, :] * mask[0:1, at])

    mean_here2 = lane_sum(dwm[:W, 0:128]) / here_count
    dwm[:W, 128:256] = jnp.zeros((W, 128), F32)

    @pl.loop(0, blocks)
    def _(b):
        at = pl.ds(pl.multiple_of(b * W, W), W)
        off = (x[at, :] - wide(mean_here2)) * mask[0:1, at]
        dwm[:W, 128:256] += fold(off * off)

    got2[me, 0:1, :] = to_row(mean_here2)
    got2[me, 1:2, :] = to_row(lane_sum(dwm[:W, 128:256]))
    send_all(got2, 2)

    stage = hops * rows
    for h in range(hops):
        load = pltpu.make_async_copy(
            mid_weight.at[h * W : (h + 1) * W, :],
            tab.at[stage : stage + W, :],
            load_sem.at[0],
        )
        load.start()
        load.wait()
        high, low = split(tab[stage : stage + W, :])
        wmh[h * W : (h + 1) * W, :] = high
        wml[h * W : (h + 1) * W, :] = low

    classes = bias.shape[1]
    kinds = 48
    dwm[0:kinds, :] = jnp.zeros((kinds, W), F32)
    dwm[0:classes, :] = out_t[...]
    oh, ol = split(dwm[0:kinds, :])
    nh, nl = split(dwm[0:kinds, :].T)
    vec[6:7, :] = jnp.zeros((1, W), F32)
    vec[6:7, 0:classes] = bias[...]
    bias_col = wide(to_column(vec[6:7, 0:128])[0:kinds, :])

    wait_all(got2, 2)
    vec[2:6, :] = jnp.zeros((4, W), F32)

    @pl.loop(0, n)
    def _(d):
        vec[2:3, :] += got2[d, 0:1, :] * got1[d, 1:2, 2 * W : 3 * W]
        vec[3:4, :] += got2[d, 1:2, :]

    mean2 = vec[2:3, :] / total

    @pl.loop(0, n)
    def _(d):
        off = got2[d, 0:1, :] - mean2
        vec[3:4, :] += off * off * got1[d, 1:2, 2 * W : 3 * W]

    inv2 = lax.rsqrt(vec[3:4, :] / total + 1e-05)
    mcol[3] = to_column(mean2)
    mcol[4] = to_column(inv2)
    mcol[2] = 0.5 + 0.5 * mcol[2]

    for j in range(4):
        acc[j] = jnp.zeros((W, 128), F32)
    small[...] = jnp.zeros_like(small)
    kind = lax.broadcasted_iota(jnp.int32, (kinds, W), 0)

    @pl.loop(0, blocks)
    def _(b):
        at = pl.ds(pl.multiple_of(b * W, W), W)
        live = mask[0:1, at]
        normed = (x[at, :] - wide(mcol[3])) * wide(mcol[4])
        v = 0.5 * (normed * wide(mcol[0]) + wide(mcol[1]))
        t = jnp.tanh(v)
        keep = wide(mcol[2])
        rest = 1.0 - t
        ah, al = split((v + v) * (t + keep * rest))
        q = v * rest
        logits = dot3(oh, ol, ah, al) + bias_col
        logits = jnp.where(kind < classes, logits, -1e30)
        top = jnp.max(logits, axis=0, keepdims=True)
        e = jnp.exp(logits - top)
        norm = jnp.sum(e, axis=0, keepdims=True)
        logp = logits - top - jnp.log(norm)
        hit = kind == lab[0:1, at]
        loss = jnp.sum(jnp.where(hit, logp, 0.0), axis=0, keepdims=True) * live
        back = (e / norm - jnp.where(hit, 1.0, 0.0)) * (live / total)
        bh, bl = split(back)
        small[0:kinds, :] += dot3(bh, bl, ah, al, NT)
        small[49:50, :] -= loss
        acc[3, 0:kinds, :] += fold(back)
        grad = dot3(nh, nl, bh, bl)
        acc[0] += fold(grad * q)
        m = t + q + q * t
        grad = grad * (m + keep * (1.0 - m))
        dwm[at, :] = grad
        acc[1] += fold(grad)
        acc[2] += fold(grad * normed)

    small[48:49, :] = to_row(lane_sum(acc[0]))
    small[50:51, 0:128] = to_row(lane_sum(acc[3])[0:128, :])
    got3[me, 0:1, :] = to_row(lane_sum(acc[1]))
    got3[me, 1:2, :] = to_row(lane_sum(acc[2]))
    send_all(got3, 3)
    wait_all(got3, 3)
    vec[2:4, :] = jnp.zeros((2, W), F32)

    @pl.loop(0, n)
    def _(d):
        vec[2:4, :] += got3[d]

    mid_norm[...] = vec[2:4, :]
    shift_part = to_column(vec[2:3, :] / total)
    gain_part = to_column(vec[3:4, :] / total)
    factor = mcol[0] * mcol[4]

    @pl.loop(0, blocks)
    def _(b):
        at = pl.ds(pl.multiple_of(b * W, W), W)
        normed = (x[at, :] - wide(mcol[3])) * wide(mcol[4])
        grad = dwm[at, :] - wide(shift_part) - normed * wide(gain_part)
        high, low = split(grad * wide(factor) * mask[0:1, at])
        pgh[at, :] = high
        pgl[at, :] = low

    def mid_out(h):
        here = slice(h * W, (h + 1) * W)
        return pltpu.make_async_copy(dwm.at[here], mid_grad.at[here], table_sem.at[h])

    for h in range(hops):
        here = slice(h * W, (h + 1) * W)
        for part in range(2):
            cat_load(h, 0, 0, part).start()

        @pl.loop(0, blocks)
        def _(b):
            at = pl.ds(pl.multiple_of(b * W, W), W)
            slot = lax.rem(b, 2)
            for part in range(2):
                cat_load(h, b, slot, part).wait()

            @pl.when(b + 1 < blocks)
            def _():
                for part in range(2):
                    cat_load(h, b + 1, 1 - slot, part).start()

            part_sum = dot3(cath[slot], catl[slot], pgh[at, :], pgl[at, :], NT)

            @pl.when(b == 0)
            def _():
                dwm[here, :] = part_sum

            @pl.when(b > 0)
            def _():
                dwm[here, :] += part_sum

        mid_out(h).start()

    for h in range(hops):
        here = slice(h * W, (h + 1) * W)
        window = slice(win_start(h), win_start(h) + WIN)
        for j in range(3):
            acc[j] = jnp.zeros((W, 128), F32)

        @pl.loop(0, blocks)
        def _(b):
            at = pl.ds(pl.multiple_of(b * W, W), W)
            x[0:W, :] = dot3(wmh[here, :], wml[here, :], pgh[at, :], pgl[at, :])
            for c in range(8):
                sub = slice(c * 64, (c + 1) * 64)
                col = slice(h * W + c * 64, h * W + (c + 1) * 64)
                grad = x[sub, :]
                pre = tab[pl.ds(pl.multiple_of((h * blocks + b) * W + c * 64, 64), 64), :]
                keep1, keep2 = wide(par[2, col, :]), wide(par[3, col, :])
                u = pre * wide(par[0, col, :]) + wide(par[1, col, :])
                t1 = jnp.tanh(u)
                r1 = 1.0 - t1
                v = u * (t1 + keep1 * r1)
                t2 = jnp.tanh(v)
                q = v * (1.0 - t2)
                acc[0, sub, :] += fold(grad * q)
                m = t2 + q + q * t2
                grad = grad * (m + keep2 * (1.0 - m))
                q = u * r1
                acc[1, sub, :] += fold(grad * q)
                m = t1 + q + q * t1
                grad = grad * (m + keep1 * (1.0 - m))
                acc[2, sub, :] += fold(grad)
                high, low = split(grad)
                cath[0, sub, :] = high
                catl[0, sub, :] = low
            part_sum = dot3(cath[0], catl[0], xh[window, at], xl[window, at], NT)

            @pl.when(b == 0)
            def _():
                hop_grad[here, :] = part_sum

            @pl.when(b > 0)
            def _():
                hop_grad[here, :] += part_sum

        for j in range(3):
            small[52 + 4 * j + h : 53 + 4 * j + h, :] = to_row(lane_sum(acc[j]))
        offset = jnp.broadcast_to(delta[n : n + 1, win_start(h) : win_start(h) + WIN], (8, WIN))[0:1]
        hop_grad[here, :] += jnp.concatenate([lane_sum(acc[2])] * 2, axis=1) * offset

    for h in range(hops):
        mid_out(h).wait()

    for j in range(3):
        off = jnp.broadcast_to(delta[n : n + 1, j * 128 : j * 128 + WIN], (128, WIN))
        tall = off.T
        gram[j] += jnp.concatenate([tall] * 2, axis=1) * off[0:1, :] * jnp.concatenate(
            [here_count] * 2, axis=1
        )


def on_device(
    node_table, batch_nodes, send_counts, labels, hop_weight, hop_gain, hop_shift, hop_slope,
    cat_slope, mid_weight, mid_gain, mid_shift, mid_slope, out_weight, out_bias,
):
    n = lax.axis_size("nodes")
    node_rows, feats = node_table.shape
    rows = batch_nodes.shape[0]
    slots = rows // n
    hops, width, units = hop_weight.shape
    blocks = rows // W
    classes = out_weight.shape[1]

    local = batch_nodes.reshape(n, slots) - jnp.arange(n, dtype=jnp.int32)[:, None] * node_rows
    top = jnp.pad(local, ((0, 0), (0, 128 - slots)))
    low = jnp.concatenate(
        [
            jnp.pad(labels.reshape(n, slots), ((0, 0), (0, 127 - slots))),
            send_counts.reshape(n, 1),
        ],
        axis=1,
    )
    pack = jnp.stack([top, low], axis=1)
    weights = jnp.concatenate(
        [
            jnp.pad(
                hop_weight[h].T,
                ((0, 0), (h * width - win_start(h), WIN - width - (h * width - win_start(h)))),
            )
            for h in range(hops)
        ],
        axis=0,
    )
    mid_rows = jnp.stack([mid_gain, mid_shift, mid_slope])

    vmem = pl.BlockSpec(memory_space=pltpu.VMEM)
    hbm = pl.BlockSpec(memory_space=pl.ANY)
    shape = jax.ShapeDtypeStruct
    tab_rows = max(node_rows, hops * rows + W)
    outs = pl.pallas_call(
        functools.partial(main_kernel, n, slots),
        out_shape=(
            shape((hops * units, W), F32),
            shape((hops * units, WIN), F32),
            shape((3, WIN, WIN), F32),
            shape((64, W), F32),
            shape((2, W), F32),
            shape((hops, W), F32),
            shape((2, hops, blocks, W, W), BF16),
        ),
        in_specs=[hbm, vmem, vmem, hbm] + [vmem] * 7,
        out_specs=(hbm,) + (vmem,) * 5 + (hbm,),
        scratch_shapes=[
            pltpu.VMEM((tab_rows, 512), F32),
            pltpu.VMEM((max(rows, hops * W), W), F32),
            pltpu.VMEM((max(rows, hops * W), W), F32),
            pltpu.VMEM((512, rows), BF16),
            pltpu.VMEM((512, rows), BF16),
            pltpu.VMEM((hops * W, W), BF16),
            pltpu.VMEM((hops * W, W), BF16),
            pltpu.VMEM((rows, W), BF16),
            pltpu.VMEM((rows, W), BF16),
            pltpu.VMEM((4, W, W), BF16),
            pltpu.VMEM((4, W, W), BF16),
            pltpu.VMEM((4, hops * W, 128), F32),
            pltpu.VMEM((5, W, 128), F32),
            pltpu.VMEM((4, W, 128), F32),
            pltpu.VMEM((8, W), F32),
            pltpu.VMEM((1, rows), F32),
            pltpu.VMEM((1, rows), jnp.int32),
            pltpu.VMEM((n + 8, W), F32),
            pltpu.SMEM((n, 2, 128), jnp.int32),
            pltpu.VMEM((n, 2, 128), jnp.int32),
            pltpu.VMEM((n, 2, 3 * W), F32),
            pltpu.VMEM((n, 2, W), F32),
            pltpu.VMEM((n, 2, W), F32),
            pltpu.SemaphoreType.DMA((4, n)),
            pltpu.SemaphoreType.DMA((4, n)),
            pltpu.SemaphoreType.DMA((8,)),
            pltpu.SemaphoreType.DMA((2,)),
            pltpu.SemaphoreType.DMA((2, 4)),
        ],
        compiler_params=pltpu.CompilerParams(
            collective_id=0, has_side_effects=True, vmem_limit_bytes=63 * 2**20
        ),
    )(
        node_table.T, pack, weights, mid_weight, hop_gain, hop_shift, hop_slope,
        cat_slope.reshape(1, hops * units), mid_rows, out_weight.T, out_bias.reshape(1, classes),
    )
    mid_grad, hop_raw, gram, small, mid_norm, inv_rows = outs[:6]
    total_rows = lax.psum(jnp.sum(send_counts).astype(F32), "nodes")
    mid_grad, hop_raw, gram, small = lax.psum((mid_grad, hop_raw, gram, small), "nodes")
    shift_grad = small[60:64]
    gains, weight_grads = [], []
    for h in range(hops):
        start = h * width - win_start(h)
        raw = hop_raw[h * units : (h + 1) * units, start : start + width].T
        part = gram[win_start(h) // 128, start : start + width, start : start + width]
        inv = inv_rows[h]
        weight = hop_weight[h]
        gain_grad = inv * jnp.sum(weight * raw, axis=0)
        along = jnp.dot(part, weight, precision=lax.Precision.HIGHEST) * inv
        gains.append(gain_grad)
        weight_grads.append(hop_gain[h] * inv * (raw - along * (gain_grad / total_rows)))
    return (
        jnp.sum(small[49]) / total_rows,
        jnp.stack(weight_grads),
        jnp.stack(gains),
        shift_grad,
        small[56:60],
        small[52:56].reshape(-1),
        mid_grad,
        mid_norm[1],
        mid_norm[0],
        small[48],
        small[0:classes].T,
        small[50, 0:classes],
    )


def solution(mesh):
    placed = (P("nodes", None), P("nodes"), P("nodes", None), P("nodes")) + (P(),) * 11
    return jax.shard_map(
        on_device, mesh=mesh, in_specs=placed, out_specs=(P(),) * 12, check_vma=False
    )
```

```python
import functools

import jax
import jax.numpy as jnp
from jax import lax
from jax.experimental import pallas as pl
from jax.experimental.pallas import tpu as pltpu
from jax.sharding import PartitionSpec as P

MESH = pl.DeviceIdType.MESH
F32, BF16 = jnp.float32, jnp.bfloat16
NN = (((1,), (0,)), ((), ()))
NT = (((1,), (1,)), ((), ()))
W = 512
WIN = 256


def win_start(hop):
    return max(hop - 1, 0) * 128


def split(values):
    high = values.astype(BF16)
    return high, (values - high.astype(F32)).astype(BF16)


def dot(a, b, dims):
    return lax.dot_general(a, b, dims, preferred_element_type=F32)


def dot3(ah, al, bh, bl, dims=NN):
    return dot(ah, bh, dims) + (dot(al, bh, dims) + dot(ah, bl, dims))


def wide(column):
    return jnp.concatenate([column] * (W // 128), axis=1)


def fold(values):
    out = values[:, 0:128]
    for tile in range(1, W // 128):
        out = out + values[:, tile * 128 : (tile + 1) * 128]
    return out


def lane_sum(values):
    return jnp.broadcast_to(jnp.sum(values, axis=1, keepdims=True), values.shape)


def to_row(column):
    return column.T[0:1, :]


def to_column(row):
    return jnp.broadcast_to(row, (128, row.shape[1])).T


def main_kernel(
    n,
    slots,
    table,
    nodes,
    labels,
    counts,
    weights,
    mid_weight,
    gain,
    shift,
    slope,
    cat_slope,
    mid_gain,
    mid_shift,
    mid_slope,
    out_t,
    bias,
    mid_sum,
    rest_sum,
    stats,
    cat_hbm,
    tab,
    x,
    dwm,
    xh,
    xl,
    wmh,
    wml,
    pgh,
    pgl,
    cath,
    catl,
    par,
    mcol,
    acc,
    vec,
    mask,
    lab,
    delta,
    ext,
    hop_grad,
    ids,
    pack,
    got0,
    got1,
    got2,
    got3,
    send_sem,
    recv_sem,
    sum_send,
    sum_recv,
    credit,
    freed,
    table_sem,
    load_sem,
    cat_sem,
):
    me = lax.axis_index("nodes")
    rows = slots * n
    blocks = rows // W
    feats, node_rows = table.shape
    hops = 4
    chunk = next(c for c in (512, 384, 256, 128) if node_rows % c == 0)
    chunks = node_rows // chunk
    depth = min(dwm.shape[0] // feats, chunks)

    def peer(k):
        return lax.rem(me + k, n)

    def table_copy(i, slot):
        return pltpu.make_async_copy(
            table.at[:, pl.ds(pl.multiple_of(i * chunk, 128), chunk)],
            dwm.at[pl.ds(pl.multiple_of(slot * feats, 8), feats), 0:chunk],
            table_sem.at[slot],
        )

    def exchange(buf, e, k, out):
        at = me if out else lax.rem(me + n - k, n)
        return pltpu.make_async_remote_copy(
            buf.at[me], buf.at[at], send_sem.at[e, k], recv_sem.at[e, at],
            device_id=(peer(k),), device_id_type=MESH,
        )

    def send_all(buf, e):
        @pl.loop(1, n)
        def _(k):
            exchange(buf, e, k, True).start()

    def wait_all(buf, e):
        @pl.loop(1, n)
        def _(k):
            exchange(buf, e, k, False).wait()

    def ids_copy(k, out):
        at = me if out else lax.rem(me + n - k, n)
        return pltpu.make_async_remote_copy(
            pack.at[peer(k)], got0.at[at], send_sem.at[0, k], recv_sem.at[0, at],
            device_id=(peer(k),), device_id_type=MESH,
        )

    for i in range(depth):
        table_copy(i, i).start()
    weight_load = pltpu.make_async_copy(mid_weight, x, load_sem.at[0])
    weight_load.start()

    barrier = pltpu.get_barrier_semaphore()

    @pl.loop(1, n)
    def _(k):
        pl.semaphore_signal(barrier, inc=1, device_id=(peer(k),), device_id_type=MESH)

    ext[...] = jnp.zeros_like(ext)
    for h in range(hops):
        here = slice(h * W, (h + 1) * W)
        par[0, here, :] = to_column(gain[h : h + 1, :])
        par[1, here, :] = to_column(shift[h : h + 1, :])
        par[2, here, :] = to_column(0.5 + 0.5 * slope[h : h + 1, :])
        par[3, here, :] = to_column(0.5 + 0.5 * cat_slope[0:1, here])
    for j, row in enumerate((mid_gain, mid_shift, mid_slope)):
        mcol[j] = to_column(row[...])

    per = 128 // slots
    lane8 = lax.broadcasted_iota(jnp.int32, (8, 128), 1)

    @pl.loop(0, rows // 128)
    def _(j):
        own = jnp.broadcast_to(nodes[pl.ds(j, 1), :], (8, 128))
        names = jnp.broadcast_to(labels[pl.ds(j, 1), :], (8, 128))
        for q in range(per):
            d = j * per + q
            turn = (128 - q * slots) % 128
            ids_row = pltpu.roll(own, turn, 1) if q else own
            names_row = pltpu.roll(names, turn, 1) if q else names
            names_row = jnp.where(lane8 == 127, counts[0, d], names_row)
            place_row = jnp.clip(ids_row - d * node_rows, 0, node_rows - 1)
            pack[d, 0:1, :] = place_row[0:1, :]
            pack[d, 1:2, :] = names_row[0:1, :]

    pl.semaphore_wait(barrier, n - 1)
    got0[me] = pack[me]

    @pl.loop(1, n)
    def _(k):
        ids_copy(k, True).start()

    @pl.loop(0, chunks)
    def _(i):
        slot = lax.rem(i, depth)
        table_copy(i, slot).wait()
        for k in range(chunk // 128):
            tab[pl.ds(pl.multiple_of(i * chunk + k * 128, 128), 128), 0:feats] = dwm[
                pl.ds(pl.multiple_of(slot * feats, 8), feats), k * 128 : (k + 1) * 128
            ].T

        @pl.when(i + depth < chunks)
        def _():
            table_copy(i + depth, slot).start()

    width = weights.shape[0]
    for h in range(hops):
        start = h * width - win_start(h)
        ext[0:WIN, :] = jnp.zeros((WIN, W), F32)
        ext[start : start + width, :] = weights[:, h, :]
        high, low = split(ext[0:WIN, :].T)
        pgh[h * W : (h + 1) * W, 0:WIN] = high
        pgh[h * W : (h + 1) * W, WIN : 2 * WIN] = low

    weight_load.wait()
    for h in range(hops):
        high, low = split(x[h * W : (h + 1) * W, :].T)
        wmh[h * W : (h + 1) * W, :] = high
        wml[h * W : (h + 1) * W, :] = low

    @pl.loop(1, n)
    def _(k):
        ids_copy(k, False).wait()

    to_smem = pltpu.make_async_copy(got0, ids, load_sem.at[1])
    to_smem.start()
    to_smem.wait()

    step = min(slots, 16)

    @pl.loop(0, n)
    def _(s):
        @pl.loop(0, slots // step)
        def _(g):
            for k in range(step):
                at = g * step + k
                x[pl.ds(s * slots + at, 1), :] = tab[pl.ds(ids[s, 0, at], 1), :]

    @pl.loop(0, rows // 128)
    def _(j):
        live = jnp.zeros((8, 128), F32)
        names = jnp.zeros((8, 128), jnp.int32)
        for q in range(per):
            s = j * per + q
            mine = (lane8 >= q * slots) & (lane8 < (q + 1) * slots)
            live = live + jnp.where(
                mine & (lane8 < q * slots + ids[s, 1, 127]), 1.0, 0.0
            )
            row = jnp.broadcast_to(got0[s, 1:2, :], (8, 128))
            if q:
                row = pltpu.roll(row, q * slots, 1)
            names = jnp.where(mine, row, names)
        at = pl.ds(pl.multiple_of(j * 128, 128), 128)
        mask[0:1, at] = live[0:1, :]
        lab[0:1, at] = names[0:1, :]

    here_count = jnp.broadcast_to(
        jnp.sum(mask[...], axis=1, keepdims=True), (1, 128)
    )
    acc[0] = jnp.zeros((W, 128), F32)
    top_row = lax.broadcasted_iota(jnp.int32, (128, W), 0)

    @pl.loop(0, blocks)
    def _(b):
        at = pl.ds(pl.multiple_of(b * W, W), W)
        live = mask[0:1, at]
        for f in range(4):
            block = x[at, f * 128 : (f + 1) * 128].T
            if (f + 1) * 128 > feats:
                block = jnp.where(top_row < feats - f * 128, block, 0.0)
            tab[pl.ds(pl.multiple_of(b * W + f * 128, 128), 128), :] = block
            acc[0, f * 128 : (f + 1) * 128, :] += fold(block * live)

    mean_here = lane_sum(acc[0]) / here_count

    @pl.loop(0, blocks)
    def _(b):
        at = pl.ds(pl.multiple_of(b * W, W), W)
        live = mask[0:1, at]
        high, low = split((tab[at, :] - wide(mean_here)) * live)
        xh[:, at] = high
        xl[:, at] = low

    def pre_at(h, b):
        return pl.ds(pl.multiple_of((h * blocks + b) * W, W), W)

    for h in range(hops):
        wh = pgh[h * W : (h + 1) * W, 0:WIN]
        wl = pgh[h * W : (h + 1) * W, WIN : 2 * WIN]
        window = slice(win_start(h), win_start(h) + WIN)
        acc[h] = jnp.zeros((W, 128), F32)

        @pl.loop(0, blocks)
        def _(b):
            at = pl.ds(pl.multiple_of(b * W, W), W)
            pre = dot3(wh, wl, xh[window, at], xl[window, at])
            tab[pre_at(h, b), :] = pre
            acc[h] += fold(pre * pre)

    for h in range(hops):
        row = to_row(lane_sum(acc[h]))
        if h < 3:
            got1[me, 0:1, h * W : (h + 1) * W] = row
        else:
            got1[me, 1:2, 0:W] = row
    got1[me, 1:2, W : 2 * W] = to_row(mean_here)
    got1[me, 1:2, 2 * W : 3 * W] = wide(here_count)
    send_all(got1, 1)

    for h in range(hops):
        if h != 1:
            window = slice(win_start(h), win_start(h) + WIN)
            products = dot3(xh[window, :], xl[window, :], xh[window, :], xl[window, :], NT)
        start = h * width - win_start(h)
        hop_grad[0:WIN, :] = products
        part = pltpu.roll(hop_grad[start : start + 104, :], (WIN - start) % WIN, 1)
        ext[GRAM : GRAM + 104, h * 128 : (h + 1) * 128] = part[:, 0:128]

    wait_all(got1, 1)

    vec[...] = jnp.zeros_like(vec)
    delta[...] = jnp.zeros_like(delta)

    @pl.loop(0, n)
    def _(d):
        counts = got1[d, 1:2, 2 * W : 3 * W]
        vec[0:1, :] += counts
        vec[1:2, :] += counts * got1[d, 1:2, W : 2 * W]
        for h in range(3):
            vec[2 + h : 3 + h, :] += got1[d, 0:1, h * W : (h + 1) * W]
        vec[5:6, :] += got1[d, 1:2, 0:W]

    total = vec[0:1, :]
    total_lane = vec[0:1, 0:128]
    mean_row = vec[1:2, :] / total
    stats[2:3, :] = total

    @pl.loop(0, n)
    def _(d):
        counts = got1[d, 1:2, 2 * W : 3 * W]
        delta[pl.ds(d, 1), :] = (got1[d, 1:2, W : 2 * W] - mean_row) * jnp.sqrt(counts)

    delta[n : n + 1, :] = got1[me, 1:2, W : 2 * W] - mean_row
    for h in range(hops):
        off = jnp.broadcast_to(delta[n : n + 1, :], (8, W))
        off = pltpu.roll(off, (W - h * width) % W, 1)[0:1, 0:128]
        tall = jnp.broadcast_to(off, (128, 128)).T[0:104, :]
        ext[GRAM : GRAM + 104, h * 128 : (h + 1) * 128] += tall * off * here_count
    span = delta.shape[0]
    span_lane = lax.broadcasted_iota(jnp.int32, (W, span), 1)
    for h in range(hops):
        here = slice(h * W, (h + 1) * W)
        wh, wl = pgh[here, 0:WIN], pgh[here, WIN : 2 * WIN]
        dh, dl = split(delta[:, win_start(h) : win_start(h) + WIN])
        apart = dot3(wh, wl, dh, dl, NT)
        between = jnp.sum(jnp.where(span_lane < n, apart * apart, 0.0), axis=1, keepdims=True)
        offset = jnp.sum(jnp.where(span_lane == n, apart, 0.0), axis=1, keepdims=True)
        spread = to_column(vec[2 + h : 3 + h, :]) + between
        inv = lax.rsqrt(spread / total_lane + 1e-05)
        stats[3 + h : 4 + h, :] = to_row(inv)
        scale = 0.5 * par[0, here, :] * inv
        par[1, here, :] = 0.5 * par[1, here, :] + scale * offset
        par[0, here, :] = scale

    def cat_copy(h, b, slot, part):
        ref = (cath, catl)[part]
        return pltpu.make_async_copy(
            ref.at[slot], cat_hbm.at[part, h, b], cat_sem.at[part, slot]
        )

    def cat_load(h, b, slot, part):
        ref = (cath, catl)[part]
        return pltpu.make_async_copy(
            cat_hbm.at[part, h, b], ref.at[slot], cat_sem.at[part, slot]
        )

    def hop_act(h, b, slot):
        for c in range(8):
            sub = slice(c * 64, (c + 1) * 64)
            here = slice(h * W + c * 64, h * W + (c + 1) * 64)
            pre = tab[pl.ds(pl.multiple_of((h * blocks + b) * W + c * 64, 64), 64), :]
            u = pre * wide(par[0, here, :]) + wide(par[1, here, :])
            t = jnp.tanh(u)
            v = u * (t + wide(par[2, here, :]) * (1.0 - t))
            t = jnp.tanh(v)
            high, low = split((v + v) * (t + wide(par[3, here, :]) * (1.0 - t)))
            cath[slot, sub, :] = high
            catl[slot, sub, :] = low

    @pl.loop(0, blocks)
    def _(b):
        at = pl.ds(pl.multiple_of(b * W, W), W)
        for h in range(hops):
            @pl.when(b > 0)
            def _():
                for part in range(2):
                    cat_copy(h, b - 1, h, part).wait()

            hop_act(h, b, h)
            for part in range(2):
                cat_copy(h, b, h, part).start()
            here = slice(h * W, (h + 1) * W)
            part_sum = dot3(wmh[here, :], wml[here, :], cath[h], catl[h])
            if h == 0:
                x[at, :] = part_sum
            else:
                x[at, :] += part_sum

    for h in range(hops):
        for part in range(2):
            cat_copy(h, blocks - 1, h, part).wait()

    dwm[:W, 0:128] = jnp.zeros((W, 128), F32)

    @pl.loop(0, blocks)
    def _(b):
        at = pl.ds(pl.multiple_of(b * W, W), W)
        dwm[:W, 0:128] += fold(x[at, :] * mask[0:1, at])

    mean_here2 = lane_sum(dwm[:W, 0:128]) / here_count
    dwm[:W, 128:256] = jnp.zeros((W, 128), F32)

    @pl.loop(0, blocks)
    def _(b):
        at = pl.ds(pl.multiple_of(b * W, W), W)
        off = (x[at, :] - wide(mean_here2)) * mask[0:1, at]
        dwm[:W, 128:256] += fold(off * off)

    got2[me, 0:1, :] = to_row(mean_here2)
    got2[me, 1:2, :] = to_row(lane_sum(dwm[:W, 128:256]))
    send_all(got2, 2)

    stage = hops * rows
    for h in range(hops):
        load = pltpu.make_async_copy(
            mid_weight.at[h * W : (h + 1) * W, :],
            tab.at[stage : stage + W, :],
            load_sem.at[0],
        )
        load.start()
        load.wait()
        high, low = split(tab[stage : stage + W, :])
        wmh[h * W : (h + 1) * W, :] = high
        wml[h * W : (h + 1) * W, :] = low

    classes = bias.shape[1]
    kinds = 48
    dwm[0:kinds, :] = jnp.zeros((kinds, W), F32)
    dwm[0:classes, :] = out_t[...]
    oh, ol = split(dwm[0:kinds, :])
    nh, nl = split(dwm[0:kinds, :].T)
    vec[6:7, :] = jnp.zeros((1, W), F32)
    vec[6:7, 0:classes] = bias[...]
    bias_col = wide(to_column(vec[6:7, 0:128])[0:kinds, :])

    wait_all(got2, 2)
    vec[2:6, :] = jnp.zeros((4, W), F32)

    @pl.loop(0, n)
    def _(d):
        vec[2:3, :] += got2[d, 0:1, :] * got1[d, 1:2, 2 * W : 3 * W]
        vec[3:4, :] += got2[d, 1:2, :]

    mean2 = vec[2:3, :] / total

    @pl.loop(0, n)
    def _(d):
        off = got2[d, 0:1, :] - mean2
        vec[3:4, :] += off * off * got1[d, 1:2, 2 * W : 3 * W]

    inv2 = lax.rsqrt(vec[3:4, :] / total + 1e-05)
    mcol[3] = to_column(mean2)
    mcol[4] = to_column(inv2)
    mcol[2] = 0.5 + 0.5 * mcol[2]

    for j in range(4):
        acc[j] = jnp.zeros((W, 128), F32)
    ext[SMALL : SMALL + 64, :] = jnp.zeros((64, W), F32)
    kind = lax.broadcasted_iota(jnp.int32, (kinds, W), 0)

    @pl.loop(0, blocks)
    def _(b):
        at = pl.ds(pl.multiple_of(b * W, W), W)
        live = mask[0:1, at]
        normed = (x[at, :] - wide(mcol[3])) * wide(mcol[4])
        v = 0.5 * (normed * wide(mcol[0]) + wide(mcol[1]))
        t = jnp.tanh(v)
        keep = wide(mcol[2])
        rest = 1.0 - t
        ah, al = split((v + v) * (t + keep * rest))
        q = v * rest
        logits = dot3(oh, ol, ah, al) + bias_col
        logits = jnp.where(kind < classes, logits, -1e30)
        top = jnp.max(logits, axis=0, keepdims=True)
        e = jnp.exp(logits - top)
        norm = jnp.sum(e, axis=0, keepdims=True)
        logp = logits - top - jnp.log(norm)
        hit = kind == lab[0:1, at]
        loss = jnp.sum(jnp.where(hit, logp, 0.0), axis=0, keepdims=True) * live
        back = (e / norm - jnp.where(hit, 1.0, 0.0)) * (live / total)
        bh, bl = split(back)
        ext[SMALL : SMALL + kinds, :] += dot3(bh, bl, ah, al, NT)
        ext[SMALL + 49 : SMALL + 50, :] -= loss
        acc[3, 0:kinds, :] += fold(back)
        grad = dot3(nh, nl, bh, bl)
        acc[0] += fold(grad * q)
        m = t + q + q * t
        grad = grad * (m + keep * (1.0 - m))
        dwm[at, :] = grad
        acc[1] += fold(grad)
        acc[2] += fold(grad * normed)

    ext[SMALL + 48 : SMALL + 49, :] = to_row(lane_sum(acc[0]))
    ext[SMALL + 50 : SMALL + 51, 0:128] = to_row(lane_sum(acc[3])[0:128, :])
    got3[me, 0:1, :] = to_row(lane_sum(acc[1]))
    got3[me, 1:2, :] = to_row(lane_sum(acc[2]))
    send_all(got3, 3)
    wait_all(got3, 3)
    vec[2:4, :] = jnp.zeros((2, W), F32)

    @pl.loop(0, n)
    def _(d):
        vec[2:4, :] += got3[d]

    stats[0:2, :] = vec[2:4, :]
    shift_part = to_column(vec[2:3, :] / total)
    gain_part = to_column(vec[3:4, :] / total)
    factor = mcol[0] * mcol[4]

    @pl.loop(0, blocks)
    def _(b):
        at = pl.ds(pl.multiple_of(b * W, W), W)
        normed = (x[at, :] - wide(mcol[3])) * wide(mcol[4])
        grad = dwm[at, :] - wide(shift_part) - normed * wide(gain_part)
        high, low = split(grad * wide(factor) * mask[0:1, at])
        pgh[at, :] = high
        pgl[at, :] = low

    bits = n.bit_length() - 1

    def bit_of(b):
        return lax.rem(me // (1 << b), 2)

    def across(b):
        return me + (1 << b) * (1 - 2 * bit_of(b))

    for b in range(bits):
        pl.semaphore_signal(credit, inc=1, device_id=(across(b),), device_id_type=MESH)

    chip_bits = list(range(1, bits))
    orders = [chip_bits[k:] + chip_bits[:k] for k in (0, 1, 2)]
    orders.append([1] + chip_bits[2:] + [2])

    def summing(batch, buf, base, size, tmp, tmp_base):
        sem = [0]

        def remote(src, dst, b):
            at = sem[0]
            sem[0] += 1
            return pltpu.make_async_remote_copy(
                src, dst, sum_send.at[batch, at], sum_recv.at[batch, at],
                device_id=(across(b),), device_id_type=MESH,
            )

        def rows_at(off, length):
            return pl.ds(pl.multiple_of(off, 8), length)

        everything = slice(0, W)
        half = size // 2
        levels = []
        at = tmp_base
        levels.append([(0, everything, base + bit_of(0) * half, base + (1 - bit_of(0)) * half, half, at)])
        at += half
        offs = [base + bit_of(0) * half] * 4
        length = half
        for j in range(bits - 1):
            length //= 2
            level = []
            for q in range(4):
                b = orders[q][j]
                keep = offs[q] + bit_of(b) * length
                give = offs[q] + (1 - bit_of(b)) * length
                level.append((b, slice(q * 128, (q + 1) * 128), keep, give, length, at))
                offs[q] = keep
            at += length
            levels.append(level)

        stages = []
        pieces = 0
        counted = []
        for level in levels:
            numbers = range(pieces, pieces + len(level))
            pieces += len(level)
            counted.append((level, numbers))
            copies = [
                remote(buf.at[rows_at(give, ln), lanes], tmp.at[t : t + ln, lanes], b)
                for b, lanes, keep, give, ln, t in level
            ]

            def start(copies=copies):
                for c in copies:
                    c.start()

            def finish(copies=copies, level=level, numbers=numbers):
                for c, (b, lanes, keep, give, ln, t), k in zip(copies, level, numbers):
                    c.wait()
                    pl.semaphore_signal(
                        freed.at[batch, k], inc=1, device_id=(across(b),), device_id_type=MESH
                    )
                    buf[rows_at(keep, ln), lanes] += tmp[t : t + ln, lanes]

            stages.append((start, finish))
        for level, numbers in counted[::-1]:
            copies = [
                remote(buf.at[rows_at(keep, ln), lanes], buf.at[rows_at(keep, ln), lanes], b)
                for b, lanes, keep, give, ln, t in level
            ]

            def start(copies=copies, numbers=numbers):
                for c, k in zip(copies, numbers):
                    pl.semaphore_wait(freed.at[batch, k], 1)
                    c.start()

            def finish(copies=copies):
                for c in copies:
                    c.wait()

            stages.append((start, finish))
        return stages

    mid_batch = max(W, 8 * n)
    batches = []
    spots = [(x, W, x.shape[0] - W), (tab, stage, tab.shape[0] - stage)]

    def place(size):
        for k, (ref, first, left) in enumerate(spots):
            if left >= size:
                spots[k] = (ref, first + size, left - size)
                return ref, first

    DW, HB, GAP = 0.8, 2.2, 3.4
    clock = [(t + 1) * DW for t in range(hops * blocks)]
    clock += [clock[-1] + (t + 1) * HB for t in range(hops * blocks)]
    per_hop = blocks
    for k in range(hops * W // mid_batch):
        ref, first = place(mid_batch)
        ready = (k + 1) * mid_batch // W * per_hop - 1
        batches.append((ready, summing(len(batches), dwm, k * mid_batch, mid_batch, ref, first)))
    for first_row, size, after in rest_batches(n):
        ref, first = place(size)
        ready = hops * per_hop + (after + 1) * per_hop - 1
        batches.append((ready, summing(len(batches), ext, first_row, size, ref, first)))

    ticks = {}
    events = []
    for k, (ready, stages) in enumerate(batches):
        when = clock[ready]
        for j in range(len(stages) + 1):
            events.append((when, k, j))
            when += GAP
    for when, k, j in sorted(events):
        tick = next((t for t, c in enumerate(clock) if c >= when - 1e-6), len(clock))
        tick = max(tick, batches[k][0])
        ticks.setdefault(tick, []).append((k, j))

    def mid_out(k):
        here = slice(k * mid_batch, (k + 1) * mid_batch)
        return pltpu.make_async_copy(dwm.at[here], mid_sum.at[here], table_sem.at[k])

    def act(tick):
        for k, j in ticks.get(tick, []):
            stages = batches[k][1]
            if j:
                stages[j - 1][1]()
            elif k == 0:
                pl.semaphore_wait(credit, bits)
            if j < len(stages):
                stages[j][0]()
            elif k < hops * W // mid_batch:
                mid_out(k).start()

    def tick_after(h, b, first):
        for t in range(blocks):
            if ticks.get(first + h * blocks + t):

                @pl.when(b == t)
                def _():
                    act(first + h * blocks + t)

    for h in range(hops):
        here = slice(h * W, (h + 1) * W)
        for part in range(2):
            cat_load(h, 0, 0, part).start()

        @pl.loop(0, blocks)
        def _(b):
            at = pl.ds(pl.multiple_of(b * W, W), W)
            slot = lax.rem(b, 2)
            for part in range(2):
                cat_load(h, b, slot, part).wait()

            @pl.when(b + 1 < blocks)
            def _():
                for part in range(2):
                    cat_load(h, b + 1, 1 - slot, part).start()

            part_sum = dot3(cath[slot], catl[slot], pgh[at, :], pgl[at, :], NT)

            @pl.when(b == 0)
            def _():
                dwm[here, :] = part_sum

            @pl.when(b > 0)
            def _():
                dwm[here, :] += part_sum

            tick_after(h, b, 0)

    for h in range(hops):
        here = slice(h * W, (h + 1) * W)
        window = slice(win_start(h), win_start(h) + WIN)
        for j in range(3):
            acc[j] = jnp.zeros((W, 128), F32)

        @pl.loop(0, blocks)
        def _(b):
            at = pl.ds(pl.multiple_of(b * W, W), W)
            x[0:W, :] = dot3(wmh[here, :], wml[here, :], pgh[at, :], pgl[at, :])
            for c in range(8):
                sub = slice(c * 64, (c + 1) * 64)
                col = slice(h * W + c * 64, h * W + (c + 1) * 64)
                grad = x[sub, :]
                pre = tab[pl.ds(pl.multiple_of((h * blocks + b) * W + c * 64, 64), 64), :]
                keep1, keep2 = wide(par[2, col, :]), wide(par[3, col, :])
                u = pre * wide(par[0, col, :]) + wide(par[1, col, :])
                t1 = jnp.tanh(u)
                r1 = 1.0 - t1
                v = u * (t1 + keep1 * r1)
                t2 = jnp.tanh(v)
                q = v * (1.0 - t2)
                acc[0, sub, :] += fold(grad * q)
                m = t2 + q + q * t2
                grad = grad * (m + keep2 * (1.0 - m))
                q = u * r1
                acc[1, sub, :] += fold(grad * q)
                m = t1 + q + q * t1
                grad = grad * (m + keep1 * (1.0 - m))
                acc[2, sub, :] += fold(grad)
                high, low = split(grad)
                cath[0, sub, :] = high
                catl[0, sub, :] = low
            part_sum = dot3(cath[0], catl[0], xh[window, at], xl[window, at], NT)

            @pl.when(b == 0)
            def _():
                hop_grad[...] = part_sum

            @pl.when(b > 0)
            def _():
                hop_grad[...] += part_sum

            @pl.when(b == blocks - 1)
            def _():
                sums = lane_sum(acc[2])
                offset = delta[n : n + 1, win_start(h) : win_start(h) + WIN]
                tall = hop_grad[...] + jnp.concatenate([sums] * 2, axis=1) * offset
                first = hop_row(n, h)
                start = h * width - win_start(h)
                x[0:WIN, :] = tall.T
                ext[first : first + width, :] = x[start : start + width, :]
                for j in range(3):
                    row = first + width + j
                    ext[row : row + 1, :] = to_row(lane_sum(acc[j]))

            tick_after(h, b, hops * blocks)

    act(len(clock))
    for k in range(hops * W // mid_batch):
        mid_out(k).wait()
    rest_out = pltpu.make_async_copy(ext, rest_sum, load_sem.at[0])
    rest_out.start()
    rest_out.wait()


GRAM, SMALL = 208, 312


def hop_row(n, h):
    if h < 2:
        return h * 104
    return SMALL + 64 if h == 2 else (512 if 8 * n <= 256 else SMALL + 168)


def rest_batches(n):
    if 8 * n <= 256:
        return [(0, 512, 2), (512, 256, 3)]
    return [(0, -(-(SMALL + 272) // (8 * n)) * 8 * n, 3)]


def rest_rows(n):
    first, size, _ = rest_batches(n)[-1]
    return first + size


def final_kernel(
    n, mid_sum, rest, stats, weights, gain, loss, hop_w, hop_g, hop_s, hop_l, cat_l, mid_w,
    mid_g, mid_s, mid_l, out_w, out_b, buf, wide_w, sem,
):
    parts = 4
    size = mid_sum.shape[0] // parts

    def load(k):
        here = slice(k * size, (k + 1) * size)
        return pltpu.make_async_copy(mid_sum.at[here], buf.at[here], sem.at[0, k])

    def store(k):
        here = slice(k * size, (k + 1) * size)
        return pltpu.make_async_copy(buf.at[here], mid_w.at[here], sem.at[1, k])

    for k in range(parts):
        load(k).start()
    total = stats[2:3, :]
    width, hops, _ = weights.shape
    wide_w[...] = jnp.zeros_like(wide_w)
    for h in range(hops):
        first = hop_row(n, h)
        raw = rest[first : first + width, :]
        weight = weights[:, h, :]
        inv = stats[3 + h : 4 + h, :]
        gain_grad = inv * jnp.sum(weight * raw, axis=0, keepdims=True)
        wide_w[0:width, :] = weight
        along = lax.dot_general(
            rest[GRAM : GRAM + 104, h * 128 : (h + 1) * 128], wide_w[...], NN,
            precision=lax.Precision.HIGHEST, preferred_element_type=F32,
        )[0:width, :]
        grad = raw - along * (inv * gain_grad / total)
        hop_w[:, h, :] = gain[h : h + 1, :] * inv * grad
        hop_g[h : h + 1, :] = gain_grad
        cat_l[0:1, h * W : (h + 1) * W] = rest[first + width : first + width + 1, :]
        hop_l[h : h + 1, :] = rest[first + width + 1 : first + width + 2, :]
        hop_s[h : h + 1, :] = rest[first + width + 2 : first + width + 3, :]
        load(h).wait()
        store(h).start()
    mid_s[...] = stats[0:1, :]
    mid_g[...] = stats[1:2, :]
    mid_l[...] = rest[SMALL + 48 : SMALL + 49, :]
    out_w[...] = rest[SMALL : SMALL + out_w.shape[0], :]
    out_b[...] = rest[SMALL + 50 : SMALL + 51, 0 : out_b.shape[1]]
    loss[...] = jnp.sum(rest[SMALL + 49 : SMALL + 50, :], axis=1, keepdims=True) / total[:, 0:1]
    for k in range(parts):
        store(k).wait()


def on_device(
    node_table, batch_nodes, send_counts, labels, hop_weight, hop_gain, hop_shift, hop_slope,
    cat_slope, mid_weight, mid_gain, mid_shift, mid_slope, out_weight, out_bias,
):
    n = lax.axis_size("nodes")
    node_rows, feats = node_table.shape
    rows = batch_nodes.shape[0]
    slots = rows // n
    hops, width, units = hop_weight.shape
    blocks = rows // W
    classes = out_weight.shape[1]
    vmem = pl.BlockSpec(memory_space=pltpu.VMEM)
    hbm = pl.BlockSpec(memory_space=pl.ANY)
    shape = jax.ShapeDtypeStruct
    bits = n.bit_length() - 1
    mid_batch = max(W, 8 * n)
    sums = hops * W // mid_batch + len(rest_batches(n))
    spill = hops * W + rest_rows(n) - (hops * W - W) // mid_batch * mid_batch
    tab_rows = max(node_rows, hops * rows + max(spill, W))
    weights = hop_weight.transpose(1, 0, 2)
    mid_sum, rest_sum, stats, _ = pl.pallas_call(
        functools.partial(main_kernel, n, slots),
        out_shape=(
            shape((hops * units, W), F32),
            shape((rest_rows(n), W), F32),
            shape((8, W), F32),
            shape((2, hops, blocks, W, W), BF16),
        ),
        in_specs=[hbm, vmem, vmem, pl.BlockSpec(memory_space=pltpu.SMEM), vmem, hbm] + [vmem] * 9,
        out_specs=(hbm, hbm, vmem, hbm),
        scratch_shapes=[
            pltpu.VMEM((tab_rows, 512), F32),
            pltpu.VMEM((max(rows, hops * W), W), F32),
            pltpu.VMEM((max(rows, hops * W), W), F32),
            pltpu.VMEM((512, rows), BF16),
            pltpu.VMEM((512, rows), BF16),
            pltpu.VMEM((hops * W, W), BF16),
            pltpu.VMEM((hops * W, W), BF16),
            pltpu.VMEM((max(rows, hops * W), W), BF16),
            pltpu.VMEM((max(rows, hops * W), W), BF16),
            pltpu.VMEM((4, W, W), BF16),
            pltpu.VMEM((4, W, W), BF16),
            pltpu.VMEM((4, hops * W, 128), F32),
            pltpu.VMEM((5, W, 128), F32),
            pltpu.VMEM((4, W, 128), F32),
            pltpu.VMEM((8, W), F32),
            pltpu.VMEM((1, rows), F32),
            pltpu.VMEM((1, rows), jnp.int32),
            pltpu.VMEM((n + 8, W), F32),
            pltpu.VMEM((rest_rows(n), W), F32),
            pltpu.VMEM((W, WIN), F32),
            pltpu.SMEM((n, 2, 128), jnp.int32),
            pltpu.VMEM((n, 2, 128), jnp.int32),
            pltpu.VMEM((n, 2, 128), jnp.int32),
            pltpu.VMEM((n, 2, 3 * W), F32),
            pltpu.VMEM((n, 2, W), F32),
            pltpu.VMEM((n, 2, W), F32),
            pltpu.SemaphoreType.DMA((4, n)),
            pltpu.SemaphoreType.DMA((4, n)),
            pltpu.SemaphoreType.DMA((sums, 8 * bits - 6)),
            pltpu.SemaphoreType.DMA((sums, 8 * bits - 6)),
            pltpu.SemaphoreType.REGULAR,
            pltpu.SemaphoreType.REGULAR((sums, 4 * bits - 3)),
            pltpu.SemaphoreType.DMA((8,)),
            pltpu.SemaphoreType.DMA((2,)),
            pltpu.SemaphoreType.DMA((2, 4)),
        ],
        compiler_params=pltpu.CompilerParams(
            collective_id=0, has_side_effects=True, vmem_limit_bytes=63 * 2**20
        ),
    )(
        node_table.T, batch_nodes.reshape(rows // 128, 128), labels.reshape(rows // 128, 128),
        send_counts, weights, mid_weight, hop_gain, hop_shift, hop_slope,
        cat_slope.reshape(1, hops * units), mid_gain.reshape(1, W), mid_shift.reshape(1, W),
        mid_slope.reshape(1, W), out_weight.T, out_bias.reshape(1, classes),
    )
    (
        loss, hop_w, hop_g, hop_s, hop_l, cat_l, mid_w, mid_g, mid_s, mid_l, out_w, out_b,
    ) = pl.pallas_call(
        functools.partial(final_kernel, n),
        out_shape=(
            shape((1, 1), F32), shape((width, hops, units), F32), shape((hops, units), F32),
            shape((hops, units), F32), shape((hops, units), F32), shape((1, hops * units), F32),
            shape((hops * units, W), F32), shape((1, W), F32), shape((1, W), F32),
            shape((1, W), F32), shape((classes, W), F32), shape((1, classes), F32),
        ),
        in_specs=[hbm] + [vmem] * 4,
        out_specs=(vmem,) * 6 + (hbm,) + (vmem,) * 5,
        scratch_shapes=[
            pltpu.VMEM((hops * units, W), F32),
            pltpu.VMEM((128, W), F32),
            pltpu.SemaphoreType.DMA((2, 4)),
        ],
        compiler_params=pltpu.CompilerParams(vmem_limit_bytes=32 * 2**20),
    )(mid_sum, rest_sum, stats, weights, hop_gain)
    return (
        loss.reshape(()), hop_w.transpose(1, 0, 2), hop_g, hop_s, hop_l, cat_l.reshape(-1),
        mid_w, mid_g.reshape(-1), mid_s.reshape(-1), mid_l.reshape(-1), out_w.T,
        out_b.reshape(-1),
    )


def solution(mesh):
    placed = (P("nodes", None), P("nodes"), P("nodes", None), P("nodes")) + (P(),) * 11
    return jax.shard_map(
        on_device, mesh=mesh, in_specs=placed, out_specs=(P(),) * 12, check_vma=False
    )
```

```python
import functools

import jax
import jax.numpy as jnp
from jax import lax
from jax.experimental import pallas as pl
from jax.experimental.pallas import tpu as pltpu
from jax.sharding import PartitionSpec as P

MESH = pl.DeviceIdType.MESH
F32, BF16 = jnp.float32, jnp.bfloat16
NN = (((1,), (0,)), ((), ()))
NT = (((1,), (1,)), ((), ()))
W = 512
WIN = 256


def win_start(hop):
    return max(hop - 1, 0) * 128


def split(values):
    high = values.astype(BF16)
    return high, (values - high.astype(F32)).astype(BF16)


def dot(a, b, dims):
    return lax.dot_general(a, b, dims, preferred_element_type=F32)


def dot3(ah, al, bh, bl, dims=NN):
    (da,), (db,) = dims[0]
    return dot(
        jnp.concatenate([ah, al, ah], da), jnp.concatenate([bh, bh, bl], db), dims
    )


def wide(column):
    return jnp.concatenate([column] * (W // 128), axis=1)


def fold(values):
    out = values[:, 0:128]
    for tile in range(1, W // 128):
        out = out + values[:, tile * 128 : (tile + 1) * 128]
    return out


def lane_sum(values):
    return jnp.broadcast_to(jnp.sum(values, axis=1, keepdims=True), values.shape)


def to_row(column):
    return column.T[0:1, :]


def to_column(row):
    return jnp.broadcast_to(row, (128, row.shape[1])).T


def main_kernel(
    n,
    slots,
    table,
    nodes,
    labels,
    counts,
    weights,
    mid_weight,
    gain,
    shift,
    slope,
    cat_slope,
    mid_gain,
    mid_shift,
    mid_slope,
    out_t,
    bias,
    mid_sum,
    rest_sum,
    stats,
    cat_hbm,
    tab,
    x,
    dwm,
    xh,
    xl,
    wmh,
    wml,
    pgh,
    pgl,
    cath,
    catl,
    par,
    mcol,
    acc,
    vec,
    mask,
    lab,
    delta,
    ext,
    res,
    own,
    hop_grad,
    cg,
    ids,
    pack,
    got0,
    got1,
    got2,
    got3,
    send_sem,
    recv_sem,
    sum_send,
    sum_recv,
    part_send,
    part_recv,
    credit,
    freed,
    table_sem,
    load_sem,
    cat_sem,
):
    me = lax.axis_index("nodes")
    rows = slots * n
    blocks = rows // W
    feats, node_rows = table.shape
    hops = 4
    chunk = next(c for c in (512, 384, 256, 128) if node_rows % c == 0)
    chunks = node_rows // chunk
    depth = min(dwm.shape[0] // feats, chunks)

    def peer(k):
        return lax.rem(me + k, n)

    def table_copy(i, slot):
        return pltpu.make_async_copy(
            table.at[:, pl.ds(pl.multiple_of(i * chunk, 128), chunk)],
            dwm.at[pl.ds(pl.multiple_of(slot * feats, 8), feats), 0:chunk],
            table_sem.at[slot],
        )

    def send_all(buf, e):
        @pl.loop(1, n)
        def _(k):
            pltpu.make_async_remote_copy(
                buf.at[me], buf.at[me], send_sem.at[e], recv_sem.at[e],
                device_id=(peer(k),), device_id_type=MESH,
            ).start()

    def wait_all(buf, e):
        others = buf.at[pl.ds(0, n - 1)]
        pltpu.make_async_copy(others, others, send_sem.at[e]).wait()
        pltpu.make_async_copy(others, others, recv_sem.at[e]).wait()

    for i in range(depth):
        table_copy(i, i).start()
    weight_load = pltpu.make_async_copy(mid_weight, x, load_sem.at[0])
    weight_load.start()

    barrier = pltpu.get_barrier_semaphore()

    @pl.loop(1, n)
    def _(k):
        pl.semaphore_signal(barrier, inc=1, device_id=(peer(k),), device_id_type=MESH)

    ext[...] = jnp.zeros_like(ext)
    for h in range(hops):
        here = slice(h * W, (h + 1) * W)
        par[0, here, :] = to_column(gain[h : h + 1, :])
        par[1, here, :] = to_column(shift[h : h + 1, :])
        par[2, here, :] = to_column(0.5 + 0.5 * slope[h : h + 1, :])
        par[3, here, :] = to_column(0.5 + 0.5 * cat_slope[0:1, here])
    for j, row in enumerate((mid_gain, mid_shift, mid_slope)):
        mcol[j] = to_column(row[...])

    per = 128 // slots
    lane8 = lax.broadcasted_iota(jnp.int32, (8, 128), 1)

    @pl.loop(0, rows // 128)
    def _(j):
        own = jnp.broadcast_to(nodes[pl.ds(j, 1), :], (8, 128))
        names = jnp.broadcast_to(labels[pl.ds(j, 1), :], (8, 128))
        for q in range(per):
            d = j * per + q
            turn = (128 - q * slots) % 128
            ids_row = pltpu.roll(own, turn, 1) if q else own
            names_row = pltpu.roll(names, turn, 1) if q else names
            names_row = jnp.where(lane8 == 127, counts[0, d], names_row)
            place_row = jnp.clip(ids_row - d * node_rows, 0, node_rows - 1)
            pack[d, 0:1, :] = place_row[0:1, :]
            pack[d, 1:2, :] = names_row[0:1, :]

    pl.semaphore_wait(barrier, n - 1)
    got0[me] = pack[me]

    @pl.loop(1, n)
    def _(k):
        pltpu.make_async_remote_copy(
            pack.at[peer(k)], got0.at[me], send_sem.at[0], recv_sem.at[0],
            device_id=(peer(k),), device_id_type=MESH,
        ).start()

    @pl.loop(0, chunks)
    def _(i):
        slot = lax.rem(i, depth)
        table_copy(i, slot).wait()
        for k in range(chunk // 128):
            tab[pl.ds(pl.multiple_of(i * chunk + k * 128, 128), 128), 0:feats] = dwm[
                pl.ds(pl.multiple_of(slot * feats, 8), feats), k * 128 : (k + 1) * 128
            ].T

        @pl.when(i + depth < chunks)
        def _():
            table_copy(i + depth, slot).start()

    plain_load = pltpu.make_async_copy(mid_weight, dwm, load_sem.at[0])
    width = weights.shape[0]
    for h in range(hops):
        start = h * width - win_start(h)
        ext[0:WIN, :] = jnp.zeros((WIN, W), F32)
        ext[start : start + width, :] = weights[:, h, :]
        high, low = split(ext[0:WIN, :].T)
        pgh[h * W : (h + 1) * W, 0:WIN] = high
        pgh[h * W : (h + 1) * W, WIN : 2 * WIN] = low

    weight_load.wait()
    for h in range(hops):
        high, low = split(x[h * W : (h + 1) * W, :].T)
        wmh[h * W : (h + 1) * W, :] = high
        wml[h * W : (h + 1) * W, :] = low
    plain_load.start()

    wait_all(got0, 0)

    to_smem = pltpu.make_async_copy(got0, ids, load_sem.at[1])
    to_smem.start()
    to_smem.wait()

    step = min(slots, 16)

    @pl.loop(0, n)
    def _(s):
        @pl.loop(0, slots // step)
        def _(g):
            for k in range(step):
                at = g * step + k
                x[pl.ds(s * slots + at, 1), :] = tab[pl.ds(ids[s, 0, at], 1), :]

    @pl.loop(0, rows // 128)
    def _(j):
        live = jnp.zeros((8, 128), F32)
        names = jnp.zeros((8, 128), jnp.int32)
        for q in range(per):
            s = j * per + q
            mine = (lane8 >= q * slots) & (lane8 < (q + 1) * slots)
            live = live + jnp.where(
                mine & (lane8 < q * slots + ids[s, 1, 127]), 1.0, 0.0
            )
            row = jnp.broadcast_to(got0[s, 1:2, :], (8, 128))
            if q:
                row = pltpu.roll(row, q * slots, 1)
            names = jnp.where(mine, row, names)
        at = pl.ds(pl.multiple_of(j * 128, 128), 128)
        mask[0:1, at] = live[0:1, :]
        lab[0:1, at] = names[0:1, :]

    here_count = jnp.broadcast_to(
        jnp.sum(mask[...], axis=1, keepdims=True), (1, 128)
    )
    acc[0] = jnp.zeros((W, 128), F32)
    top_row = lax.broadcasted_iota(jnp.int32, (128, W), 0)

    @pl.loop(0, blocks)
    def _(b):
        at = pl.ds(pl.multiple_of(b * W, W), W)
        live = mask[0:1, at]
        for f in range(4):
            block = x[at, f * 128 : (f + 1) * 128].T
            if (f + 1) * 128 > feats:
                block = jnp.where(top_row < feats - f * 128, block, 0.0)
            tab[pl.ds(pl.multiple_of(b * W + f * 128, 128), 128), :] = block
            acc[0, f * 128 : (f + 1) * 128, :] += fold(block * live)

    mean_here = lane_sum(acc[0]) / here_count

    @pl.loop(0, blocks)
    def _(b):
        at = pl.ds(pl.multiple_of(b * W, W), W)
        live = mask[0:1, at]
        high, low = split((tab[at, :] - wide(mean_here)) * live)
        xh[:, at] = high
        xl[:, at] = low

    def pre_at(h, b):
        return pl.ds(pl.multiple_of((h * blocks + b) * W, W), W)

    for h in range(hops):
        wh = pgh[h * W : (h + 1) * W, 0:WIN]
        wl = pgh[h * W : (h + 1) * W, WIN : 2 * WIN]
        window = slice(win_start(h), win_start(h) + WIN)
        acc[h] = jnp.zeros((W, 128), F32)

        @pl.loop(0, blocks)
        def _(b):
            at = pl.ds(pl.multiple_of(b * W, W), W)
            pre = dot3(wh, wl, xh[window, at], xl[window, at])
            tab[pre_at(h, b), :] = pre
            acc[h] += fold(pre * pre)

    for h in range(hops):
        row = to_row(lane_sum(acc[h]))
        if h < 3:
            got1[me, 0:1, h * W : (h + 1) * W] = row
        else:
            got1[me, 1:2, 0:W] = row
    got1[me, 1:2, W : 2 * W] = to_row(mean_here)
    got1[me, 1:2, 2 * W : 3 * W] = wide(here_count)
    send_all(got1, 1)

    for h in range(hops):
        if h != 1:
            window = slice(win_start(h), win_start(h) + WIN)
            products = dot3(xh[window, :], xl[window, :], xh[window, :], xl[window, :], NT)
        start = h * width - win_start(h)
        hop_grad[0:WIN, :] = products
        part = pltpu.roll(hop_grad[start : start + 104, :], (WIN - start) % WIN, 1)
        ext[GRAM : GRAM + 104, h * 128 : (h + 1) * 128] = part[:, 0:128]

    wait_all(got1, 1)

    delta[...] = jnp.zeros_like(delta)
    every_count = got1[:, 1:2, 2 * W : 3 * W]
    vec[0:1, :] = jnp.sum(every_count, axis=0)
    vec[1:2, :] = jnp.sum(every_count * got1[:, 1:2, W : 2 * W], axis=0)
    for h in range(3):
        vec[2 + h : 3 + h, :] = jnp.sum(got1[:, 0:1, h * W : (h + 1) * W], axis=0)
    vec[5:6, :] = jnp.sum(got1[:, 1:2, 0:W], axis=0)

    total = vec[0:1, :]
    total_lane = vec[0:1, 0:128]
    mean_row = vec[1:2, :] / total
    stats[2:3, :] = total

    @pl.loop(0, n, unroll=8)
    def _(d):
        counts = got1[d, 1:2, 2 * W : 3 * W]
        delta[pl.ds(d, 1), :] = (got1[d, 1:2, W : 2 * W] - mean_row) * jnp.sqrt(counts)

    delta[n : n + 1, :] = got1[me, 1:2, W : 2 * W] - mean_row
    for h in range(hops):
        off = jnp.broadcast_to(delta[n : n + 1, :], (8, W))
        off = pltpu.roll(off, (W - h * width) % W, 1)[0:1, 0:128]
        tall = jnp.broadcast_to(off, (128, 128)).T[0:104, :]
        ext[GRAM : GRAM + 104, h * 128 : (h + 1) * 128] += tall * off * here_count
    span = delta.shape[0]
    span_lane = lax.broadcasted_iota(jnp.int32, (W, span), 1)
    for h in range(hops):
        here = slice(h * W, (h + 1) * W)
        wh, wl = pgh[here, 0:WIN], pgh[here, WIN : 2 * WIN]
        dh, dl = split(delta[:, win_start(h) : win_start(h) + WIN])
        apart = dot3(wh, wl, dh, dl, NT)
        between = jnp.sum(jnp.where(span_lane < n, apart * apart, 0.0), axis=1, keepdims=True)
        offset = jnp.sum(jnp.where(span_lane == n, apart, 0.0), axis=1, keepdims=True)
        spread = to_column(vec[2 + h : 3 + h, :]) + between
        inv = lax.rsqrt(spread / total_lane + 1e-05)
        stats[3 + h : 4 + h, :] = to_row(inv)
        scale = 0.5 * par[0, here, :] * inv
        par[1, here, :] = 0.5 * par[1, here, :] + scale * offset
        par[0, here, :] = scale

    def cat_copy(h, b, slot, part):
        ref = (cath, catl)[part]
        return pltpu.make_async_copy(
            ref.at[slot], cat_hbm.at[part, h, b], cat_sem.at[part, slot]
        )

    def cat_load(h, b, slot, part):
        ref = (cath, catl)[part]
        return pltpu.make_async_copy(
            cat_hbm.at[part, h, b], ref.at[slot], cat_sem.at[part, slot]
        )

    def hop_act(h, b, slot):
        for c in range(8):
            sub = slice(c * 64, (c + 1) * 64)
            here = slice(h * W + c * 64, h * W + (c + 1) * 64)
            pre = tab[pl.ds(pl.multiple_of((h * blocks + b) * W + c * 64, 64), 64), :]
            u = pre * wide(par[0, here, :]) + wide(par[1, here, :])
            t = jnp.tanh(u)
            v = u * (t + wide(par[2, here, :]) * (1.0 - t))
            t = jnp.tanh(v)
            high, low = split((v + v) * (t + wide(par[3, here, :]) * (1.0 - t)))
            cath[slot, sub, :] = high
            catl[slot, sub, :] = low

    @pl.loop(0, blocks)
    def _(b):
        at = pl.ds(pl.multiple_of(b * W, W), W)
        for h in range(hops):

            @pl.when(b > 0)
            def _():
                for part in range(2):
                    cat_copy(h, b - 1, h, part).wait()

        for h in range(hops):
            hop_act(h, b, h)
            here = slice(h * W, (h + 1) * W)
            part_sum = dot3(wmh[here, :], wml[here, :], cath[h], catl[h])
            if h == 0:
                x[at, :] = part_sum
            else:
                x[at, :] += part_sum
        for h in range(hops):
            for part in range(2):
                cat_copy(h, b, h, part).start()

    for h in range(hops):
        for part in range(2):
            cat_copy(h, blocks - 1, h, part).wait()

    acc[0] = jnp.zeros((W, 128), F32)

    @pl.loop(0, blocks)
    def _(b):
        at = pl.ds(pl.multiple_of(b * W, W), W)
        acc[0] += fold(x[at, :] * mask[0:1, at])

    mean_here2 = lane_sum(acc[0]) / here_count
    acc[1] = jnp.zeros((W, 128), F32)

    @pl.loop(0, blocks)
    def _(b):
        at = pl.ds(pl.multiple_of(b * W, W), W)
        off = (x[at, :] - wide(mean_here2)) * mask[0:1, at]
        acc[1] += fold(off * off)

    got2[me, 0:1, :] = to_row(mean_here2)
    got2[me, 1:2, :] = to_row(lane_sum(acc[1]))
    send_all(got2, 2)

    plain_load.wait()
    for h in range(hops):
        high, low = split(dwm[h * W : (h + 1) * W, :])
        wmh[h * W : (h + 1) * W, :] = high
        wml[h * W : (h + 1) * W, :] = low

    classes = bias.shape[1]
    kinds = 48
    ext[SMALL : SMALL + kinds, :] = jnp.zeros((kinds, W), F32)
    ext[SMALL : SMALL + classes, :] = out_t[...]
    oh, ol = split(ext[SMALL : SMALL + kinds, :])
    nh, nl = split(ext[SMALL : SMALL + kinds, :].T)
    vec[6:7, :] = jnp.zeros((1, W), F32)
    vec[6:7, 0:classes] = bias[...]
    bias_col = wide(to_column(vec[6:7, 0:128])[0:kinds, :])

    wait_all(got2, 2)
    every_count = got1[:, 1:2, 2 * W : 3 * W]
    mean2 = jnp.sum(got2[:, 0:1, :] * every_count, axis=0) / total
    off = got2[:, 0:1, :] - mean2
    vec[3:4, :] = jnp.sum(got2[:, 1:2, :] + off * off * every_count, axis=0)
    inv2 = lax.rsqrt(vec[3:4, :] / total + 1e-05)
    mcol[3] = to_column(mean2)
    mcol[4] = to_column(inv2)
    mcol[2] = 0.5 + 0.5 * mcol[2]

    for b in range(blocks):
        for part in range(2):
            cat_load(0, b, b % 4, part).start()

    for j in range(4):
        acc[j] = jnp.zeros((W, 128), F32)
    ext[SMALL : SMALL + 64, :] = jnp.zeros((64, W), F32)
    kind = lax.broadcasted_iota(jnp.int32, (kinds, W), 0)

    @pl.loop(0, blocks)
    def _(b):
        at = pl.ds(pl.multiple_of(b * W, W), W)
        live = mask[0:1, at]
        normed = (x[at, :] - wide(mcol[3])) * wide(mcol[4])
        v = 0.5 * (normed * wide(mcol[0]) + wide(mcol[1]))
        t = jnp.tanh(v)
        keep = wide(mcol[2])
        rest = 1.0 - t
        ah, al = split((v + v) * (t + keep * rest))
        q = v * rest
        logits = dot3(oh, ol, ah, al) + bias_col
        logits = jnp.where(kind < classes, logits, -1e30)
        top = jnp.max(logits, axis=0, keepdims=True)
        e = jnp.exp(logits - top)
        norm = jnp.sum(e, axis=0, keepdims=True)
        logp = logits - top - jnp.log(norm)
        hit = kind == lab[0:1, at]
        loss = jnp.sum(jnp.where(hit, logp, 0.0), axis=0, keepdims=True) * live
        back = (e / norm - jnp.where(hit, 1.0, 0.0)) * (live / total)
        bh, bl = split(back)
        ext[SMALL : SMALL + kinds, :] += dot3(bh, bl, ah, al, NT)
        ext[SMALL + 49 : SMALL + 50, :] -= loss
        acc[3, 0:kinds, :] += fold(back)
        grad = dot3(nh, nl, bh, bl)
        acc[0] += fold(grad * q)
        m = t + q + q * t
        grad = grad * (m + keep * (1.0 - m))
        dwm[at, :] = grad
        acc[1] += fold(grad)
        acc[2] += fold(grad * normed)

    ext[SMALL + 48 : SMALL + 49, :] = to_row(lane_sum(acc[0]))
    ext[SMALL + 50 : SMALL + 51, 0:128] = to_row(lane_sum(acc[3])[0:128, :])
    got3[me, 0:1, :] = to_row(lane_sum(acc[1]))
    got3[me, 1:2, :] = to_row(lane_sum(acc[2]))
    send_all(got3, 3)
    wait_all(got3, 3)
    vec[2:4, :] = jnp.sum(got3[...], axis=0)
    stats[0:2, :] = vec[2:4, :]
    shift_part = to_column(vec[2:3, :] / total)
    gain_part = to_column(vec[3:4, :] / total)
    factor = mcol[0] * mcol[4]

    @pl.loop(0, blocks)
    def _(b):
        at = pl.ds(pl.multiple_of(b * W, W), W)
        normed = (x[at, :] - wide(mcol[3])) * wide(mcol[4])
        grad = dwm[at, :] - wide(shift_part) - normed * wide(gain_part)
        high, low = split(grad * wide(factor) * mask[0:1, at])
        pgh[at, :] = high
        pgl[at, :] = low

    bits = n.bit_length() - 1

    def bit_of(b):
        return lax.rem(me // (1 << b), 2)

    def across(b):
        return me + (1 << b) * (1 - 2 * bit_of(b))

    def remote(src, dst, send, recv, to):
        return pltpu.make_async_remote_copy(
            src, dst, send, recv, device_id=(to,), device_id_type=MESH
        )

    def wait_bytes(ref, sem):
        pltpu.make_async_copy(ref, ref, sem).wait()

    for b in range(bits):
        pl.semaphore_signal(credit, inc=1, device_id=(across(b),), device_id_type=MESH)

    far = list(range(3, bits))
    orders = [[1] + far + [2], [2] + far + [1]]
    span = W // len(orders)

    def halving(batch, base, size, take):
        def rows_at(off, length):
            return pl.ds(pl.multiple_of(off, 8), length)

        half = size // 2
        tmps = [take(half)]
        levels = [
            [(0, slice(0, W), base + bit_of(0) * half, base + (1 - bit_of(0)) * half, half, tmps[0][1])]
        ]
        rest_tmp, at = take(half)
        tmps += [(rest_tmp, at)] * (bits - 1)
        offs = [base + bit_of(0) * half] * len(orders)
        length = half
        for j in range(bits - 1):
            length //= 2
            level = []
            for q in range(len(orders)):
                b = orders[q][j]
                keep = offs[q] + bit_of(b) * length
                give = offs[q] + (1 - bit_of(b)) * length
                level.append((b, slice(q * span, (q + 1) * span), keep, give, length, at))
                offs[q] = keep
            at += length
            levels.append(level)

        stages = []
        for k, level in enumerate(levels):
            send, recv = sum_send.at[batch, k], sum_recv.at[batch, k]
            free = freed.at[batch, k]
            length, first = level[0][4:]
            tmp = tmps[k][0]
            arrived = tmp.at[first : first + length, :]

            def start(level=level, send=send, recv=recv, tmp=tmp):
                for b, lanes, keep, give, ln, t in level:
                    remote(
                        dwm.at[rows_at(give, ln), lanes], tmp.at[t : t + ln, lanes],
                        send, recv, across(b),
                    ).start()

            def finish(level=level, send=send, recv=recv, free=free, arrived=arrived, tmp=tmp):
                wait_bytes(arrived, send)
                wait_bytes(arrived, recv)
                for b, lanes, keep, give, ln, t in level:
                    pl.semaphore_signal(
                        free, inc=1, device_id=(across(b),), device_id_type=MESH
                    )
                    dwm[rows_at(keep, ln), lanes] += tmp[t : t + ln, lanes]

            stages.append((start, finish))
        for k in range(bits - 1, -1, -1):
            level = levels[k]
            send, recv = sum_send.at[batch, bits + k], sum_recv.at[batch, bits + k]
            free = freed.at[batch, k]
            length, first = level[0][4:]
            arrived = tmps[k][0].at[first : first + length, :]

            def start(level=level, send=send, recv=recv, free=free):
                pl.semaphore_wait(free, len(level))
                for b, lanes, keep, give, ln, t in level:
                    here = dwm.at[rows_at(keep, ln), lanes]
                    remote(here, here, send, recv, across(b)).start()

            def finish(send=send, recv=recv, arrived=arrived):
                wait_bytes(arrived, send)
                wait_bytes(arrived, recv)

            stages.append((start, finish))
        return stages

    chips = n // 2
    core, chip = lax.rem(me, 2), me // 2
    half_lanes = W // 2
    mine = pl.ds(pl.multiple_of(core * half_lanes, 128), half_lanes)
    other = pl.ds(pl.multiple_of((1 - core) * half_lanes, 128), half_lanes)

    def direct(batch, base, size, rows_each, tmp_base, tmp_lane):
        owners = size // rows_each
        cols = slice(tmp_lane, tmp_lane + half_lanes)
        block = pl.ds(base, size)
        from_core = tab.at[tmp_base : tmp_base + size, cols]
        first = tmp_base + size
        slot = tab.at[pl.ds(pl.multiple_of(first + chip * rows_each, 8), rows_each), cols]
        summed = own.at[batch, 0:rows_each, :]
        sends = [part_send.at[batch, k] for k in range(4)]
        recvs = [part_recv.at[batch, k] for k in range(4)]

        def many(k):
            return tab.at[first : first + rows_each * k, cols]

        def piece(q):
            return pl.ds(pl.multiple_of(base + q * rows_each, 8), rows_each)

        def start():
            remote(ext.at[block, other], from_core, sends[0], recvs[0], across(0)).start()

        def spread():
            wait_bytes(from_core, sends[0])
            wait_bytes(from_core, recvs[0])
            ext[block, mine] += tab[tmp_base : tmp_base + size, cols]

            @pl.loop(0, owners)
            def _(k):
                q = lax.rem(chip + k, owners)

                @pl.when(q == chip)
                def _():
                    pltpu.make_async_copy(ext.at[piece(q), mine], slot, recvs[1]).start()

                @pl.when(q != chip)
                def _():
                    remote(ext.at[piece(q), mine], slot, sends[1], recvs[1], q * 2 + core).start()

        def middle():
            @pl.when(chip < owners)
            def _():
                wait_bytes(many(owners - 1), sends[1])
                wait_bytes(many(chips), recvs[1])
                out = tab[first : first + rows_each, cols]
                for d in range(1, chips):
                    at = first + rows_each * d
                    out = out + tab[at : at + rows_each, cols]
                own[batch, 0:rows_each, :] = out
                there = res.at[piece(chip), mine]
                pltpu.make_async_copy(summed, there, recvs[2]).start()

                @pl.loop(1, chips)
                def _(k):
                    to = lax.rem(chip + k, chips) * 2 + core
                    remote(summed, there, sends[2], recvs[2], to).start()

            @pl.when(chip >= owners)
            def _():
                wait_bytes(many(owners), sends[1])

        def join():
            wait_bytes(res.at[block, mine], recvs[2])

            @pl.when(chip < owners)
            def _():
                wait_bytes(many(chips - 1), sends[2])

            here = res.at[block, mine]
            remote(here, here, sends[3], recvs[3], across(0)).start()

        def finish():
            wait_bytes(res.at[block, other], sends[3])
            wait_bytes(res.at[block, other], recvs[3])

        return [start, spread, middle, join, finish]

    mid_batch = max(W, 8 * n)
    mids = hops * W // mid_batch
    DW, HB, GAP = 1.0, 2.1, 4.0
    PART = (2.5, 5.0, 5.0, 2.5)
    clock = [(t + 1) * DW for t in range(hops * blocks)]
    clock += [clock[-1] + (t + 1) * HB for t in range(hops * blocks)]
    spare = hops * rows
    part_rows = 208 + 16 * chips
    spots = [(x, W, x.shape[0] - W), (tab, spare + part_rows, tab.shape[0] - spare - part_rows)]

    def take(size):
        spot = next(i for i in range(2) if spots[i][2] >= size)
        ref, first, left = spots[spot]
        spots[spot] = (ref, first + size, left - size)
        return ref, first

    events = []
    for k in range(mids):
        stages = halving(k, k * mid_batch, mid_batch, take)
        when = clock[(k + 1) * mid_batch // W * blocks - 1]
        for j in range(len(stages) + 1):
            todo = []
            if j:
                todo.append(stages[j - 1][1])
            elif k == 0:
                todo.append(lambda: pl.semaphore_wait(credit, bits))
            if j < len(stages):
                todo.append(stages[j][0])
            else:
                todo.append(lambda k=k: mid_out(k).start())
            events.append((when, len(events), todo))
            when += GAP
    ends = [clock[hops * blocks + (h + 1) * blocks - 1] for h in range(hops)]
    for batch, (when, base, size, rows_each) in enumerate(
        (
            (clock[0], 0, HOPS_AT, 16),
            (ends[1], hop_row(0), 208, 16),
            (ends[2], hop_row(2), 104, 8),
            (ends[3], hop_row(3), 104, 8),
        )
    ):
        stages = direct(batch, base, size, rows_each, spare, batch % 2 * half_lanes)
        for j, stage in enumerate(stages):
            at = when + sum(PART[:j])
            if batch == 1:
                at = min(at, ends[3] - 1e-3)
            events.append((at, len(events), [stage]))

    ticks = {}
    for when, _, todo in sorted(events, key=lambda e: e[:2]):
        tick = next((t for t, c in enumerate(clock) if c >= when - 1e-6), len(clock))
        ticks.setdefault(tick, []).extend(todo)

    def mid_out(k):
        here = slice(k * mid_batch, (k + 1) * mid_batch)
        return pltpu.make_async_copy(dwm.at[here], mid_sum.at[here], table_sem.at[k])

    def act(tick):
        for todo in ticks.get(tick, []):
            todo()

    for h in range(hops):
        here = slice(h * W, (h + 1) * W)

        @pl.loop(0, blocks)
        def _(b):
            at = pl.ds(pl.multiple_of(b * W, W), W)
            slot = lax.rem(b, 4)
            for part in range(2):
                cat_load(h, b, slot, part).wait()
            part_sum = dot3(cath[slot], catl[slot], pgh[at, :], pgl[at, :], NT)
            if h + 1 < hops:
                for part in range(2):
                    cat_load(h + 1, b, slot, part).start()

            @pl.when(b == 0)
            def _():
                dwm[here, :] = part_sum

            @pl.when(b > 0)
            def _():
                dwm[here, :] += part_sum

            for t in range(blocks):
                if ticks.get(h * blocks + t):

                    @pl.when(b == t)
                    def _():
                        act(h * blocks + t)

    grads = (x.at[0:W], cg)

    def head_back(h, b, rs):
        at = pl.ds(b * W, W)
        here = pl.ds(pl.multiple_of(h * W + rs.start, 128), rs.stop - rs.start)
        return dot3(wmh[here, :], wml[here, :], pgh[at, :], pgl[at, :])

    def weight_back(h, b, rs):
        window = pl.ds(pl.multiple_of(jnp.maximum(h - 1, 0) * 128, 128), WIN)
        at = pl.ds(b * W, W)
        part_sum = dot3(
            cath[b % 2, rs, :], catl[b % 2, rs, :], xh[window, at], xl[window, at], NT
        )
        if b == 0:
            hop_grad[rs, :] = part_sum
        else:
            hop_grad[rs, :] += part_sum

    def act_back(h, b, c):
        sub = slice(c * 64, (c + 1) * 64)
        col = pl.ds(pl.multiple_of(h * W + c * 64, 64), 64)
        grad = grads[b % 2][sub, :]
        pre = tab[pl.ds(pl.multiple_of((h * blocks + b) * W + c * 64, 64), 64), :]
        keep1, keep2 = wide(par[2, col, :]), wide(par[3, col, :])
        u = pre * wide(par[0, col, :]) + wide(par[1, col, :])
        t1 = jnp.tanh(u)
        r1 = 1.0 - t1
        v = u * (t1 + keep1 * r1)
        t2 = jnp.tanh(v)
        q = v * (1.0 - t2)
        sum2 = fold(grad * q)
        m = t2 + q + q * t2
        grad = grad * (m + keep2 * (1.0 - m))
        q = u * r1
        sum1 = fold(grad * q)
        m = t1 + q + q * t1
        grad = grad * (m + keep1 * (1.0 - m))
        for j, value in enumerate((sum2, sum1, fold(grad))):
            if b == 0:
                acc[j, sub, :] = value
            else:
                acc[j, sub, :] += value
        high, low = split(grad)
        cath[b % 2, sub, :] = high
        catl[b % 2, sub, :] = low

    halves = (slice(0, W // 2), slice(W // 2, W))
    grads[0][...] = head_back(0, 0, slice(0, W))

    @pl.loop(0, hops)
    def _(h):
        for b in range(blocks):
            for m, rs in enumerate(halves):
                if b + 1 < blocks:
                    grads[(b + 1) % 2][rs, :] = head_back(h, b + 1, rs)
                else:
                    grads[(b + 1) % 2][rs, :] = head_back(jnp.minimum(h + 1, hops - 1), 0, rs)
                if b:
                    weight_back(h, b - 1, rs)
                for c in range(4 * m, 4 * m + 4):
                    act_back(h, b, c)
            if b + 1 < blocks:
                for t in range(hops):
                    if ticks.get(hops * blocks + t * blocks + b):

                        @pl.when(h == t)
                        def _():
                            act(hops * blocks + t * blocks + b)

        weight_back(h, blocks - 1, slice(0, W))
        for t in range(hops):

            @pl.when(h == t)
            def _():
                sums = lane_sum(acc[2])
                offset = delta[n : n + 1, win_start(t) : win_start(t) + WIN]
                tall = hop_grad[...] + jnp.concatenate([sums] * 2, axis=1) * offset
                first = hop_row(t)
                start = t * width - win_start(t)
                cg[0:WIN, :] = tall.T
                ext[first : first + width, :] = cg[start : start + width, :]
                for j in range(3):
                    row = first + width + j
                    ext[row : row + 1, :] = to_row(lane_sum(acc[j]))
                act(hops * blocks + t * blocks + blocks - 1)

    act(len(clock))
    rest_out = pltpu.make_async_copy(res, rest_sum, load_sem.at[0])
    rest_out.start()
    for k in range(mids):
        mid_out(k).wait()
    rest_out.wait()


GRAM, SMALL, HOPS_AT = 0, 104, 176


def hop_row(h):
    return HOPS_AT + h * 104


def final_kernel(
    mid_sum, rest, stats, weights, gain, loss, hop_w, hop_g, hop_s, hop_l, cat_l, mid_w,
    mid_g, mid_s, mid_l, out_w, out_b, buf, wide_w, sem,
):
    parts = 4
    size = mid_sum.shape[0] // parts

    def load(k):
        here = slice(k * size, (k + 1) * size)
        return pltpu.make_async_copy(mid_sum.at[here], buf.at[here], sem.at[0, k])

    def store(k):
        here = slice(k * size, (k + 1) * size)
        return pltpu.make_async_copy(buf.at[here], mid_w.at[here], sem.at[1, k])

    for k in range(parts):
        load(k).start()
    total = stats[2:3, :]
    width, hops, _ = weights.shape
    wide_w[...] = jnp.zeros_like(wide_w)
    for h in range(hops):
        first = hop_row(h)
        raw = rest[first : first + width, :]
        weight = weights[:, h, :]
        inv = stats[3 + h : 4 + h, :]
        gain_grad = inv * jnp.sum(weight * raw, axis=0, keepdims=True)
        wide_w[0:width, :] = weight
        along = lax.dot_general(
            rest[GRAM : GRAM + 104, h * 128 : (h + 1) * 128], wide_w[...], NN,
            precision=lax.Precision.HIGHEST, preferred_element_type=F32,
        )[0:width, :]
        grad = raw - along * (inv * gain_grad / total)
        hop_w[:, h, :] = gain[h : h + 1, :] * inv * grad
        hop_g[h : h + 1, :] = gain_grad
        cat_l[0:1, h * W : (h + 1) * W] = rest[first + width : first + width + 1, :]
        hop_l[h : h + 1, :] = rest[first + width + 1 : first + width + 2, :]
        hop_s[h : h + 1, :] = rest[first + width + 2 : first + width + 3, :]
        load(h).wait()
        store(h).start()
    mid_s[...] = stats[0:1, :]
    mid_g[...] = stats[1:2, :]
    mid_l[...] = rest[SMALL + 48 : SMALL + 49, :]
    out_w[...] = rest[SMALL : SMALL + out_w.shape[0], :]
    out_b[...] = rest[SMALL + 50 : SMALL + 51, 0 : out_b.shape[1]]
    loss[...] = jnp.sum(rest[SMALL + 49 : SMALL + 50, :], axis=1, keepdims=True) / total[:, 0:1]
    for k in range(parts):
        store(k).wait()


def on_device(
    node_table, batch_nodes, send_counts, labels, hop_weight, hop_gain, hop_shift, hop_slope,
    cat_slope, mid_weight, mid_gain, mid_shift, mid_slope, out_weight, out_bias,
):
    n = lax.axis_size("nodes")
    node_rows, feats = node_table.shape
    rows = batch_nodes.shape[0]
    slots = rows // n
    hops, width, units = hop_weight.shape
    blocks = rows // W
    classes = out_weight.shape[1]
    vmem = pl.BlockSpec(memory_space=pltpu.VMEM)
    hbm = pl.BlockSpec(memory_space=pl.ANY)
    shape = jax.ShapeDtypeStruct
    bits = n.bit_length() - 1
    mid_batch = max(W, 8 * n)
    sums = hops * W // mid_batch
    small_rows = HOPS_AT + 104 * hops
    halves = 2 * sums - (hops * W - W) // (mid_batch // 2)
    spill = 208 + 8 * n + halves * mid_batch // 2
    tab_rows = max(node_rows, hops * rows + spill)
    weights = hop_weight.transpose(1, 0, 2)
    mid_sum, rest_sum, stats, _ = pl.pallas_call(
        functools.partial(main_kernel, n, slots),
        out_shape=(
            shape((hops * units, W), F32),
            shape((small_rows, W), F32),
            shape((8, W), F32),
            shape((2, hops, blocks, W, W), BF16),
        ),
        in_specs=[hbm, vmem, vmem, pl.BlockSpec(memory_space=pltpu.SMEM), vmem, hbm] + [vmem] * 9,
        out_specs=(hbm, hbm, vmem, hbm),
        scratch_shapes=[
            pltpu.VMEM((tab_rows, 512), F32),
            pltpu.VMEM((max(rows, hops * W), W), F32),
            pltpu.VMEM((max(rows, hops * W), W), F32),
            pltpu.VMEM((512, rows), BF16),
            pltpu.VMEM((512, rows), BF16),
            pltpu.VMEM((hops * W, W), BF16),
            pltpu.VMEM((hops * W, W), BF16),
            pltpu.VMEM((max(rows, hops * W), W), BF16),
            pltpu.VMEM((max(rows, hops * W), W), BF16),
            pltpu.VMEM((4, W, W), BF16),
            pltpu.VMEM((4, W, W), BF16),
            pltpu.VMEM((4, hops * W, 128), F32),
            pltpu.VMEM((5, W, 128), F32),
            pltpu.VMEM((4, W, 128), F32),
            pltpu.VMEM((8, W), F32),
            pltpu.VMEM((1, rows), F32),
            pltpu.VMEM((1, rows), jnp.int32),
            pltpu.VMEM((n + 8, W), F32),
            pltpu.VMEM((small_rows, W), F32),
            pltpu.VMEM((small_rows, W), F32),
            pltpu.VMEM((4, 16, W // 2), F32),
            pltpu.VMEM((W, WIN), F32),
            pltpu.VMEM((W, W), F32),
            pltpu.SMEM((n, 2, 128), jnp.int32),
            pltpu.VMEM((n, 2, 128), jnp.int32),
            pltpu.VMEM((n, 2, 128), jnp.int32),
            pltpu.VMEM((n, 2, 3 * W), F32),
            pltpu.VMEM((n, 2, W), F32),
            pltpu.VMEM((n, 2, W), F32),
            pltpu.SemaphoreType.DMA((4,)),
            pltpu.SemaphoreType.DMA((4,)),
            pltpu.SemaphoreType.DMA((sums, 2 * bits)),
            pltpu.SemaphoreType.DMA((sums, 2 * bits)),
            pltpu.SemaphoreType.DMA((4, 4)),
            pltpu.SemaphoreType.DMA((4, 4)),
            pltpu.SemaphoreType.REGULAR,
            pltpu.SemaphoreType.REGULAR((sums, bits)),
            pltpu.SemaphoreType.DMA((8,)),
            pltpu.SemaphoreType.DMA((2,)),
            pltpu.SemaphoreType.DMA((2, 4)),
        ],
        compiler_params=pltpu.CompilerParams(
            collective_id=0, has_side_effects=True, vmem_limit_bytes=66_900_000
        ),
    )(
        node_table.T, batch_nodes.reshape(rows // 128, 128), labels.reshape(rows // 128, 128),
        send_counts, weights, mid_weight, hop_gain, hop_shift, hop_slope,
        cat_slope.reshape(1, hops * units), mid_gain.reshape(1, W), mid_shift.reshape(1, W),
        mid_slope.reshape(1, W), out_weight.T, out_bias.reshape(1, classes),
    )
    (
        loss, hop_w, hop_g, hop_s, hop_l, cat_l, mid_w, mid_g, mid_s, mid_l, out_w, out_b,
    ) = pl.pallas_call(
        final_kernel,
        out_shape=(
            shape((1, 1), F32), shape((width, hops, units), F32), shape((hops, units), F32),
            shape((hops, units), F32), shape((hops, units), F32), shape((1, hops * units), F32),
            shape((hops * units, W), F32), shape((1, W), F32), shape((1, W), F32),
            shape((1, W), F32), shape((classes, W), F32), shape((1, classes), F32),
        ),
        in_specs=[hbm] + [vmem] * 4,
        out_specs=(vmem,) * 6 + (hbm,) + (vmem,) * 5,
        scratch_shapes=[
            pltpu.VMEM((hops * units, W), F32),
            pltpu.VMEM((128, W), F32),
            pltpu.SemaphoreType.DMA((2, 4)),
        ],
        compiler_params=pltpu.CompilerParams(vmem_limit_bytes=32 * 2**20),
    )(mid_sum, rest_sum, stats, weights, hop_gain)
    return (
        loss.reshape(()), hop_w.transpose(1, 0, 2), hop_g, hop_s, hop_l, cat_l.reshape(-1),
        mid_w, mid_g.reshape(-1), mid_s.reshape(-1), mid_l.reshape(-1), out_w.T,
        out_b.reshape(-1),
    )


def solution(mesh):
    placed = (P("nodes", None), P("nodes"), P("nodes", None), P("nodes")) + (P(),) * 11
    return jax.shard_map(
        on_device, mesh=mesh, in_specs=placed, out_specs=(P(),) * 12, check_vma=False
    )
```

```python
import functools

import jax
import jax.numpy as jnp
from jax import lax
from jax.experimental import pallas as pl
from jax.experimental.pallas import tpu as pltpu
from jax.sharding import PartitionSpec as P

MESH = pl.DeviceIdType.MESH
F32, BF16 = jnp.float32, jnp.bfloat16
NN = (((1,), (0,)), ((), ()))
NT = (((1,), (1,)), ((), ()))
W = 512
WIN = 256


def win_start(hop):
    return max(hop - 1, 0) * 128


def split(values):
    high = values.astype(BF16)
    return high, (values - high.astype(F32)).astype(BF16)


def dot(a, b, dims):
    return lax.dot_general(a, b, dims, preferred_element_type=F32)


def dot3(ah, al, bh, bl, dims=NN):
    (da,), (db,) = dims[0]
    return dot(
        jnp.concatenate([ah, al, ah], da), jnp.concatenate([bh, bh, bl], db), dims
    )


def wide(column):
    return jnp.concatenate([column] * (W // 128), axis=1)


def fold(values):
    out = values[:, 0:128]
    for tile in range(1, W // 128):
        out = out + values[:, tile * 128 : (tile + 1) * 128]
    return out


def lane_sum(values):
    return jnp.broadcast_to(jnp.sum(values, axis=1, keepdims=True), values.shape)


def to_row(column):
    return column.T[0:1, :]


def to_column(row):
    return jnp.broadcast_to(row, (128, row.shape[1])).T


def main_kernel(
    n,
    slots,
    table,
    nodes,
    labels,
    counts,
    weights,
    mid_weight,
    gain,
    shift,
    slope,
    cat_slope,
    mid_gain,
    mid_shift,
    mid_slope,
    out_t,
    bias,
    mid_sum,
    rest_sum,
    stats,
    cat_hbm,
    tab,
    x,
    dwm,
    xh,
    xl,
    wmh,
    wml,
    pgh,
    pgl,
    cath,
    catl,
    par,
    mcol,
    acc,
    vec,
    mask,
    lab,
    delta,
    ext,
    res,
    own,
    hop_grad,
    cg,
    ids,
    pack,
    got0,
    got1,
    got2,
    got3,
    send_sem,
    recv_sem,
    sum_send,
    sum_recv,
    part_send,
    part_recv,
    credit,
    freed,
    table_sem,
    load_sem,
    cat_sem,
):
    me = lax.axis_index("nodes")
    rows = slots * n
    blocks = rows // W
    feats, node_rows = table.shape
    hops = 4
    chunk = next(c for c in (512, 384, 256, 128) if node_rows % c == 0)
    chunks = node_rows // chunk
    depth = min(dwm.shape[0] // feats, chunks)

    def peer(k):
        return lax.rem(me + k, n)

    def table_copy(i, slot):
        return pltpu.make_async_copy(
            table.at[:, pl.ds(pl.multiple_of(i * chunk, 128), chunk)],
            dwm.at[pl.ds(pl.multiple_of(slot * feats, 8), feats), 0:chunk],
            table_sem.at[slot],
        )

    def send_all(buf, e):
        @pl.loop(1, n)
        def _(k):
            pltpu.make_async_remote_copy(
                buf.at[me], buf.at[me], send_sem.at[e], recv_sem.at[e],
                device_id=(peer(k),), device_id_type=MESH,
            ).start()

    def wait_all(buf, e):
        others = buf.at[pl.ds(0, n - 1)]
        pltpu.make_async_copy(others, others, send_sem.at[e]).wait()
        pltpu.make_async_copy(others, others, recv_sem.at[e]).wait()

    for i in range(depth):
        table_copy(i, i).start()
    weight_load = pltpu.make_async_copy(mid_weight, x, load_sem.at[0])
    weight_load.start()

    barrier = pltpu.get_barrier_semaphore()

    @pl.loop(1, n)
    def _(k):
        pl.semaphore_signal(barrier, inc=1, device_id=(peer(k),), device_id_type=MESH)

    ext[...] = jnp.zeros_like(ext)
    for h in range(hops):
        here = slice(h * W, (h + 1) * W)
        par[0, here, :] = to_column(gain[h : h + 1, :])
        par[1, here, :] = to_column(shift[h : h + 1, :])
        par[2, here, :] = to_column(0.5 + 0.5 * slope[h : h + 1, :])
        par[3, here, :] = to_column(0.5 + 0.5 * cat_slope[0:1, here])
    for j, row in enumerate((mid_gain, mid_shift, mid_slope)):
        mcol[j] = to_column(row[...])

    per = 128 // slots
    lane8 = lax.broadcasted_iota(jnp.int32, (8, 128), 1)

    @pl.loop(0, rows // 128)
    def _(j):
        own = jnp.broadcast_to(nodes[pl.ds(j, 1), :], (8, 128))
        names = jnp.broadcast_to(labels[pl.ds(j, 1), :], (8, 128))
        for q in range(per):
            d = j * per + q
            turn = (128 - q * slots) % 128
            ids_row = pltpu.roll(own, turn, 1) if q else own
            names_row = pltpu.roll(names, turn, 1) if q else names
            names_row = jnp.where(lane8 == 127, counts[0, d], names_row)
            place_row = jnp.clip(ids_row - d * node_rows, 0, node_rows - 1)
            pack[d, 0:1, :] = place_row[0:1, :]
            pack[d, 1:2, :] = names_row[0:1, :]

    pl.semaphore_wait(barrier, n - 1)
    got0[me] = pack[me]

    @pl.loop(1, n)
    def _(k):
        pltpu.make_async_remote_copy(
            pack.at[peer(k)], got0.at[me], send_sem.at[0], recv_sem.at[0],
            device_id=(peer(k),), device_id_type=MESH,
        ).start()

    @pl.loop(0, chunks)
    def _(i):
        slot = lax.rem(i, depth)
        table_copy(i, slot).wait()
        for k in range(chunk // 128):
            tab[pl.ds(pl.multiple_of(i * chunk + k * 128, 128), 128), 0:feats] = dwm[
                pl.ds(pl.multiple_of(slot * feats, 8), feats), k * 128 : (k + 1) * 128
            ].T

        @pl.when(i + depth < chunks)
        def _():
            table_copy(i + depth, slot).start()

    plain_load = pltpu.make_async_copy(mid_weight, dwm, load_sem.at[0])
    width = weights.shape[0]
    for h in range(hops):
        start = h * width - win_start(h)
        ext[0:WIN, :] = jnp.zeros((WIN, W), F32)
        ext[start : start + width, :] = weights[:, h, :]
        high, low = split(ext[0:WIN, :].T)
        pgh[h * W : (h + 1) * W, 0:WIN] = high
        pgh[h * W : (h + 1) * W, WIN : 2 * WIN] = low

    weight_load.wait()
    for h in range(hops):
        high, low = split(x[h * W : (h + 1) * W, :].T)
        wmh[h * W : (h + 1) * W, :] = high
        wml[h * W : (h + 1) * W, :] = low
    plain_load.start()

    wait_all(got0, 0)

    to_smem = pltpu.make_async_copy(got0, ids, load_sem.at[1])
    to_smem.start()
    to_smem.wait()

    step = min(slots, 32)

    @pl.loop(0, n)
    def _(s):
        @pl.loop(0, slots // step)
        def _(g):
            for first in range(0, step, 8):
                at = g * step + first
                x[pl.ds(pl.multiple_of(s * slots + at, 8), 8), :] = jnp.concatenate(
                    [tab[pl.ds(ids[s, 0, at + k], 1), :] for k in range(8)], axis=0
                )

    @pl.loop(0, rows // 128)
    def _(j):
        live = jnp.zeros((8, 128), F32)
        names = jnp.zeros((8, 128), jnp.int32)
        for q in range(per):
            s = j * per + q
            mine = (lane8 >= q * slots) & (lane8 < (q + 1) * slots)
            live = live + jnp.where(
                mine & (lane8 < q * slots + ids[s, 1, 127]), 1.0, 0.0
            )
            row = jnp.broadcast_to(got0[s, 1:2, :], (8, 128))
            if q:
                row = pltpu.roll(row, q * slots, 1)
            names = jnp.where(mine, row, names)
        at = pl.ds(pl.multiple_of(j * 128, 128), 128)
        mask[0:1, at] = live[0:1, :]
        lab[0:1, at] = names[0:1, :]

    here_count = jnp.broadcast_to(
        jnp.sum(mask[...], axis=1, keepdims=True), (1, 128)
    )
    acc[0] = jnp.zeros((W, 128), F32)
    top_row = lax.broadcasted_iota(jnp.int32, (128, W), 0)

    @pl.loop(0, blocks)
    def _(b):
        at = pl.ds(pl.multiple_of(b * W, W), W)
        live = mask[0:1, at]
        for f in range(4):
            block = x[at, f * 128 : (f + 1) * 128].T
            if (f + 1) * 128 > feats:
                block = jnp.where(top_row < feats - f * 128, block, 0.0)
            tab[pl.ds(pl.multiple_of(b * W + f * 128, 128), 128), :] = block
            acc[0, f * 128 : (f + 1) * 128, :] += fold(block * live)

    mean_here = lane_sum(acc[0]) / here_count

    @pl.loop(0, blocks)
    def _(b):
        at = pl.ds(pl.multiple_of(b * W, W), W)
        live = mask[0:1, at]
        high, low = split((tab[at, :] - wide(mean_here)) * live)
        xh[:, at] = high
        xl[:, at] = low

    def pre_at(h, b):
        return pl.ds(pl.multiple_of((h * blocks + b) * W, W), W)

    for h in range(hops):
        wh = pgh[h * W : (h + 1) * W, 0:WIN]
        wl = pgh[h * W : (h + 1) * W, WIN : 2 * WIN]
        window = slice(win_start(h), win_start(h) + WIN)
        acc[h] = jnp.zeros((W, 128), F32)

        @pl.loop(0, blocks, unroll=4)
        def _(b):
            at = pl.ds(pl.multiple_of(b * W, W), W)
            pre = dot3(wh, wl, xh[window, at], xl[window, at])
            tab[pre_at(h, b), :] = pre
            acc[h] += fold(pre * pre)

    for h in range(hops):
        row = to_row(lane_sum(acc[h]))
        if h < 3:
            got1[me, 0:1, h * W : (h + 1) * W] = row
        else:
            got1[me, 1:2, 0:W] = row
    got1[me, 1:2, W : 2 * W] = to_row(mean_here)
    got1[me, 1:2, 2 * W : 3 * W] = wide(here_count)
    send_all(got1, 1)

    for h in range(hops):
        if h != 1:
            window = slice(win_start(h), win_start(h) + WIN)
            products = dot3(xh[window, :], xl[window, :], xh[window, :], xl[window, :], NT)
        start = h * width - win_start(h)
        hop_grad[0:WIN, :] = products
        part = pltpu.roll(hop_grad[start : start + 104, :], (WIN - start) % WIN, 1)
        ext[GRAM : GRAM + 104, h * 128 : (h + 1) * 128] = part[:, 0:128]

    wait_all(got1, 1)

    delta[...] = jnp.zeros_like(delta)
    every_count = got1[:, 1:2, 2 * W : 3 * W]
    vec[0:1, :] = jnp.sum(every_count, axis=0)
    vec[1:2, :] = jnp.sum(every_count * got1[:, 1:2, W : 2 * W], axis=0)
    for h in range(3):
        vec[2 + h : 3 + h, :] = jnp.sum(got1[:, 0:1, h * W : (h + 1) * W], axis=0)
    vec[5:6, :] = jnp.sum(got1[:, 1:2, 0:W], axis=0)

    total = vec[0:1, :]
    total_lane = vec[0:1, 0:128]
    mean_row = vec[1:2, :] / total
    stats[2:3, :] = total

    @pl.loop(0, n, unroll=8)
    def _(d):
        counts = got1[d, 1:2, 2 * W : 3 * W]
        delta[pl.ds(d, 1), :] = (got1[d, 1:2, W : 2 * W] - mean_row) * jnp.sqrt(counts)

    delta[n : n + 1, :] = got1[me, 1:2, W : 2 * W] - mean_row
    for h in range(hops):
        off = jnp.broadcast_to(delta[n : n + 1, :], (8, W))
        off = pltpu.roll(off, (W - h * width) % W, 1)[0:1, 0:128]
        tall = jnp.broadcast_to(off, (128, 128)).T[0:104, :]
        ext[GRAM : GRAM + 104, h * 128 : (h + 1) * 128] += tall * off * here_count
    span = delta.shape[0]
    span_lane = lax.broadcasted_iota(jnp.int32, (W, span), 1)
    for h in range(hops):
        here = slice(h * W, (h + 1) * W)
        wh, wl = pgh[here, 0:WIN], pgh[here, WIN : 2 * WIN]
        dh, dl = split(delta[:, win_start(h) : win_start(h) + WIN])
        apart = dot3(wh, wl, dh, dl, NT)
        between = jnp.sum(jnp.where(span_lane < n, apart * apart, 0.0), axis=1, keepdims=True)
        offset = jnp.sum(jnp.where(span_lane == n, apart, 0.0), axis=1, keepdims=True)
        spread = to_column(vec[2 + h : 3 + h, :]) + between
        inv = lax.rsqrt(spread / total_lane + 1e-05)
        stats[3 + h : 4 + h, :] = to_row(inv)
        scale = 0.5 * par[0, here, :] * inv
        par[1, here, :] = 0.5 * par[1, here, :] + scale * offset
        par[0, here, :] = scale

    def cat_copy(h, b, slot, part):
        ref = (cath, catl)[part]
        return pltpu.make_async_copy(
            ref.at[slot], cat_hbm.at[part, h, b], cat_sem.at[part, slot]
        )

    def cat_load(h, b, slot, part):
        ref = (cath, catl)[part]
        return pltpu.make_async_copy(
            cat_hbm.at[part, h, b], ref.at[slot], cat_sem.at[part, slot]
        )

    def hop_act(h, b, slot):
        for c in range(8):
            sub = slice(c * 64, (c + 1) * 64)
            here = slice(h * W + c * 64, h * W + (c + 1) * 64)
            pre = tab[pl.ds(pl.multiple_of((h * blocks + b) * W + c * 64, 64), 64), :]
            u = pre * wide(par[0, here, :]) + wide(par[1, here, :])
            t = jnp.tanh(u)
            v = u * (t + wide(par[2, here, :]) * (1.0 - t))
            t = jnp.tanh(v)
            high, low = split((v + v) * (t + wide(par[3, here, :]) * (1.0 - t)))
            cath[slot, sub, :] = high
            catl[slot, sub, :] = low

    @pl.loop(0, blocks)
    def _(b):
        at = pl.ds(pl.multiple_of(b * W, W), W)
        for h in range(hops):

            @pl.when(b > 0)
            def _():
                for part in range(2):
                    cat_copy(h, b - 1, h, part).wait()

        for h in range(hops):
            hop_act(h, b, h)
            for part in range(2):
                cat_copy(h, b, h, part).start()
            here = slice(h * W, (h + 1) * W)
            part_sum = dot3(wmh[here, :], wml[here, :], cath[h], catl[h])
            if h == 0:
                x[at, :] = part_sum
            else:
                x[at, :] += part_sum

    for h in range(hops):
        for part in range(2):
            cat_copy(h, blocks - 1, h, part).wait()

    acc[0] = jnp.zeros((W, 128), F32)

    @pl.loop(0, blocks)
    def _(b):
        at = pl.ds(pl.multiple_of(b * W, W), W)
        acc[0] += fold(x[at, :] * mask[0:1, at])

    mean_here2 = lane_sum(acc[0]) / here_count
    acc[1] = jnp.zeros((W, 128), F32)

    @pl.loop(0, blocks)
    def _(b):
        at = pl.ds(pl.multiple_of(b * W, W), W)
        off = (x[at, :] - wide(mean_here2)) * mask[0:1, at]
        acc[1] += fold(off * off)

    got2[me, 0:1, :] = to_row(mean_here2)
    got2[me, 1:2, :] = to_row(lane_sum(acc[1]))
    send_all(got2, 2)

    plain_load.wait()
    for h in range(hops):
        high, low = split(dwm[h * W : (h + 1) * W, :])
        wmh[h * W : (h + 1) * W, :] = high
        wml[h * W : (h + 1) * W, :] = low

    classes = bias.shape[1]
    kinds = 48
    ext[SMALL : SMALL + kinds, :] = jnp.zeros((kinds, W), F32)
    ext[SMALL : SMALL + classes, :] = out_t[...]
    oh, ol = split(ext[SMALL : SMALL + kinds, :])
    nh, nl = split(ext[SMALL : SMALL + kinds, :].T)
    vec[6:7, :] = jnp.zeros((1, W), F32)
    vec[6:7, 0:classes] = bias[...]
    bias_col = wide(to_column(vec[6:7, 0:128])[0:kinds, :])

    wait_all(got2, 2)
    every_count = got1[:, 1:2, 2 * W : 3 * W]
    mean2 = jnp.sum(got2[:, 0:1, :] * every_count, axis=0) / total
    off = got2[:, 0:1, :] - mean2
    vec[3:4, :] = jnp.sum(got2[:, 1:2, :] + off * off * every_count, axis=0)
    inv2 = lax.rsqrt(vec[3:4, :] / total + 1e-05)
    mcol[3] = to_column(mean2)
    mcol[4] = to_column(inv2)
    mcol[2] = 0.5 + 0.5 * mcol[2]

    for b in range(blocks):
        for part in range(2):
            cat_load(0, b, b % 4, part).start()

    for j in range(4):
        acc[j] = jnp.zeros((W, 128), F32)
    ext[SMALL : SMALL + 64, :] = jnp.zeros((64, W), F32)
    kind = lax.broadcasted_iota(jnp.int32, (kinds, W), 0)

    @pl.loop(0, blocks)
    def _(b):
        at = pl.ds(pl.multiple_of(b * W, W), W)
        live = mask[0:1, at]
        normed = (x[at, :] - wide(mcol[3])) * wide(mcol[4])
        v = 0.5 * (normed * wide(mcol[0]) + wide(mcol[1]))
        t = jnp.tanh(v)
        keep = wide(mcol[2])
        rest = 1.0 - t
        ah, al = split((v + v) * (t + keep * rest))
        q = v * rest
        logits = dot3(oh, ol, ah, al) + bias_col
        logits = jnp.where(kind < classes, logits, -1e30)
        top = jnp.max(logits, axis=0, keepdims=True)
        e = jnp.exp(logits - top)
        norm = jnp.sum(e, axis=0, keepdims=True)
        logp = logits - top - jnp.log(norm)
        hit = kind == lab[0:1, at]
        loss = jnp.sum(jnp.where(hit, logp, 0.0), axis=0, keepdims=True) * live
        back = (e / norm - jnp.where(hit, 1.0, 0.0)) * (live / total)
        bh, bl = split(back)
        ext[SMALL : SMALL + kinds, :] += dot3(bh, bl, ah, al, NT)
        ext[SMALL + 49 : SMALL + 50, :] -= loss
        acc[3, 0:kinds, :] += fold(back)
        grad = dot3(nh, nl, bh, bl)
        acc[0] += fold(grad * q)
        m = t + q + q * t
        grad = grad * (m + keep * (1.0 - m))
        dwm[at, :] = grad
        acc[1] += fold(grad)
        acc[2] += fold(grad * normed)

    ext[SMALL + 48 : SMALL + 49, :] = to_row(lane_sum(acc[0]))
    ext[SMALL + 50 : SMALL + 51, 0:128] = to_row(lane_sum(acc[3])[0:128, :])
    got3[me, 0:1, :] = to_row(lane_sum(acc[1]))
    got3[me, 1:2, :] = to_row(lane_sum(acc[2]))
    send_all(got3, 3)
    wait_all(got3, 3)
    vec[2:4, :] = jnp.sum(got3[...], axis=0)
    stats[0:2, :] = vec[2:4, :]
    shift_part = to_column(vec[2:3, :] / total)
    gain_part = to_column(vec[3:4, :] / total)
    factor = mcol[0] * mcol[4]

    @pl.loop(0, blocks)
    def _(b):
        at = pl.ds(pl.multiple_of(b * W, W), W)
        normed = (x[at, :] - wide(mcol[3])) * wide(mcol[4])
        grad = dwm[at, :] - wide(shift_part) - normed * wide(gain_part)
        high, low = split(grad * wide(factor) * mask[0:1, at])
        pgh[at, :] = high
        pgl[at, :] = low

    bits = n.bit_length() - 1

    def bit_of(b):
        return lax.rem(me // (1 << b), 2)

    def across(b):
        return me + (1 << b) * (1 - 2 * bit_of(b))

    def remote(src, dst, send, recv, to):
        return pltpu.make_async_remote_copy(
            src, dst, send, recv, device_id=(to,), device_id_type=MESH
        )

    def wait_bytes(ref, sem):
        pltpu.make_async_copy(ref, ref, sem).wait()

    for b in range(bits):
        pl.semaphore_signal(credit, inc=1, device_id=(across(b),), device_id_type=MESH)

    far = list(range(3, bits))
    orders = [[1, 2] + far, [2, 1] + far, [1] + far + [2], [2] + far + [1]]
    span = W // len(orders)

    def halving(batch, base, size, take):
        def rows_at(off, length):
            return pl.ds(pl.multiple_of(off, 8), length)

        half = size // 2
        tmps = [take(half)]
        levels = [
            [(0, slice(0, W), base + bit_of(0) * half, base + (1 - bit_of(0)) * half, half, tmps[0][1])]
        ]
        rest_tmp, at = take(half)
        tmps += [(rest_tmp, at)] * (bits - 1)
        offs = [base + bit_of(0) * half] * len(orders)
        length = half
        for j in range(bits - 1):
            length //= 2
            level = []
            for q in range(len(orders)):
                b = orders[q][j]
                keep = offs[q] + bit_of(b) * length
                give = offs[q] + (1 - bit_of(b)) * length
                level.append((b, slice(q * span, (q + 1) * span), keep, give, length, at))
                offs[q] = keep
            at += length
            levels.append(level)

        stages = []
        for k, level in enumerate(levels):
            send, recv = sum_send.at[batch, k], sum_recv.at[batch, k]
            free = freed.at[batch, k]
            length, first = level[0][4:]
            tmp = tmps[k][0]
            arrived = tmp.at[first : first + length, :]

            def start(level=level, send=send, recv=recv, tmp=tmp):
                for b, lanes, keep, give, ln, t in level:
                    remote(
                        dwm.at[rows_at(give, ln), lanes], tmp.at[t : t + ln, lanes],
                        send, recv, across(b),
                    ).start()

            def finish(level=level, send=send, recv=recv, free=free, arrived=arrived, tmp=tmp):
                wait_bytes(arrived, send)
                wait_bytes(arrived, recv)
                for b, lanes, keep, give, ln, t in level:
                    pl.semaphore_signal(
                        free, inc=1, device_id=(across(b),), device_id_type=MESH
                    )
                    dwm[rows_at(keep, ln), lanes] += tmp[t : t + ln, lanes]

            stages.append((start, finish))
        for k in range(bits - 1, -1, -1):
            level = levels[k]
            send, recv = sum_send.at[batch, bits + k], sum_recv.at[batch, bits + k]
            free = freed.at[batch, k]
            length, first = level[0][4:]
            arrived = tmps[k][0].at[first : first + length, :]

            def start(level=level, send=send, recv=recv, free=free):
                pl.semaphore_wait(free, len(level))
                for b, lanes, keep, give, ln, t in level:
                    here = dwm.at[rows_at(keep, ln), lanes]
                    remote(here, here, send, recv, across(b)).start()

            def finish(send=send, recv=recv, arrived=arrived):
                wait_bytes(arrived, send)
                wait_bytes(arrived, recv)

            stages.append((start, finish))
        return stages

    chips = n // 2
    core, chip = lax.rem(me, 2), me // 2
    half_lanes = W // 2
    mine = pl.ds(pl.multiple_of(core * half_lanes, 128), half_lanes)
    other = pl.ds(pl.multiple_of((1 - core) * half_lanes, 128), half_lanes)

    def direct(batch, base, size, rows_each, tmp_base, tmp_lane):
        owners = size // rows_each
        cols = slice(tmp_lane, tmp_lane + half_lanes)
        block = pl.ds(base, size)
        from_core = tab.at[tmp_base : tmp_base + size, cols]
        first = tmp_base + size
        slot = tab.at[pl.ds(pl.multiple_of(first + chip * rows_each, 8), rows_each), cols]
        summed = own.at[batch, 0:rows_each, :]
        sends = [part_send.at[batch, k] for k in range(4)]
        recvs = [part_recv.at[batch, k] for k in range(4)]

        def many(k):
            return tab.at[first : first + rows_each * k, cols]

        def piece(q):
            return pl.ds(pl.multiple_of(base + q * rows_each, 8), rows_each)

        def start():
            remote(ext.at[block, other], from_core, sends[0], recvs[0], across(0)).start()

        def spread():
            wait_bytes(from_core, sends[0])
            wait_bytes(from_core, recvs[0])
            ext[block, mine] += tab[tmp_base : tmp_base + size, cols]

            @pl.loop(0, owners)
            def _(k):
                q = lax.rem(chip + k, owners)

                @pl.when(q == chip)
                def _():
                    pltpu.make_async_copy(ext.at[piece(q), mine], slot, recvs[1]).start()

                @pl.when(q != chip)
                def _():
                    remote(ext.at[piece(q), mine], slot, sends[1], recvs[1], q * 2 + core).start()

        def middle():
            @pl.when(chip < owners)
            def _():
                wait_bytes(many(owners - 1), sends[1])
                wait_bytes(many(chips), recvs[1])
                out = tab[first : first + rows_each, cols]
                for d in range(1, chips):
                    at = first + rows_each * d
                    out = out + tab[at : at + rows_each, cols]
                own[batch, 0:rows_each, :] = out
                there = res.at[piece(chip), mine]
                pltpu.make_async_copy(summed, there, recvs[2]).start()

                @pl.loop(1, chips)
                def _(k):
                    to = lax.rem(chip + k, chips) * 2 + core
                    remote(summed, there, sends[2], recvs[2], to).start()

            @pl.when(chip >= owners)
            def _():
                wait_bytes(many(owners), sends[1])

        def join():
            wait_bytes(res.at[block, mine], recvs[2])

            @pl.when(chip < owners)
            def _():
                wait_bytes(many(chips - 1), sends[2])

            here = res.at[block, mine]
            remote(here, here, sends[3], recvs[3], across(0)).start()

        def finish():
            wait_bytes(res.at[block, other], sends[3])
            wait_bytes(res.at[block, other], recvs[3])

        return [start, spread, middle, join, finish]

    mid_batch = max(W, 8 * n)
    mids = hops * W // mid_batch
    DW, HB, GAP = 1.0, 2.1, 4.5
    PART = (2.5, 5.0, 5.0, 2.5)
    clock = [(t + 1) * DW for t in range(hops * blocks)]
    clock += [clock[-1] + (t + 1) * HB for t in range(hops * blocks)]
    spare = hops * rows
    part_rows = 208 + 16 * chips
    spots = [(x, W, x.shape[0] - W), (tab, spare + part_rows, tab.shape[0] - spare - part_rows)]

    def take(size):
        spot = next(i for i in range(2) if spots[i][2] >= size)
        ref, first, left = spots[spot]
        spots[spot] = (ref, first + size, left - size)
        return ref, first

    events = []
    for k in range(mids):
        stages = halving(k, k * mid_batch, mid_batch, take)
        when = clock[(k + 1) * mid_batch // W * blocks - 1]
        for j in range(len(stages) + 1):
            todo = []
            if j:
                todo.append(stages[j - 1][1])
            elif k == 0:
                todo.append(lambda: pl.semaphore_wait(credit, bits))
            if j < len(stages):
                todo.append(stages[j][0])
            else:
                todo.append(lambda k=k: mid_out(k).start())
            events.append((when, len(events), todo))
            when += GAP
    ends = [clock[hops * blocks + (h + 1) * blocks - 1] for h in range(hops)]
    for batch, (when, base, size, rows_each) in enumerate(
        (
            (clock[0], 0, HOPS_AT, 16),
            (ends[1], hop_row(0), 208, 16),
            (ends[2], hop_row(2), 104, 8),
            (ends[3], hop_row(3), 104, 8),
        )
    ):
        stages = direct(batch, base, size, rows_each, spare, batch % 2 * half_lanes)
        for j, stage in enumerate(stages):
            at = when + sum(PART[:j])
            if batch == 1:
                at = min(at, ends[3] - 1e-3)
            events.append((at, len(events), [stage]))

    ticks = {}
    for when, _, todo in sorted(events, key=lambda e: e[:2]):
        tick = next((t for t, c in enumerate(clock) if c >= when - 1e-6), len(clock))
        ticks.setdefault(tick, []).extend(todo)

    def mid_out(k):
        here = slice(k * mid_batch, (k + 1) * mid_batch)
        return pltpu.make_async_copy(dwm.at[here], mid_sum.at[here], table_sem.at[k])

    def act(tick):
        for todo in ticks.get(tick, []):
            todo()

    for h in range(hops):
        here = slice(h * W, (h + 1) * W)

        @pl.loop(0, blocks)
        def _(b):
            at = pl.ds(pl.multiple_of(b * W, W), W)
            slot = lax.rem(b, 4)
            for part in range(2):
                cat_load(h, b, slot, part).wait()
            part_sum = dot3(cath[slot], catl[slot], pgh[at, :], pgl[at, :], NT)
            if h + 1 < hops:
                for part in range(2):
                    cat_load(h + 1, b, slot, part).start()

            @pl.when(b == 0)
            def _():
                dwm[here, :] = part_sum

            @pl.when(b > 0)
            def _():
                dwm[here, :] += part_sum

            for t in range(blocks):
                if ticks.get(h * blocks + t):

                    @pl.when(b == t)
                    def _():
                        act(h * blocks + t)

    grads = (x.at[0:W], cg)

    def head_back(h, b, rs):
        at = pl.ds(b * W, W)
        here = pl.ds(pl.multiple_of(h * W + rs.start, 128), rs.stop - rs.start)
        return dot3(wmh[here, :], wml[here, :], pgh[at, :], pgl[at, :])

    def weight_back(h, b, rs):
        window = pl.ds(pl.multiple_of(jnp.maximum(h - 1, 0) * 128, 128), WIN)
        at = pl.ds(b * W, W)
        part_sum = dot3(
            cath[b % 2, rs, :], catl[b % 2, rs, :], xh[window, at], xl[window, at], NT
        )
        if b == 0:
            hop_grad[rs, :] = part_sum
        else:
            hop_grad[rs, :] += part_sum

    def act_back(h, b, c):
        sub = slice(c * 64, (c + 1) * 64)
        col = pl.ds(pl.multiple_of(h * W + c * 64, 64), 64)
        grad = grads[b % 2][sub, :]
        pre = tab[pl.ds(pl.multiple_of((h * blocks + b) * W + c * 64, 64), 64), :]
        keep1, keep2 = wide(par[2, col, :]), wide(par[3, col, :])
        u = pre * wide(par[0, col, :]) + wide(par[1, col, :])
        t1 = jnp.tanh(u)
        r1 = 1.0 - t1
        v = u * (t1 + keep1 * r1)
        t2 = jnp.tanh(v)
        q = v * (1.0 - t2)
        sum2 = fold(grad * q)
        m = t2 + q + q * t2
        grad = grad * (m + keep2 * (1.0 - m))
        q = u * r1
        sum1 = fold(grad * q)
        m = t1 + q + q * t1
        grad = grad * (m + keep1 * (1.0 - m))
        for j, value in enumerate((sum2, sum1, fold(grad))):
            if b == 0:
                acc[j, sub, :] = value
            else:
                acc[j, sub, :] += value
        high, low = split(grad)
        cath[b % 2, sub, :] = high
        catl[b % 2, sub, :] = low

    halves = (slice(0, W // 2), slice(W // 2, W))
    grads[0][...] = head_back(0, 0, slice(0, W))

    @pl.loop(0, hops)
    def _(h):
        for b in range(blocks):
            for m, rs in enumerate(halves):
                if b + 1 < blocks:
                    grads[(b + 1) % 2][rs, :] = head_back(h, b + 1, rs)
                else:
                    grads[(b + 1) % 2][rs, :] = head_back(jnp.minimum(h + 1, hops - 1), 0, rs)
                if b:
                    weight_back(h, b - 1, rs)
                for c in range(4 * m, 4 * m + 4):
                    act_back(h, b, c)
            if b + 1 < blocks:
                for t in range(hops):
                    if ticks.get(hops * blocks + t * blocks + b):

                        @pl.when(h == t)
                        def _():
                            act(hops * blocks + t * blocks + b)

        weight_back(h, blocks - 1, slice(0, W))
        for t in range(hops):

            @pl.when(h == t)
            def _():
                sums = lane_sum(acc[2])
                offset = delta[n : n + 1, win_start(t) : win_start(t) + WIN]
                tall = hop_grad[...] + jnp.concatenate([sums] * 2, axis=1) * offset
                first = hop_row(t)
                start = t * width - win_start(t)
                cg[0:WIN, :] = tall.T
                ext[first : first + width, :] = cg[start : start + width, :]
                for j in range(3):
                    row = first + width + j
                    ext[row : row + 1, :] = to_row(lane_sum(acc[j]))
                act(hops * blocks + t * blocks + blocks - 1)

    act(len(clock))
    rest_out = pltpu.make_async_copy(res, rest_sum, load_sem.at[0])
    rest_out.start()
    for k in range(mids):
        mid_out(k).wait()
    rest_out.wait()


GRAM, SMALL, HOPS_AT = 0, 104, 176


def hop_row(h):
    return HOPS_AT + h * 104


def final_kernel(
    mid_sum, rest_sum, stats_sum, weights_in, gain, loss, hop_w, hop_g, hop_s, hop_l, cat_l, mid_w,
    mid_g, mid_s, mid_l, out_w, out_b, buf, wide_w, rest, stats, weights, sem,
):
    parts = 4
    size = mid_sum.shape[0] // parts

    def load(k):
        here = slice(k * size, (k + 1) * size)
        return pltpu.make_async_copy(mid_sum.at[here], buf.at[here], sem.at[0, k])

    def store(k):
        here = slice(k * size, (k + 1) * size)
        return pltpu.make_async_copy(buf.at[here], mid_w.at[here], sem.at[1, k])

    loads = [
        pltpu.make_async_copy(src, dst, sem.at[2, k])
        for k, (src, dst) in enumerate(((rest_sum, rest), (stats_sum, stats), (weights_in, weights)))
    ]
    for copy in loads:
        copy.start()
    for k in range(parts):
        load(k).start()
    for copy in loads:
        copy.wait()
    total = stats[2:3, :]
    width, hops, _ = weights.shape
    wide_w[...] = jnp.zeros_like(wide_w)
    for h in range(hops):
        first = hop_row(h)
        raw = rest[first : first + width, :]
        weight = weights[:, h, :]
        inv = stats[3 + h : 4 + h, :]
        gain_grad = inv * jnp.sum(weight * raw, axis=0, keepdims=True)
        wide_w[0:width, :] = weight
        along = lax.dot_general(
            rest[GRAM : GRAM + 104, h * 128 : (h + 1) * 128], wide_w[...], NN,
            precision=lax.Precision.HIGHEST, preferred_element_type=F32,
        )[0:width, :]
        grad = raw - along * (inv * gain_grad / total)
        hop_w[:, h, :] = gain[h : h + 1, :] * inv * grad
        hop_g[h : h + 1, :] = gain_grad
        cat_l[0:1, h * W : (h + 1) * W] = rest[first + width : first + width + 1, :]
        hop_l[h : h + 1, :] = rest[first + width + 1 : first + width + 2, :]
        hop_s[h : h + 1, :] = rest[first + width + 2 : first + width + 3, :]
        load(h).wait()
        store(h).start()
    mid_s[...] = stats[0:1, :]
    mid_g[...] = stats[1:2, :]
    mid_l[...] = rest[SMALL + 48 : SMALL + 49, :]
    out_w[...] = rest[SMALL : SMALL + out_w.shape[0], :]
    out_b[...] = rest[SMALL + 50 : SMALL + 51, 0 : out_b.shape[1]]
    loss[...] = jnp.sum(rest[SMALL + 49 : SMALL + 50, :], axis=1, keepdims=True) / total[:, 0:1]
    for k in range(parts):
        store(k).wait()


def on_device(
    node_table, batch_nodes, send_counts, labels, hop_weight, hop_gain, hop_shift, hop_slope,
    cat_slope, mid_weight, mid_gain, mid_shift, mid_slope, out_weight, out_bias,
):
    n = lax.axis_size("nodes")
    node_rows, feats = node_table.shape
    rows = batch_nodes.shape[0]
    slots = rows // n
    hops, width, units = hop_weight.shape
    blocks = rows // W
    classes = out_weight.shape[1]
    vmem = pl.BlockSpec(memory_space=pltpu.VMEM)
    hbm = pl.BlockSpec(memory_space=pl.ANY)
    shape = jax.ShapeDtypeStruct
    bits = n.bit_length() - 1
    mid_batch = max(W, 8 * n)
    sums = hops * W // mid_batch
    small_rows = HOPS_AT + 104 * hops
    halves = 2 * sums - (hops * W - W) // (mid_batch // 2)
    spill = 208 + 8 * n + halves * mid_batch // 2
    tab_rows = max(node_rows, hops * rows + spill)
    weights = hop_weight.transpose(1, 0, 2)
    mid_sum, rest_sum, stats, _ = pl.pallas_call(
        functools.partial(main_kernel, n, slots),
        out_shape=(
            shape((hops * units, W), F32),
            shape((small_rows, W), F32),
            shape((8, W), F32),
            shape((2, hops, blocks, W, W), BF16),
        ),
        in_specs=[hbm, vmem, vmem, pl.BlockSpec(memory_space=pltpu.SMEM), vmem, hbm] + [vmem] * 9,
        out_specs=(hbm, hbm, vmem, hbm),
        scratch_shapes=[
            pltpu.VMEM((tab_rows, 512), F32),
            pltpu.VMEM((max(rows, hops * W), W), F32),
            pltpu.VMEM((max(rows, hops * W), W), F32),
            pltpu.VMEM((512, rows), BF16),
            pltpu.VMEM((512, rows), BF16),
            pltpu.VMEM((hops * W, W), BF16),
            pltpu.VMEM((hops * W, W), BF16),
            pltpu.VMEM((max(rows, hops * W), W), BF16),
            pltpu.VMEM((max(rows, hops * W), W), BF16),
            pltpu.VMEM((4, W, W), BF16),
            pltpu.VMEM((4, W, W), BF16),
            pltpu.VMEM((4, hops * W, 128), F32),
            pltpu.VMEM((5, W, 128), F32),
            pltpu.VMEM((4, W, 128), F32),
            pltpu.VMEM((8, W), F32),
            pltpu.VMEM((1, rows), F32),
            pltpu.VMEM((1, rows), jnp.int32),
            pltpu.VMEM((n + 8, W), F32),
            pltpu.VMEM((small_rows, W), F32),
            pltpu.VMEM((small_rows, W), F32),
            pltpu.VMEM((4, 16, W // 2), F32),
            pltpu.VMEM((W, WIN), F32),
            pltpu.VMEM((W, W), F32),
            pltpu.SMEM((n, 2, 128), jnp.int32),
            pltpu.VMEM((n, 2, 128), jnp.int32),
            pltpu.VMEM((n, 2, 128), jnp.int32),
            pltpu.VMEM((n, 2, 3 * W), F32),
            pltpu.VMEM((n, 2, W), F32),
            pltpu.VMEM((n, 2, W), F32),
            pltpu.SemaphoreType.DMA((4,)),
            pltpu.SemaphoreType.DMA((4,)),
            pltpu.SemaphoreType.DMA((sums, 2 * bits)),
            pltpu.SemaphoreType.DMA((sums, 2 * bits)),
            pltpu.SemaphoreType.DMA((4, 4)),
            pltpu.SemaphoreType.DMA((4, 4)),
            pltpu.SemaphoreType.REGULAR,
            pltpu.SemaphoreType.REGULAR((sums, bits)),
            pltpu.SemaphoreType.DMA((8,)),
            pltpu.SemaphoreType.DMA((2,)),
            pltpu.SemaphoreType.DMA((2, 4)),
        ],
        compiler_params=pltpu.CompilerParams(
            collective_id=0, has_side_effects=True, vmem_limit_bytes=66_900_000
        ),
    )(
        node_table.T, batch_nodes.reshape(rows // 128, 128), labels.reshape(rows // 128, 128),
        send_counts, weights, mid_weight, hop_gain, hop_shift, hop_slope,
        cat_slope.reshape(1, hops * units), mid_gain.reshape(1, W), mid_shift.reshape(1, W),
        mid_slope.reshape(1, W), out_weight.T, out_bias.reshape(1, classes),
    )
    (
        loss, hop_w, hop_g, hop_s, hop_l, cat_l, mid_w, mid_g, mid_s, mid_l, out_w, out_b,
    ) = pl.pallas_call(
        final_kernel,
        out_shape=(
            shape((1, 1), F32), shape((width, hops, units), F32), shape((hops, units), F32),
            shape((hops, units), F32), shape((hops, units), F32), shape((1, hops * units), F32),
            shape((hops * units, W), F32), shape((1, W), F32), shape((1, W), F32),
            shape((1, W), F32), shape((classes, W), F32), shape((1, classes), F32),
        ),
        in_specs=[hbm] * 4 + [vmem],
        out_specs=(vmem,) * 6 + (hbm,) + (vmem,) * 5,
        scratch_shapes=[
            pltpu.VMEM((hops * units, W), F32),
            pltpu.VMEM((128, W), F32),
            pltpu.VMEM((small_rows, W), F32),
            pltpu.VMEM((8, W), F32),
            pltpu.VMEM((width, hops, units), F32),
            pltpu.SemaphoreType.DMA((3, 4)),
        ],
        compiler_params=pltpu.CompilerParams(vmem_limit_bytes=62 * 2**20),
    )(mid_sum, rest_sum, stats, weights, hop_gain)
    return (
        loss.reshape(()), hop_w.transpose(1, 0, 2), hop_g, hop_s, hop_l, cat_l.reshape(-1),
        mid_w, mid_g.reshape(-1), mid_s.reshape(-1), mid_l.reshape(-1), out_w.T,
        out_b.reshape(-1),
    )


def solution(mesh):
    placed = (P("nodes", None), P("nodes"), P("nodes", None), P("nodes")) + (P(),) * 11
    return jax.shard_map(
        on_device, mesh=mesh, in_specs=placed, out_specs=(P(),) * 12, check_vma=False
    )
```

```python
import functools

import jax
import jax.numpy as jnp
from jax import lax
from jax.experimental import pallas as pl
from jax.experimental.pallas import tpu as pltpu
from jax.sharding import PartitionSpec as P

MESH = pl.DeviceIdType.MESH
F32, BF16 = jnp.float32, jnp.bfloat16
NN = (((1,), (0,)), ((), ()))
NT = (((1,), (1,)), ((), ()))
W = 512
WIN = 256


def win_start(hop):
    return max(hop - 1, 0) * 128


def split(values):
    high = values.astype(BF16)
    return high, (values - high.astype(F32)).astype(BF16)


def dot(a, b, dims):
    return lax.dot_general(a, b, dims, preferred_element_type=F32)


def dot3(ah, al, bh, bl, dims=NN):
    (da,), (db,) = dims[0]
    return dot(
        jnp.concatenate([ah, al, ah], da), jnp.concatenate([bh, bh, bl], db), dims
    )


def wide(column):
    return jnp.concatenate([column] * (W // 128), axis=1)


def fold(values):
    out = values[:, 0:128]
    for tile in range(1, W // 128):
        out = out + values[:, tile * 128 : (tile + 1) * 128]
    return out


def lane_sum(values):
    return jnp.broadcast_to(jnp.sum(values, axis=1, keepdims=True), values.shape)


def to_row(column):
    return column.T[0:1, :]


def to_column(row):
    return jnp.broadcast_to(row, (128, row.shape[1])).T


def main_kernel(
    n,
    slots,
    table,
    nodes,
    labels,
    counts,
    weights,
    mid_weight,
    gain,
    shift,
    slope,
    cat_slope,
    mid_gain,
    mid_shift,
    mid_slope,
    out_t,
    bias,
    mid_sum,
    rest_sum,
    stats,
    cat_hbm,
    tab,
    x,
    dwm,
    xh,
    xl,
    wmh,
    wml,
    pgh,
    pgl,
    cath,
    catl,
    par,
    mcol,
    acc,
    vec,
    mask,
    lab,
    delta,
    ext,
    res,
    own,
    hop_grad,
    cg,
    ids,
    pack,
    got0,
    got1,
    got2,
    got3,
    send_sem,
    recv_sem,
    sum_send,
    sum_recv,
    part_send,
    part_recv,
    credit,
    freed,
    table_sem,
    load_sem,
    cat_sem,
):
    me = lax.axis_index("nodes")
    rows = slots * n
    blocks = rows // W
    feats, node_rows = table.shape
    hops = 4
    chunk = next(c for c in (512, 384, 256, 128) if node_rows % c == 0)
    chunks = node_rows // chunk
    depth = min(dwm.shape[0] // feats, chunks)

    def peer(k):
        return lax.rem(me + k, n)

    def table_copy(i, slot):
        return pltpu.make_async_copy(
            table.at[:, pl.ds(pl.multiple_of(i * chunk, 128), chunk)],
            dwm.at[pl.ds(pl.multiple_of(slot * feats, 8), feats), 0:chunk],
            table_sem.at[slot],
        )

    def send_all(buf, e):
        @pl.loop(1, n)
        def _(k):
            pltpu.make_async_remote_copy(
                buf.at[me], buf.at[me], send_sem.at[e], recv_sem.at[e],
                device_id=(peer(k),), device_id_type=MESH,
            ).start()

    def wait_all(buf, e):
        others = buf.at[pl.ds(0, n - 1)]
        pltpu.make_async_copy(others, others, send_sem.at[e]).wait()
        pltpu.make_async_copy(others, others, recv_sem.at[e]).wait()

    for i in range(depth):
        table_copy(i, i).start()
    weight_load = pltpu.make_async_copy(mid_weight, x, load_sem.at[0])
    weight_load.start()

    barrier = pltpu.get_barrier_semaphore()

    @pl.loop(1, n)
    def _(k):
        pl.semaphore_signal(barrier, inc=1, device_id=(peer(k),), device_id_type=MESH)

    ext[...] = jnp.zeros_like(ext)
    for h in range(hops):
        here = slice(h * W, (h + 1) * W)
        par[0, here, :] = to_column(gain[h : h + 1, :])
        par[1, here, :] = to_column(shift[h : h + 1, :])
        par[2, here, :] = to_column(0.5 + 0.5 * slope[h : h + 1, :])
        par[3, here, :] = to_column(0.5 + 0.5 * cat_slope[0:1, here])
    for j, row in enumerate((mid_gain, mid_shift, mid_slope)):
        mcol[j] = to_column(row[...])

    per = 128 // slots
    lane8 = lax.broadcasted_iota(jnp.int32, (8, 128), 1)

    @pl.loop(0, rows // 128)
    def _(j):
        own = jnp.broadcast_to(nodes[pl.ds(j, 1), :], (8, 128))
        names = jnp.broadcast_to(labels[pl.ds(j, 1), :], (8, 128))
        for q in range(per):
            d = j * per + q
            turn = (128 - q * slots) % 128
            ids_row = pltpu.roll(own, turn, 1) if q else own
            names_row = pltpu.roll(names, turn, 1) if q else names
            names_row = jnp.where(lane8 == 127, counts[0, d], names_row)
            place_row = jnp.clip(ids_row - d * node_rows, 0, node_rows - 1)
            pack[d, 0:1, :] = place_row[0:1, :]
            pack[d, 1:2, :] = names_row[0:1, :]

    pl.semaphore_wait(barrier, n - 1)
    got0[me] = pack[me]

    @pl.loop(1, n)
    def _(k):
        pltpu.make_async_remote_copy(
            pack.at[peer(k)], got0.at[me], send_sem.at[0], recv_sem.at[0],
            device_id=(peer(k),), device_id_type=MESH,
        ).start()

    @pl.loop(0, chunks)
    def _(i):
        slot = lax.rem(i, depth)
        table_copy(i, slot).wait()
        for k in range(chunk // 128):
            tab[pl.ds(pl.multiple_of(i * chunk + k * 128, 128), 128), 0:feats] = dwm[
                pl.ds(pl.multiple_of(slot * feats, 8), feats), k * 128 : (k + 1) * 128
            ].T

        @pl.when(i + depth < chunks)
        def _():
            table_copy(i + depth, slot).start()

    plain_load = pltpu.make_async_copy(mid_weight, dwm, load_sem.at[0])
    width = weights.shape[0]
    for h in range(hops):
        start = h * width - win_start(h)
        ext[0:WIN, :] = jnp.zeros((WIN, W), F32)
        ext[start : start + width, :] = weights[:, h, :]
        high, low = split(ext[0:WIN, :].T)
        pgh[h * W : (h + 1) * W, 0:WIN] = high
        pgh[h * W : (h + 1) * W, WIN : 2 * WIN] = low

    weight_load.wait()
    for h in range(hops):
        high, low = split(x[h * W : (h + 1) * W, :].T)
        wmh[h * W : (h + 1) * W, :] = high
        wml[h * W : (h + 1) * W, :] = low
    plain_load.start()

    wait_all(got0, 0)

    to_smem = pltpu.make_async_copy(got0, ids, load_sem.at[1])
    to_smem.start()
    to_smem.wait()

    step = min(slots, 32)

    @pl.loop(0, n)
    def _(s):
        @pl.loop(0, slots // step)
        def _(g):
            for first in range(0, step, 8):
                at = g * step + first
                x[pl.ds(pl.multiple_of(s * slots + at, 8), 8), :] = jnp.concatenate(
                    [tab[pl.ds(ids[s, 0, at + k], 1), :] for k in range(8)], axis=0
                )

    @pl.loop(0, rows // 128)
    def _(j):
        live = jnp.zeros((8, 128), F32)
        names = jnp.zeros((8, 128), jnp.int32)
        for q in range(per):
            s = j * per + q
            mine = (lane8 >= q * slots) & (lane8 < (q + 1) * slots)
            live = live + jnp.where(
                mine & (lane8 < q * slots + ids[s, 1, 127]), 1.0, 0.0
            )
            row = jnp.broadcast_to(got0[s, 1:2, :], (8, 128))
            if q:
                row = pltpu.roll(row, q * slots, 1)
            names = jnp.where(mine, row, names)
        at = pl.ds(pl.multiple_of(j * 128, 128), 128)
        mask[0:1, at] = live[0:1, :]
        lab[0:1, at] = names[0:1, :]

    here_count = jnp.broadcast_to(
        jnp.sum(mask[...], axis=1, keepdims=True), (1, 128)
    )
    acc[0] = jnp.zeros((W, 128), F32)
    top_row = lax.broadcasted_iota(jnp.int32, (128, W), 0)

    @pl.loop(0, blocks)
    def _(b):
        at = pl.ds(pl.multiple_of(b * W, W), W)
        live = mask[0:1, at]
        for f in range(4):
            block = x[at, f * 128 : (f + 1) * 128].T
            if (f + 1) * 128 > feats:
                block = jnp.where(top_row < feats - f * 128, block, 0.0)
            tab[pl.ds(pl.multiple_of(b * W + f * 128, 128), 128), :] = block
            acc[0, f * 128 : (f + 1) * 128, :] += fold(block * live)

    mean_here = lane_sum(acc[0]) / here_count

    @pl.loop(0, blocks)
    def _(b):
        at = pl.ds(pl.multiple_of(b * W, W), W)
        live = mask[0:1, at]
        high, low = split((tab[at, :] - wide(mean_here)) * live)
        xh[:, at] = high
        xl[:, at] = low

    def pre_at(h, b):
        return pl.ds(pl.multiple_of((h * blocks + b) * W, W), W)

    for h in range(hops):
        wh = pgh[h * W : (h + 1) * W, 0:WIN]
        wl = pgh[h * W : (h + 1) * W, WIN : 2 * WIN]
        window = slice(win_start(h), win_start(h) + WIN)
        acc[h] = jnp.zeros((W, 128), F32)

        @pl.loop(0, blocks, unroll=4)
        def _(b):
            at = pl.ds(pl.multiple_of(b * W, W), W)
            pre = dot3(wh, wl, xh[window, at], xl[window, at])
            tab[pre_at(h, b), :] = pre
            acc[h] += fold(pre * pre)

    for h in range(hops):
        row = to_row(lane_sum(acc[h]))
        if h < 3:
            got1[me, 0:1, h * W : (h + 1) * W] = row
        else:
            got1[me, 1:2, 0:W] = row
    got1[me, 1:2, W : 2 * W] = to_row(mean_here)
    got1[me, 1:2, 2 * W : 3 * W] = wide(here_count)
    send_all(got1, 1)

    for h in range(hops):
        if h != 1:
            window = slice(win_start(h), win_start(h) + WIN)
            products = dot3(xh[window, :], xl[window, :], xh[window, :], xl[window, :], NT)
        start = h * width - win_start(h)
        hop_grad[0:WIN, :] = products
        part = pltpu.roll(hop_grad[start : start + 104, :], (WIN - start) % WIN, 1)
        ext[GRAM : GRAM + 104, h * 128 : (h + 1) * 128] = part[:, 0:128]

    wait_all(got1, 1)

    delta[...] = jnp.zeros_like(delta)
    every_count = got1[:, 1:2, 2 * W : 3 * W]
    vec[0:1, :] = jnp.sum(every_count, axis=0)
    vec[1:2, :] = jnp.sum(every_count * got1[:, 1:2, W : 2 * W], axis=0)
    for h in range(3):
        vec[2 + h : 3 + h, :] = jnp.sum(got1[:, 0:1, h * W : (h + 1) * W], axis=0)
    vec[5:6, :] = jnp.sum(got1[:, 1:2, 0:W], axis=0)

    total = vec[0:1, :]
    total_lane = vec[0:1, 0:128]
    mean_row = vec[1:2, :] / total
    stats[2:3, :] = total

    @pl.loop(0, n, unroll=8)
    def _(d):
        counts = got1[d, 1:2, 2 * W : 3 * W]
        delta[pl.ds(d, 1), :] = (got1[d, 1:2, W : 2 * W] - mean_row) * jnp.sqrt(counts)

    delta[n : n + 1, :] = got1[me, 1:2, W : 2 * W] - mean_row
    for h in range(hops):
        off = jnp.broadcast_to(delta[n : n + 1, :], (8, W))
        off = pltpu.roll(off, (W - h * width) % W, 1)[0:1, 0:128]
        tall = jnp.broadcast_to(off, (128, 128)).T[0:104, :]
        ext[GRAM : GRAM + 104, h * 128 : (h + 1) * 128] += tall * off * here_count
    span = delta.shape[0]
    span_lane = lax.broadcasted_iota(jnp.int32, (W, span), 1)
    for h in range(hops):
        here = slice(h * W, (h + 1) * W)
        wh, wl = pgh[here, 0:WIN], pgh[here, WIN : 2 * WIN]
        dh, dl = split(delta[:, win_start(h) : win_start(h) + WIN])
        apart = dot3(wh, wl, dh, dl, NT)
        between = jnp.sum(jnp.where(span_lane < n, apart * apart, 0.0), axis=1, keepdims=True)
        offset = jnp.sum(jnp.where(span_lane == n, apart, 0.0), axis=1, keepdims=True)
        spread = to_column(vec[2 + h : 3 + h, :]) + between
        inv = lax.rsqrt(spread / total_lane + 1e-05)
        stats[3 + h : 4 + h, :] = to_row(inv)
        scale = 0.5 * par[0, here, :] * inv
        par[1, here, :] = 0.5 * par[1, here, :] + scale * offset
        par[0, here, :] = scale

    def cat_copy(h, b, slot, part):
        ref = (cath, catl)[part]
        return pltpu.make_async_copy(
            ref.at[slot], cat_hbm.at[part, h, b], cat_sem.at[part, slot]
        )

    def cat_load(h, b, slot, part):
        ref = (cath, catl)[part]
        return pltpu.make_async_copy(
            cat_hbm.at[part, h, b], ref.at[slot], cat_sem.at[part, slot]
        )

    def hop_act(h, b, slot):
        for c in range(8):
            sub = slice(c * 64, (c + 1) * 64)
            here = slice(h * W + c * 64, h * W + (c + 1) * 64)
            pre = tab[pl.ds(pl.multiple_of((h * blocks + b) * W + c * 64, 64), 64), :]
            u = pre * wide(par[0, here, :]) + wide(par[1, here, :])
            t = jnp.tanh(u)
            v = u * (t + wide(par[2, here, :]) * (1.0 - t))
            t = jnp.tanh(v)
            high, low = split((v + v) * (t + wide(par[3, here, :]) * (1.0 - t)))
            cath[slot, sub, :] = high
            catl[slot, sub, :] = low

    @pl.loop(0, blocks)
    def _(b):
        at = pl.ds(pl.multiple_of(b * W, W), W)
        for h in range(hops):

            @pl.when(b > 0)
            def _():
                for part in range(2):
                    cat_copy(h, b - 1, h, part).wait()

        for h in range(hops):
            hop_act(h, b, h)
            for part in range(2):
                cat_copy(h, b, h, part).start()
            here = slice(h * W, (h + 1) * W)
            part_sum = dot3(wmh[here, :], wml[here, :], cath[h], catl[h])
            if h == 0:
                x[at, :] = part_sum
            else:
                x[at, :] += part_sum

    for h in range(hops):
        for part in range(2):
            cat_copy(h, blocks - 1, h, part).wait()

    acc[0] = jnp.zeros((W, 128), F32)

    @pl.loop(0, blocks)
    def _(b):
        at = pl.ds(pl.multiple_of(b * W, W), W)
        acc[0] += fold(x[at, :] * mask[0:1, at])

    mean_here2 = lane_sum(acc[0]) / here_count
    acc[1] = jnp.zeros((W, 128), F32)

    @pl.loop(0, blocks)
    def _(b):
        at = pl.ds(pl.multiple_of(b * W, W), W)
        off = (x[at, :] - wide(mean_here2)) * mask[0:1, at]
        acc[1] += fold(off * off)

    got2[me, 0:1, :] = to_row(mean_here2)
    got2[me, 1:2, :] = to_row(lane_sum(acc[1]))
    send_all(got2, 2)

    plain_load.wait()
    for h in range(hops):
        high, low = split(dwm[h * W : (h + 1) * W, :])
        wmh[h * W : (h + 1) * W, :] = high
        wml[h * W : (h + 1) * W, :] = low

    classes = bias.shape[1]
    kinds = 48
    ext[SMALL : SMALL + kinds, :] = jnp.zeros((kinds, W), F32)
    ext[SMALL : SMALL + classes, :] = out_t[...]
    oh, ol = split(ext[SMALL : SMALL + kinds, :])
    nh, nl = split(ext[SMALL : SMALL + kinds, :].T)
    vec[6:7, :] = jnp.zeros((1, W), F32)
    vec[6:7, 0:classes] = bias[...]
    bias_col = wide(to_column(vec[6:7, 0:128])[0:kinds, :])

    wait_all(got2, 2)
    every_count = got1[:, 1:2, 2 * W : 3 * W]
    mean2 = jnp.sum(got2[:, 0:1, :] * every_count, axis=0) / total
    off = got2[:, 0:1, :] - mean2
    vec[3:4, :] = jnp.sum(got2[:, 1:2, :] + off * off * every_count, axis=0)
    inv2 = lax.rsqrt(vec[3:4, :] / total + 1e-05)
    mcol[3] = to_column(mean2)
    mcol[4] = to_column(inv2)
    mcol[2] = 0.5 + 0.5 * mcol[2]

    for b in range(blocks):
        for part in range(2):
            cat_load(0, b, b % 4, part).start()

    for j in range(4):
        acc[j] = jnp.zeros((W, 128), F32)
    ext[SMALL : SMALL + 64, :] = jnp.zeros((64, W), F32)
    kind = lax.broadcasted_iota(jnp.int32, (kinds, W), 0)

    @pl.loop(0, blocks)
    def _(b):
        at = pl.ds(pl.multiple_of(b * W, W), W)
        live = mask[0:1, at]
        normed = (x[at, :] - wide(mcol[3])) * wide(mcol[4])
        v = 0.5 * (normed * wide(mcol[0]) + wide(mcol[1]))
        t = jnp.tanh(v)
        keep = wide(mcol[2])
        rest = 1.0 - t
        ah, al = split((v + v) * (t + keep * rest))
        q = v * rest
        logits = dot3(oh, ol, ah, al) + bias_col
        logits = jnp.where(kind < classes, logits, -1e30)
        top = jnp.max(logits, axis=0, keepdims=True)
        e = jnp.exp(logits - top)
        norm = jnp.sum(e, axis=0, keepdims=True)
        logp = logits - top - jnp.log(norm)
        hit = kind == lab[0:1, at]
        loss = jnp.sum(jnp.where(hit, logp, 0.0), axis=0, keepdims=True) * live
        back = (e / norm - jnp.where(hit, 1.0, 0.0)) * (live / total)
        bh, bl = split(back)
        ext[SMALL : SMALL + kinds, :] += dot3(bh, bl, ah, al, NT)
        ext[SMALL + 49 : SMALL + 50, :] -= loss
        acc[3, 0:kinds, :] += fold(back)
        grad = dot3(nh, nl, bh, bl)
        acc[0] += fold(grad * q)
        m = t + q + q * t
        grad = grad * (m + keep * (1.0 - m))
        dwm[at, :] = grad
        acc[1] += fold(grad)
        acc[2] += fold(grad * normed)

    ext[SMALL + 48 : SMALL + 49, :] = to_row(lane_sum(acc[0]))
    ext[SMALL + 50 : SMALL + 51, 0:128] = to_row(lane_sum(acc[3])[0:128, :])
    got3[me, 0:1, :] = to_row(lane_sum(acc[1]))
    got3[me, 1:2, :] = to_row(lane_sum(acc[2]))
    send_all(got3, 3)
    wait_all(got3, 3)
    vec[2:4, :] = jnp.sum(got3[...], axis=0)
    stats[0:2, :] = vec[2:4, :]
    shift_part = to_column(vec[2:3, :] / total)
    gain_part = to_column(vec[3:4, :] / total)
    factor = mcol[0] * mcol[4]

    @pl.loop(0, blocks)
    def _(b):
        at = pl.ds(pl.multiple_of(b * W, W), W)
        normed = (x[at, :] - wide(mcol[3])) * wide(mcol[4])
        grad = dwm[at, :] - wide(shift_part) - normed * wide(gain_part)
        high, low = split(grad * wide(factor) * mask[0:1, at])
        pgh[at, :] = high
        pgl[at, :] = low

    bits = n.bit_length() - 1

    def bit_of(b):
        return lax.rem(me // (1 << b), 2)

    def across(b):
        return me + (1 << b) * (1 - 2 * bit_of(b))

    def remote(src, dst, send, recv, to):
        return pltpu.make_async_remote_copy(
            src, dst, send, recv, device_id=(to,), device_id_type=MESH
        )

    def wait_bytes(ref, sem):
        pltpu.make_async_copy(ref, ref, sem).wait()

    for b in range(bits):
        pl.semaphore_signal(credit, inc=1, device_id=(across(b),), device_id_type=MESH)

    far = list(range(3, bits))
    orders = [[1, 2] + far, [2, 1] + far, [1] + far + [2], [2] + far + [1]]
    span = W // len(orders)

    def halving(batch, base, size, take):
        def rows_at(off, length):
            return pl.ds(pl.multiple_of(off, 8), length)

        half = size // 2
        tmps = [take(half)]
        levels = [
            [(0, slice(0, W), base + bit_of(0) * half, base + (1 - bit_of(0)) * half, half, tmps[0][1])]
        ]
        rest_tmp, at = take(half)
        tmps += [(rest_tmp, at)] * (bits - 1)
        offs = [base + bit_of(0) * half] * len(orders)
        length = half
        for j in range(bits - 1):
            length //= 2
            level = []
            for q in range(len(orders)):
                b = orders[q][j]
                keep = offs[q] + bit_of(b) * length
                give = offs[q] + (1 - bit_of(b)) * length
                level.append((b, slice(q * span, (q + 1) * span), keep, give, length, at))
                offs[q] = keep
            at += length
            levels.append(level)

        stages = []
        for k, level in enumerate(levels):
            send, recv = sum_send.at[batch, k], sum_recv.at[batch, k]
            free = freed.at[batch, k]
            length, first = level[0][4:]
            tmp = tmps[k][0]
            arrived = tmp.at[first : first + length, :]

            def start(level=level, send=send, recv=recv, tmp=tmp):
                for b, lanes, keep, give, ln, t in level:
                    remote(
                        dwm.at[rows_at(give, ln), lanes], tmp.at[t : t + ln, lanes],
                        send, recv, across(b),
                    ).start()

            def finish(level=level, send=send, recv=recv, free=free, arrived=arrived, tmp=tmp):
                wait_bytes(arrived, send)
                wait_bytes(arrived, recv)
                for b, lanes, keep, give, ln, t in level:
                    pl.semaphore_signal(
                        free, inc=1, device_id=(across(b),), device_id_type=MESH
                    )
                    dwm[rows_at(keep, ln), lanes] += tmp[t : t + ln, lanes]

            stages.append((start, finish))
        for k in range(bits - 1, -1, -1):
            level = levels[k]
            send, recv = sum_send.at[batch, bits + k], sum_recv.at[batch, bits + k]
            free = freed.at[batch, k]
            length, first = level[0][4:]
            arrived = tmps[k][0].at[first : first + length, :]

            def start(level=level, send=send, recv=recv, free=free):
                pl.semaphore_wait(free, len(level))
                for b, lanes, keep, give, ln, t in level:
                    here = dwm.at[rows_at(keep, ln), lanes]
                    remote(here, here, send, recv, across(b)).start()

            def finish(send=send, recv=recv, arrived=arrived):
                wait_bytes(arrived, send)
                wait_bytes(arrived, recv)

            stages.append((start, finish))
        return stages

    chips = n // 2
    core, chip = lax.rem(me, 2), me // 2
    half_lanes = W // 2
    mine = pl.ds(pl.multiple_of(core * half_lanes, 128), half_lanes)
    other = pl.ds(pl.multiple_of((1 - core) * half_lanes, 128), half_lanes)

    def direct(batch, base, size, rows_each, tmp_base, tmp_lane):
        owners = size // rows_each
        cols = slice(tmp_lane, tmp_lane + half_lanes)
        block = pl.ds(base, size)
        from_core = tab.at[tmp_base : tmp_base + size, cols]
        first = tmp_base + size
        slot = tab.at[pl.ds(pl.multiple_of(first + chip * rows_each, 8), rows_each), cols]
        summed = own.at[batch, 0:rows_each, :]
        sends = [part_send.at[batch, k] for k in range(4)]
        recvs = [part_recv.at[batch, k] for k in range(4)]

        def many(k):
            return tab.at[first : first + rows_each * k, cols]

        def piece(q):
            return pl.ds(pl.multiple_of(base + q * rows_each, 8), rows_each)

        def start():
            remote(ext.at[block, other], from_core, sends[0], recvs[0], across(0)).start()

        def spread():
            wait_bytes(from_core, sends[0])
            wait_bytes(from_core, recvs[0])
            ext[block, mine] += tab[tmp_base : tmp_base + size, cols]

            @pl.loop(0, owners)
            def _(k):
                q = lax.rem(chip + k, owners)

                @pl.when(q == chip)
                def _():
                    pltpu.make_async_copy(ext.at[piece(q), mine], slot, recvs[1]).start()

                @pl.when(q != chip)
                def _():
                    remote(ext.at[piece(q), mine], slot, sends[1], recvs[1], q * 2 + core).start()

        def middle():
            @pl.when(chip < owners)
            def _():
                wait_bytes(many(owners - 1), sends[1])
                wait_bytes(many(chips), recvs[1])
                out = tab[first : first + rows_each, cols]
                for d in range(1, chips):
                    at = first + rows_each * d
                    out = out + tab[at : at + rows_each, cols]
                own[batch, 0:rows_each, :] = out
                there = res.at[piece(chip), mine]
                pltpu.make_async_copy(summed, there, recvs[2]).start()

                @pl.loop(1, chips)
                def _(k):
                    to = lax.rem(chip + k, chips) * 2 + core
                    remote(summed, there, sends[2], recvs[2], to).start()

            @pl.when(chip >= owners)
            def _():
                wait_bytes(many(owners), sends[1])

        def join():
            wait_bytes(res.at[block, mine], recvs[2])

            @pl.when(chip < owners)
            def _():
                wait_bytes(many(chips - 1), sends[2])

            here = res.at[block, mine]
            remote(here, here, sends[3], recvs[3], across(0)).start()

        def finish():
            wait_bytes(res.at[block, other], sends[3])
            wait_bytes(res.at[block, other], recvs[3])

        return [start, spread, middle, join, finish]

    mid_batch = max(W, 8 * n)
    mids = hops * W // mid_batch
    DW, HB, GAP = 1.0, 2.1, 4.5
    PART = (4.2, 6.3, 6.3, 4.2)
    clock = [(t + 1) * DW for t in range(hops * blocks)]
    clock += [clock[-1] + (t + 1) * HB for t in range(hops * blocks)]
    spare = hops * rows
    part_rows = 208 + 16 * chips
    spots = [(x, W, x.shape[0] - W), (tab, spare + part_rows, tab.shape[0] - spare - part_rows)]

    def take(size):
        spot = next(i for i in range(2) if spots[i][2] >= size)
        ref, first, left = spots[spot]
        spots[spot] = (ref, first + size, left - size)
        return ref, first

    events = []
    for k in range(mids):
        stages = halving(k, k * mid_batch, mid_batch, take)
        when = clock[(k + 1) * mid_batch // W * blocks - 1]
        for j in range(len(stages) + 1):
            todo = []
            if j:
                todo.append(stages[j - 1][1])
            elif k == 0:
                todo.append(lambda: pl.semaphore_wait(credit, bits))
            if j < len(stages):
                todo.append(stages[j][0])
            else:
                todo.append(lambda k=k: mid_out(k).start())
            events.append((when, len(events), todo))
            when += GAP
    ends = [clock[hops * blocks + (h + 1) * blocks - 1] for h in range(hops)]
    for batch, (when, base, size, rows_each) in enumerate(
        (
            (clock[0], 0, HOPS_AT, 16),
            (ends[1], hop_row(0), 208, 16),
            (ends[2], hop_row(2), 104, 8),
            (ends[3], hop_row(3), 104, 8),
        )
    ):
        stages = direct(batch, base, size, rows_each, spare, batch % 2 * half_lanes)
        for j, stage in enumerate(stages):
            at = when + sum(PART[:j])
            if batch == 1:
                at = min(at, ends[3] - 1e-3)
            events.append((at, len(events), [stage]))

    ticks = {}
    for when, _, todo in sorted(events, key=lambda e: e[:2]):
        tick = next((t for t, c in enumerate(clock) if c >= when - 1e-6), len(clock))
        ticks.setdefault(tick, []).extend(todo)

    def mid_out(k):
        here = slice(k * mid_batch, (k + 1) * mid_batch)
        return pltpu.make_async_copy(dwm.at[here], mid_sum.at[here], table_sem.at[k])

    def act(tick):
        for todo in ticks.get(tick, []):
            todo()

    for h in range(hops):
        here = slice(h * W, (h + 1) * W)

        @pl.loop(0, blocks)
        def _(b):
            at = pl.ds(pl.multiple_of(b * W, W), W)
            slot = lax.rem(b, 4)
            for part in range(2):
                cat_load(h, b, slot, part).wait()
            part_sum = dot3(cath[slot], catl[slot], pgh[at, :], pgl[at, :], NT)
            if h + 1 < hops:
                for part in range(2):
                    cat_load(h + 1, b, slot, part).start()

            @pl.when(b == 0)
            def _():
                dwm[here, :] = part_sum

            @pl.when(b > 0)
            def _():
                dwm[here, :] += part_sum

            for t in range(blocks):
                if ticks.get(h * blocks + t):

                    @pl.when(b == t)
                    def _():
                        act(h * blocks + t)

    grads = (x.at[0:W], cg)

    def head_back(h, b, rs):
        at = pl.ds(b * W, W)
        here = pl.ds(pl.multiple_of(h * W + rs.start, 128), rs.stop - rs.start)
        return dot3(wmh[here, :], wml[here, :], pgh[at, :], pgl[at, :])

    def weight_back(h, b, rs):
        window = pl.ds(pl.multiple_of(jnp.maximum(h - 1, 0) * 128, 128), WIN)
        at = pl.ds(b * W, W)
        part_sum = dot3(
            cath[b % 2, rs, :], catl[b % 2, rs, :], xh[window, at], xl[window, at], NT
        )
        if b == 0:
            hop_grad[rs, :] = part_sum
        else:
            hop_grad[rs, :] += part_sum

    def act_back(h, b, c):
        sub = slice(c * 64, (c + 1) * 64)
        col = pl.ds(pl.multiple_of(h * W + c * 64, 64), 64)
        grad = grads[b % 2][sub, :]
        pre = tab[pl.ds(pl.multiple_of((h * blocks + b) * W + c * 64, 64), 64), :]
        keep1, keep2 = wide(par[2, col, :]), wide(par[3, col, :])
        u = pre * wide(par[0, col, :]) + wide(par[1, col, :])
        t1 = jnp.tanh(u)
        r1 = 1.0 - t1
        v = u * (t1 + keep1 * r1)
        t2 = jnp.tanh(v)
        q = v * (1.0 - t2)
        sum2 = fold(grad * q)
        m = t2 + q + q * t2
        grad = grad * (m + keep2 * (1.0 - m))
        q = u * r1
        sum1 = fold(grad * q)
        m = t1 + q + q * t1
        grad = grad * (m + keep1 * (1.0 - m))
        for j, value in enumerate((sum2, sum1, fold(grad))):
            if b == 0:
                acc[j, sub, :] = value
            else:
                acc[j, sub, :] += value
        high, low = split(grad)
        cath[b % 2, sub, :] = high
        catl[b % 2, sub, :] = low

    halves = (slice(0, W // 2), slice(W // 2, W))
    grads[0][...] = head_back(0, 0, slice(0, W))

    @pl.loop(0, hops)
    def _(h):
        for b in range(blocks):
            for m, rs in enumerate(halves):
                if b + 1 < blocks:
                    grads[(b + 1) % 2][rs, :] = head_back(h, b + 1, rs)
                else:
                    grads[(b + 1) % 2][rs, :] = head_back(jnp.minimum(h + 1, hops - 1), 0, rs)
                if b:
                    weight_back(h, b - 1, rs)
                for c in range(4 * m, 4 * m + 4):
                    act_back(h, b, c)
            if b + 1 < blocks:
                for t in range(hops):
                    if ticks.get(hops * blocks + t * blocks + b):

                        @pl.when(h == t)
                        def _():
                            act(hops * blocks + t * blocks + b)

        weight_back(h, blocks - 1, slice(0, W))
        for t in range(hops):

            @pl.when(h == t)
            def _():
                sums = lane_sum(acc[2])
                offset = delta[n : n + 1, win_start(t) : win_start(t) + WIN]
                tall = hop_grad[...] + jnp.concatenate([sums] * 2, axis=1) * offset
                first = hop_row(t)
                start = t * width - win_start(t)
                cg[0:WIN, :] = tall.T
                ext[first : first + width, :] = cg[start : start + width, :]
                for j in range(3):
                    row = first + width + j
                    ext[row : row + 1, :] = to_row(lane_sum(acc[j]))
                act(hops * blocks + t * blocks + blocks - 1)

    act(len(clock))
    rest_out = pltpu.make_async_copy(res, rest_sum, load_sem.at[0])
    rest_out.start()
    for k in range(mids):
        mid_out(k).wait()
    rest_out.wait()


GRAM, SMALL, HOPS_AT = 0, 104, 176


def hop_row(h):
    return HOPS_AT + h * 104


def final_kernel(
    mid_sum, rest_sum, stats_sum, weights_in, gain, loss, hop_w, hop_g, hop_s, hop_l, cat_l, mid_w,
    mid_g, mid_s, mid_l, out_w, out_b, buf, wide_w, rest, stats, weights, sem,
):
    parts = 4
    size = mid_sum.shape[0] // parts

    def load(k):
        here = slice(k * size, (k + 1) * size)
        return pltpu.make_async_copy(mid_sum.at[here], buf.at[here], sem.at[0, k])

    def store(k):
        here = slice(k * size, (k + 1) * size)
        return pltpu.make_async_copy(buf.at[here], mid_w.at[here], sem.at[1, k])

    loads = [
        pltpu.make_async_copy(src, dst, sem.at[2, k])
        for k, (src, dst) in enumerate(((rest_sum, rest), (stats_sum, stats), (weights_in, weights)))
    ]
    for copy in loads:
        copy.start()
    for k in range(parts):
        load(k).start()
    for copy in loads:
        copy.wait()
    total = stats[2:3, :]
    width, hops, _ = weights.shape
    wide_w[...] = jnp.zeros_like(wide_w)
    for h in range(hops):
        first = hop_row(h)
        raw = rest[first : first + width, :]
        weight = weights[:, h, :]
        inv = stats[3 + h : 4 + h, :]
        gain_grad = inv * jnp.sum(weight * raw, axis=0, keepdims=True)
        wide_w[0:width, :] = weight
        along = lax.dot_general(
            rest[GRAM : GRAM + 104, h * 128 : (h + 1) * 128], wide_w[...], NN,
            precision=lax.Precision.HIGHEST, preferred_element_type=F32,
        )[0:width, :]
        grad = raw - along * (inv * gain_grad / total)
        hop_w[:, h, :] = gain[h : h + 1, :] * inv * grad
        hop_g[h : h + 1, :] = gain_grad
        cat_l[0:1, h * W : (h + 1) * W] = rest[first + width : first + width + 1, :]
        hop_l[h : h + 1, :] = rest[first + width + 1 : first + width + 2, :]
        hop_s[h : h + 1, :] = rest[first + width + 2 : first + width + 3, :]
        load(h).wait()
        store(h).start()
    mid_s[...] = stats[0:1, :]
    mid_g[...] = stats[1:2, :]
    mid_l[...] = rest[SMALL + 48 : SMALL + 49, :]
    out_w[...] = rest[SMALL : SMALL + out_w.shape[0], :]
    out_b[...] = rest[SMALL + 50 : SMALL + 51, 0 : out_b.shape[1]]
    loss[...] = jnp.sum(rest[SMALL + 49 : SMALL + 50, :], axis=1, keepdims=True) / total[:, 0:1]
    for k in range(parts):
        store(k).wait()


def on_device(
    node_table, batch_nodes, send_counts, labels, hop_weight, hop_gain, hop_shift, hop_slope,
    cat_slope, mid_weight, mid_gain, mid_shift, mid_slope, out_weight, out_bias,
):
    n = lax.axis_size("nodes")
    node_rows, feats = node_table.shape
    rows = batch_nodes.shape[0]
    slots = rows // n
    hops, width, units = hop_weight.shape
    blocks = rows // W
    classes = out_weight.shape[1]
    vmem = pl.BlockSpec(memory_space=pltpu.VMEM)
    hbm = pl.BlockSpec(memory_space=pl.ANY)
    shape = jax.ShapeDtypeStruct
    bits = n.bit_length() - 1
    mid_batch = max(W, 8 * n)
    sums = hops * W // mid_batch
    small_rows = HOPS_AT + 104 * hops
    halves = 2 * sums - (hops * W - W) // (mid_batch // 2)
    spill = 208 + 8 * n + halves * mid_batch // 2
    tab_rows = max(node_rows, hops * rows + spill)
    weights = hop_weight.transpose(1, 0, 2)
    mid_sum, rest_sum, stats, _ = pl.pallas_call(
        functools.partial(main_kernel, n, slots),
        out_shape=(
            shape((hops * units, W), F32),
            shape((small_rows, W), F32),
            shape((8, W), F32),
            shape((2, hops, blocks, W, W), BF16),
        ),
        in_specs=[hbm, vmem, vmem, pl.BlockSpec(memory_space=pltpu.SMEM), vmem, hbm] + [vmem] * 9,
        out_specs=(hbm, hbm, vmem, hbm),
        scratch_shapes=[
            pltpu.VMEM((tab_rows, 512), F32),
            pltpu.VMEM((max(rows, hops * W), W), F32),
            pltpu.VMEM((max(rows, hops * W), W), F32),
            pltpu.VMEM((512, rows), BF16),
            pltpu.VMEM((512, rows), BF16),
            pltpu.VMEM((hops * W, W), BF16),
            pltpu.VMEM((hops * W, W), BF16),
            pltpu.VMEM((max(rows, hops * W), W), BF16),
            pltpu.VMEM((max(rows, hops * W), W), BF16),
            pltpu.VMEM((4, W, W), BF16),
            pltpu.VMEM((4, W, W), BF16),
            pltpu.VMEM((4, hops * W, 128), F32),
            pltpu.VMEM((5, W, 128), F32),
            pltpu.VMEM((4, W, 128), F32),
            pltpu.VMEM((8, W), F32),
            pltpu.VMEM((1, rows), F32),
            pltpu.VMEM((1, rows), jnp.int32),
            pltpu.VMEM((n + 8, W), F32),
            pltpu.VMEM((small_rows, W), F32),
            pltpu.VMEM((small_rows, W), F32),
            pltpu.VMEM((4, 16, W // 2), F32),
            pltpu.VMEM((W, WIN), F32),
            pltpu.VMEM((W, W), F32),
            pltpu.SMEM((n, 2, 128), jnp.int32),
            pltpu.VMEM((n, 2, 128), jnp.int32),
            pltpu.VMEM((n, 2, 128), jnp.int32),
            pltpu.VMEM((n, 2, 3 * W), F32),
            pltpu.VMEM((n, 2, W), F32),
            pltpu.VMEM((n, 2, W), F32),
            pltpu.SemaphoreType.DMA((4,)),
            pltpu.SemaphoreType.DMA((4,)),
            pltpu.SemaphoreType.DMA((sums, 2 * bits)),
            pltpu.SemaphoreType.DMA((sums, 2 * bits)),
            pltpu.SemaphoreType.DMA((4, 4)),
            pltpu.SemaphoreType.DMA((4, 4)),
            pltpu.SemaphoreType.REGULAR,
            pltpu.SemaphoreType.REGULAR((sums, bits)),
            pltpu.SemaphoreType.DMA((8,)),
            pltpu.SemaphoreType.DMA((2,)),
            pltpu.SemaphoreType.DMA((2, 4)),
        ],
        compiler_params=pltpu.CompilerParams(
            collective_id=0, has_side_effects=True, vmem_limit_bytes=66_900_000
        ),
    )(
        node_table.T, batch_nodes.reshape(rows // 128, 128), labels.reshape(rows // 128, 128),
        send_counts, weights, mid_weight, hop_gain, hop_shift, hop_slope,
        cat_slope.reshape(1, hops * units), mid_gain.reshape(1, W), mid_shift.reshape(1, W),
        mid_slope.reshape(1, W), out_weight.T, out_bias.reshape(1, classes),
    )
    (
        loss, hop_w, hop_g, hop_s, hop_l, cat_l, mid_w, mid_g, mid_s, mid_l, out_w, out_b,
    ) = pl.pallas_call(
        final_kernel,
        out_shape=(
            shape((1, 1), F32), shape((width, hops, units), F32), shape((hops, units), F32),
            shape((hops, units), F32), shape((hops, units), F32), shape((1, hops * units), F32),
            shape((hops * units, W), F32), shape((1, W), F32), shape((1, W), F32),
            shape((1, W), F32), shape((classes, W), F32), shape((1, classes), F32),
        ),
        in_specs=[hbm] * 4 + [vmem],
        out_specs=(vmem,) * 6 + (hbm,) + (vmem,) * 5,
        scratch_shapes=[
            pltpu.VMEM((hops * units, W), F32),
            pltpu.VMEM((128, W), F32),
            pltpu.VMEM((small_rows, W), F32),
            pltpu.VMEM((8, W), F32),
            pltpu.VMEM((width, hops, units), F32),
            pltpu.SemaphoreType.DMA((3, 4)),
        ],
        compiler_params=pltpu.CompilerParams(vmem_limit_bytes=62 * 2**20),
    )(mid_sum, rest_sum, stats, weights, hop_gain)
    return (
        loss.reshape(()), hop_w.transpose(1, 0, 2), hop_g, hop_s, hop_l, cat_l.reshape(-1),
        mid_w, mid_g.reshape(-1), mid_s.reshape(-1), mid_l.reshape(-1), out_w.T,
        out_b.reshape(-1),
    )


def solution(mesh):
    placed = (P("nodes", None), P("nodes"), P("nodes", None), P("nodes")) + (P(),) * 11
    return jax.shard_map(
        on_device, mesh=mesh, in_specs=placed, out_specs=(P(),) * 12, check_vma=False
    )
```

```python
import functools

import jax
import jax.numpy as jnp
from jax import lax
from jax.experimental import pallas as pl
from jax.experimental.pallas import tpu as pltpu
from jax.sharding import PartitionSpec as P

MESH = pl.DeviceIdType.MESH
F32, BF16 = jnp.float32, jnp.bfloat16
NN = (((1,), (0,)), ((), ()))
NT = (((1,), (1,)), ((), ()))
W = 512
WIN = 256


def win_start(hop):
    return max(hop - 1, 0) * 128


def split(values):
    high = values.astype(BF16)
    return high, (values - high.astype(F32)).astype(BF16)


def dot(a, b, dims):
    return lax.dot_general(a, b, dims, preferred_element_type=F32)


def dot3(ah, al, bh, bl, dims=NN):
    (da,), (db,) = dims[0]
    return dot(
        jnp.concatenate([ah, al, ah], da), jnp.concatenate([bh, bh, bl], db), dims
    )


def wide(column):
    return jnp.concatenate([column] * (W // 128), axis=1)


def fold(values):
    out = values[:, 0:128]
    for tile in range(1, W // 128):
        out = out + values[:, tile * 128 : (tile + 1) * 128]
    return out


def lane_sum(values):
    return jnp.broadcast_to(jnp.sum(values, axis=1, keepdims=True), values.shape)


def to_row(column):
    return column.T[0:1, :]


def to_column(row):
    return jnp.broadcast_to(row, (128, row.shape[1])).T


def main_kernel(
    n,
    slots,
    table,
    nodes,
    labels,
    counts,
    weights,
    mid_weight,
    gain,
    shift,
    slope,
    cat_slope,
    mid_gain,
    mid_shift,
    mid_slope,
    out_t,
    bias,
    mid_sum,
    rest_sum,
    stats,
    cat_hbm,
    tab,
    x,
    dwm,
    xh,
    xl,
    wmh,
    wml,
    pgh,
    pgl,
    cath,
    catl,
    par,
    mcol,
    acc,
    vec,
    mask,
    lab,
    delta,
    ext,
    res,
    own,
    hop_grad,
    cg,
    ids,
    pack,
    got0,
    got1,
    got2,
    got3,
    send_sem,
    recv_sem,
    sum_send,
    sum_recv,
    part_send,
    part_recv,
    credit,
    freed,
    table_sem,
    load_sem,
    cat_sem,
):
    me = lax.axis_index("nodes")
    rows = slots * n
    blocks = rows // W
    feats, node_rows = table.shape
    hops = 4
    chunk = next(c for c in (512, 384, 256, 128) if node_rows % c == 0)
    chunks = node_rows // chunk
    depth = min(dwm.shape[0] // feats, chunks)

    def peer(k):
        return lax.rem(me + k, n)

    def table_copy(i, slot):
        return pltpu.make_async_copy(
            table.at[:, pl.ds(pl.multiple_of(i * chunk, 128), chunk)],
            dwm.at[pl.ds(pl.multiple_of(slot * feats, 8), feats), 0:chunk],
            table_sem.at[slot],
        )

    def send_all(buf, e):
        @pl.loop(1, n, unroll=n - 1)
        def _(k):
            pltpu.make_async_remote_copy(
                buf.at[me], buf.at[me], send_sem.at[e], recv_sem.at[e],
                device_id=(peer(k),), device_id_type=MESH,
            ).start()

    def wait_all(buf, e):
        others = buf.at[pl.ds(0, n - 1)]
        pltpu.make_async_copy(others, others, send_sem.at[e]).wait()
        pltpu.make_async_copy(others, others, recv_sem.at[e]).wait()

    for i in range(depth):
        table_copy(i, i).start()
    weight_load = pltpu.make_async_copy(mid_weight, x, load_sem.at[0])
    weight_load.start()

    barrier = pltpu.get_barrier_semaphore()

    @pl.loop(1, n)
    def _(k):
        pl.semaphore_signal(barrier, inc=1, device_id=(peer(k),), device_id_type=MESH)

    ext[...] = jnp.zeros_like(ext)
    for h in range(hops):
        here = slice(h * W, (h + 1) * W)
        par[0, here, :] = to_column(gain[h : h + 1, :])
        par[1, here, :] = to_column(shift[h : h + 1, :])
        par[2, here, :] = to_column(0.5 + 0.5 * slope[h : h + 1, :])
        par[3, here, :] = to_column(0.5 + 0.5 * cat_slope[0:1, here])
    for j, row in enumerate((mid_gain, mid_shift, mid_slope)):
        mcol[j] = to_column(row[...])

    per = 128 // slots
    lane8 = lax.broadcasted_iota(jnp.int32, (8, 128), 1)

    @pl.loop(0, rows // 128)
    def _(j):
        own = jnp.broadcast_to(nodes[pl.ds(j, 1), :], (8, 128))
        names = jnp.broadcast_to(labels[pl.ds(j, 1), :], (8, 128))
        for q in range(per):
            d = j * per + q
            turn = (128 - q * slots) % 128
            ids_row = pltpu.roll(own, turn, 1) if q else own
            names_row = pltpu.roll(names, turn, 1) if q else names
            names_row = jnp.where(lane8 == 127, counts[0, d], names_row)
            place_row = jnp.clip(ids_row - d * node_rows, 0, node_rows - 1)
            pack[d, 0:1, :] = place_row[0:1, :]
            pack[d, 1:2, :] = names_row[0:1, :]

    pl.semaphore_wait(barrier, n - 1)
    got0[me] = pack[me]

    @pl.loop(1, n)
    def _(k):
        pltpu.make_async_remote_copy(
            pack.at[peer(k)], got0.at[me], send_sem.at[0], recv_sem.at[0],
            device_id=(peer(k),), device_id_type=MESH,
        ).start()

    @pl.loop(0, chunks)
    def _(i):
        slot = lax.rem(i, depth)
        table_copy(i, slot).wait()
        for k in range(chunk // 128):
            tab[pl.ds(pl.multiple_of(i * chunk + k * 128, 128), 128), 0:feats] = dwm[
                pl.ds(pl.multiple_of(slot * feats, 8), feats), k * 128 : (k + 1) * 128
            ].T

        @pl.when(i + depth < chunks)
        def _():
            table_copy(i + depth, slot).start()

    plain_load = pltpu.make_async_copy(mid_weight, dwm, load_sem.at[0])
    width = weights.shape[0]
    for h in range(hops):
        start = h * width - win_start(h)
        ext[0:WIN, :] = jnp.zeros((WIN, W), F32)
        ext[start : start + width, :] = weights[:, h, :]
        high, low = split(ext[0:WIN, :].T)
        pgh[h * W : (h + 1) * W, 0:WIN] = high
        pgh[h * W : (h + 1) * W, WIN : 2 * WIN] = low

    weight_load.wait()
    for h in range(hops):
        high, low = split(x[h * W : (h + 1) * W, :].T)
        wmh[h * W : (h + 1) * W, :] = high
        wml[h * W : (h + 1) * W, :] = low
    plain_load.start()

    wait_all(got0, 0)

    to_smem = pltpu.make_async_copy(got0, ids, load_sem.at[1])
    to_smem.start()
    to_smem.wait()

    step = min(slots, 32)

    @pl.loop(0, n)
    def _(s):
        @pl.loop(0, slots // step)
        def _(g):
            for first in range(0, step, 8):
                at = g * step + first
                x[pl.ds(pl.multiple_of(s * slots + at, 8), 8), :] = jnp.concatenate(
                    [tab[pl.ds(ids[s, 0, at + k], 1), :] for k in range(8)], axis=0
                )

    @pl.loop(0, rows // 128)
    def _(j):
        live = jnp.zeros((8, 128), F32)
        names = jnp.zeros((8, 128), jnp.int32)
        for q in range(per):
            s = j * per + q
            mine = (lane8 >= q * slots) & (lane8 < (q + 1) * slots)
            live = live + jnp.where(
                mine & (lane8 < q * slots + ids[s, 1, 127]), 1.0, 0.0
            )
            row = jnp.broadcast_to(got0[s, 1:2, :], (8, 128))
            if q:
                row = pltpu.roll(row, q * slots, 1)
            names = jnp.where(mine, row, names)
        at = pl.ds(pl.multiple_of(j * 128, 128), 128)
        mask[0:1, at] = live[0:1, :]
        lab[0:1, at] = names[0:1, :]

    here_count = jnp.broadcast_to(
        jnp.sum(mask[...], axis=1, keepdims=True), (1, 128)
    )
    acc[0] = jnp.zeros((W, 128), F32)
    top_row = lax.broadcasted_iota(jnp.int32, (128, W), 0)

    @pl.loop(0, blocks)
    def _(b):
        at = pl.ds(pl.multiple_of(b * W, W), W)
        live = mask[0:1, at]
        for f in range(4):
            block = x[at, f * 128 : (f + 1) * 128].T
            if (f + 1) * 128 > feats:
                block = jnp.where(top_row < feats - f * 128, block, 0.0)
            tab[pl.ds(pl.multiple_of(b * W + f * 128, 128), 128), :] = block
            acc[0, f * 128 : (f + 1) * 128, :] += fold(block * live)

    mean_here = lane_sum(acc[0]) / here_count

    @pl.loop(0, blocks)
    def _(b):
        at = pl.ds(pl.multiple_of(b * W, W), W)
        live = mask[0:1, at]
        high, low = split((tab[at, :] - wide(mean_here)) * live)
        xh[:, at] = high
        xl[:, at] = low

    def pre_at(h, b):
        return pl.ds(pl.multiple_of((h * blocks + b) * W, W), W)

    for h in range(hops):
        wh = pgh[h * W : (h + 1) * W, 0:WIN]
        wl = pgh[h * W : (h + 1) * W, WIN : 2 * WIN]
        window = slice(win_start(h), win_start(h) + WIN)
        acc[h] = jnp.zeros((W, 128), F32)

        @pl.loop(0, blocks, unroll=4)
        def _(b):
            at = pl.ds(pl.multiple_of(b * W, W), W)
            pre = dot3(wh, wl, xh[window, at], xl[window, at])
            tab[pre_at(h, b), :] = pre
            acc[h] += fold(pre * pre)

    for h in range(hops):
        row = to_row(lane_sum(acc[h]))
        if h < 3:
            got1[me, 0:1, h * W : (h + 1) * W] = row
        else:
            got1[me, 1:2, 0:W] = row
    got1[me, 1:2, W : 2 * W] = to_row(mean_here)
    got1[me, 1:2, 2 * W : 3 * W] = wide(here_count)
    send_all(got1, 1)

    for h in range(hops):
        if h != 1:
            window = slice(win_start(h), win_start(h) + WIN)
            products = dot3(xh[window, :], xl[window, :], xh[window, :], xl[window, :], NT)
        start = h * width - win_start(h)
        hop_grad[0:WIN, :] = products
        part = pltpu.roll(hop_grad[start : start + 104, :], (WIN - start) % WIN, 1)
        ext[GRAM : GRAM + 104, h * 128 : (h + 1) * 128] = part[:, 0:128]

    wait_all(got1, 1)

    delta[...] = jnp.zeros_like(delta)
    every_count = got1[:, 1:2, 2 * W : 3 * W]
    vec[0:1, :] = jnp.sum(every_count, axis=0)
    vec[1:2, :] = jnp.sum(every_count * got1[:, 1:2, W : 2 * W], axis=0)
    for h in range(3):
        vec[2 + h : 3 + h, :] = jnp.sum(got1[:, 0:1, h * W : (h + 1) * W], axis=0)
    vec[5:6, :] = jnp.sum(got1[:, 1:2, 0:W], axis=0)

    total = vec[0:1, :]
    total_lane = vec[0:1, 0:128]
    mean_row = vec[1:2, :] / total
    stats[2:3, :] = total

    @pl.loop(0, n, unroll=8)
    def _(d):
        counts = got1[d, 1:2, 2 * W : 3 * W]
        delta[pl.ds(d, 1), :] = (got1[d, 1:2, W : 2 * W] - mean_row) * jnp.sqrt(counts)

    delta[n : n + 1, :] = got1[me, 1:2, W : 2 * W] - mean_row
    for h in range(hops):
        off = jnp.broadcast_to(delta[n : n + 1, :], (8, W))
        off = pltpu.roll(off, (W - h * width) % W, 1)[0:1, 0:128]
        tall = jnp.broadcast_to(off, (128, 128)).T[0:104, :]
        ext[GRAM : GRAM + 104, h * 128 : (h + 1) * 128] += tall * off * here_count
    span = delta.shape[0]
    span_lane = lax.broadcasted_iota(jnp.int32, (W, span), 1)
    for h in range(hops):
        here = slice(h * W, (h + 1) * W)
        wh, wl = pgh[here, 0:WIN], pgh[here, WIN : 2 * WIN]
        dh, dl = split(delta[:, win_start(h) : win_start(h) + WIN])
        apart = dot3(wh, wl, dh, dl, NT)
        between = jnp.sum(jnp.where(span_lane < n, apart * apart, 0.0), axis=1, keepdims=True)
        offset = jnp.sum(jnp.where(span_lane == n, apart, 0.0), axis=1, keepdims=True)
        spread = to_column(vec[2 + h : 3 + h, :]) + between
        inv = lax.rsqrt(spread / total_lane + 1e-05)
        stats[3 + h : 4 + h, :] = to_row(inv)
        scale = 0.5 * par[0, here, :] * inv
        par[1, here, :] = 0.5 * par[1, here, :] + scale * offset
        par[0, here, :] = scale

    def cat_copy(h, b, slot, part):
        ref = (cath, catl)[part]
        return pltpu.make_async_copy(
            ref.at[slot], cat_hbm.at[part, h, b], cat_sem.at[part, slot]
        )

    def cat_load(h, b, slot, part):
        ref = (cath, catl)[part]
        return pltpu.make_async_copy(
            cat_hbm.at[part, h, b], ref.at[slot], cat_sem.at[part, slot]
        )

    def hop_act(h, b, slot):
        for c in range(8):
            sub = slice(c * 64, (c + 1) * 64)
            here = slice(h * W + c * 64, h * W + (c + 1) * 64)
            pre = tab[pl.ds(pl.multiple_of((h * blocks + b) * W + c * 64, 64), 64), :]
            u = pre * wide(par[0, here, :]) + wide(par[1, here, :])
            t = jnp.tanh(u)
            v = u * (t + wide(par[2, here, :]) * (1.0 - t))
            t = jnp.tanh(v)
            high, low = split((v + v) * (t + wide(par[3, here, :]) * (1.0 - t)))
            cath[slot, sub, :] = high
            catl[slot, sub, :] = low

    @pl.loop(0, blocks)
    def _(b):
        at = pl.ds(pl.multiple_of(b * W, W), W)
        for h in range(hops):

            @pl.when(b > 0)
            def _():
                for part in range(2):
                    cat_copy(h, b - 1, h, part).wait()

        for h in range(hops):
            hop_act(h, b, h)
            for part in range(2):
                cat_copy(h, b, h, part).start()
            here = slice(h * W, (h + 1) * W)
            part_sum = dot3(wmh[here, :], wml[here, :], cath[h], catl[h])
            if h == 0:
                x[at, :] = part_sum
            else:
                x[at, :] += part_sum

    for h in range(hops):
        for part in range(2):
            cat_copy(h, blocks - 1, h, part).wait()

    acc[0] = jnp.zeros((W, 128), F32)

    @pl.loop(0, blocks)
    def _(b):
        at = pl.ds(pl.multiple_of(b * W, W), W)
        acc[0] += fold(x[at, :] * mask[0:1, at])

    mean_here2 = lane_sum(acc[0]) / here_count
    acc[1] = jnp.zeros((W, 128), F32)

    @pl.loop(0, blocks)
    def _(b):
        at = pl.ds(pl.multiple_of(b * W, W), W)
        off = (x[at, :] - wide(mean_here2)) * mask[0:1, at]
        acc[1] += fold(off * off)

    got2[me, 0:1, :] = to_row(mean_here2)
    got2[me, 1:2, :] = to_row(lane_sum(acc[1]))
    send_all(got2, 2)

    plain_load.wait()
    for h in range(hops):
        high, low = split(dwm[h * W : (h + 1) * W, :])
        wmh[h * W : (h + 1) * W, :] = high
        wml[h * W : (h + 1) * W, :] = low

    classes = bias.shape[1]
    kinds = 48
    ext[SMALL : SMALL + kinds, :] = jnp.zeros((kinds, W), F32)
    ext[SMALL : SMALL + classes, :] = out_t[...]
    oh, ol = split(ext[SMALL : SMALL + kinds, :])
    nh, nl = split(ext[SMALL : SMALL + kinds, :].T)
    vec[6:7, :] = jnp.zeros((1, W), F32)
    vec[6:7, 0:classes] = bias[...]
    bias_col = wide(to_column(vec[6:7, 0:128])[0:kinds, :])

    wait_all(got2, 2)
    every_count = got1[:, 1:2, 2 * W : 3 * W]
    mean2 = jnp.sum(got2[:, 0:1, :] * every_count, axis=0) / total
    off = got2[:, 0:1, :] - mean2
    vec[3:4, :] = jnp.sum(got2[:, 1:2, :] + off * off * every_count, axis=0)
    inv2 = lax.rsqrt(vec[3:4, :] / total + 1e-05)
    mcol[3] = to_column(mean2)
    mcol[4] = to_column(inv2)
    mcol[2] = 0.5 + 0.5 * mcol[2]

    for b in range(blocks):
        for part in range(2):
            cat_load(0, b, b % 4, part).start()

    for j in range(4):
        acc[j] = jnp.zeros((W, 128), F32)
    ext[SMALL : SMALL + 64, :] = jnp.zeros((64, W), F32)
    kind = lax.broadcasted_iota(jnp.int32, (kinds, W), 0)

    @pl.loop(0, blocks)
    def _(b):
        at = pl.ds(pl.multiple_of(b * W, W), W)
        live = mask[0:1, at]
        normed = (x[at, :] - wide(mcol[3])) * wide(mcol[4])
        v = 0.5 * (normed * wide(mcol[0]) + wide(mcol[1]))
        t = jnp.tanh(v)
        keep = wide(mcol[2])
        rest = 1.0 - t
        ah, al = split((v + v) * (t + keep * rest))
        q = v * rest
        logits = dot3(oh, ol, ah, al) + bias_col
        logits = jnp.where(kind < classes, logits, -1e30)
        top = jnp.max(logits, axis=0, keepdims=True)
        e = jnp.exp(logits - top)
        norm = jnp.sum(e, axis=0, keepdims=True)
        logp = logits - top - jnp.log(norm)
        hit = kind == lab[0:1, at]
        loss = jnp.sum(jnp.where(hit, logp, 0.0), axis=0, keepdims=True) * live
        back = (e / norm - jnp.where(hit, 1.0, 0.0)) * (live / total)
        bh, bl = split(back)
        ext[SMALL : SMALL + kinds, :] += dot3(bh, bl, ah, al, NT)
        ext[SMALL + 49 : SMALL + 50, :] -= loss
        acc[3, 0:kinds, :] += fold(back)
        grad = dot3(nh, nl, bh, bl)
        acc[0] += fold(grad * q)
        m = t + q + q * t
        grad = grad * (m + keep * (1.0 - m))
        dwm[at, :] = grad
        acc[1] += fold(grad)
        acc[2] += fold(grad * normed)

    ext[SMALL + 48 : SMALL + 49, :] = to_row(lane_sum(acc[0]))
    ext[SMALL + 50 : SMALL + 51, 0:128] = to_row(lane_sum(acc[3])[0:128, :])
    got3[me, 0:1, :] = to_row(lane_sum(acc[1]))
    got3[me, 1:2, :] = to_row(lane_sum(acc[2]))
    send_all(got3, 3)
    wait_all(got3, 3)
    vec[2:4, :] = jnp.sum(got3[...], axis=0)
    stats[0:2, :] = vec[2:4, :]
    shift_part = to_column(vec[2:3, :] / total)
    gain_part = to_column(vec[3:4, :] / total)
    factor = mcol[0] * mcol[4]

    @pl.loop(0, blocks)
    def _(b):
        at = pl.ds(pl.multiple_of(b * W, W), W)
        normed = (x[at, :] - wide(mcol[3])) * wide(mcol[4])
        grad = dwm[at, :] - wide(shift_part) - normed * wide(gain_part)
        high, low = split(grad * wide(factor) * mask[0:1, at])
        pgh[at, :] = high
        pgl[at, :] = low

    bits = n.bit_length() - 1

    def bit_of(b):
        return lax.rem(me // (1 << b), 2)

    def across(b):
        return me + (1 << b) * (1 - 2 * bit_of(b))

    def remote(src, dst, send, recv, to):
        return pltpu.make_async_remote_copy(
            src, dst, send, recv, device_id=(to,), device_id_type=MESH
        )

    def wait_bytes(ref, sem):
        pltpu.make_async_copy(ref, ref, sem).wait()

    for b in range(bits):
        pl.semaphore_signal(credit, inc=1, device_id=(across(b),), device_id_type=MESH)

    far = list(range(3, bits))
    orders = [[1, 2] + far, [2, 1] + far, [1] + far + [2], [2] + far + [1]]
    span = W // len(orders)

    def halving(batch, base, size, take):
        def rows_at(off, length):
            return pl.ds(pl.multiple_of(off, 8), length)

        half = size // 2
        tmps = [take(half)]
        levels = [
            [(0, slice(0, W), base + bit_of(0) * half, base + (1 - bit_of(0)) * half, half, tmps[0][1])]
        ]
        rest_tmp, at = take(half)
        tmps += [(rest_tmp, at)] * (bits - 1)
        offs = [base + bit_of(0) * half] * len(orders)
        length = half
        for j in range(bits - 1):
            length //= 2
            level = []
            for q in range(len(orders)):
                b = orders[q][j]
                keep = offs[q] + bit_of(b) * length
                give = offs[q] + (1 - bit_of(b)) * length
                level.append((b, slice(q * span, (q + 1) * span), keep, give, length, at))
                offs[q] = keep
            at += length
            levels.append(level)

        stages = []
        for k, level in enumerate(levels):
            send, recv = sum_send.at[batch, k], sum_recv.at[batch, k]
            free = freed.at[batch, k]
            length, first = level[0][4:]
            tmp = tmps[k][0]
            arrived = tmp.at[first : first + length, :]

            def start(level=level, send=send, recv=recv, tmp=tmp):
                for b, lanes, keep, give, ln, t in level:
                    remote(
                        dwm.at[rows_at(give, ln), lanes], tmp.at[t : t + ln, lanes],
                        send, recv, across(b),
                    ).start()

            def finish(level=level, send=send, recv=recv, free=free, arrived=arrived, tmp=tmp):
                wait_bytes(arrived, send)
                wait_bytes(arrived, recv)
                for b, lanes, keep, give, ln, t in level:
                    pl.semaphore_signal(
                        free, inc=1, device_id=(across(b),), device_id_type=MESH
                    )
                    dwm[rows_at(keep, ln), lanes] += tmp[t : t + ln, lanes]

            stages.append((start, finish))
        for k in range(bits - 1, -1, -1):
            level = levels[k]
            send, recv = sum_send.at[batch, bits + k], sum_recv.at[batch, bits + k]
            free = freed.at[batch, k]
            length, first = level[0][4:]
            arrived = tmps[k][0].at[first : first + length, :]

            def start(level=level, send=send, recv=recv, free=free):
                pl.semaphore_wait(free, len(level))
                for b, lanes, keep, give, ln, t in level:
                    here = dwm.at[rows_at(keep, ln), lanes]
                    remote(here, here, send, recv, across(b)).start()

            def finish(send=send, recv=recv, arrived=arrived):
                wait_bytes(arrived, send)
                wait_bytes(arrived, recv)

            stages.append((start, finish))
        return stages

    chips = n // 2
    core, chip = lax.rem(me, 2), me // 2
    half_lanes = W // 2
    mine = pl.ds(pl.multiple_of(core * half_lanes, 128), half_lanes)
    other = pl.ds(pl.multiple_of((1 - core) * half_lanes, 128), half_lanes)

    def direct(batch, base, size, rows_each, tmp_base, tmp_lane):
        owners = size // rows_each
        cols = slice(tmp_lane, tmp_lane + half_lanes)
        block = pl.ds(base, size)
        from_core = tab.at[tmp_base : tmp_base + size, cols]
        first = tmp_base + size
        slot = tab.at[pl.ds(pl.multiple_of(first + chip * rows_each, 8), rows_each), cols]
        summed = own.at[batch, 0:rows_each, :]
        sends = [part_send.at[batch, k] for k in range(4)]
        recvs = [part_recv.at[batch, k] for k in range(4)]

        def many(k):
            return tab.at[first : first + rows_each * k, cols]

        def piece(q):
            return pl.ds(pl.multiple_of(base + q * rows_each, 8), rows_each)

        def start():
            remote(ext.at[block, other], from_core, sends[0], recvs[0], across(0)).start()

        def spread():
            wait_bytes(from_core, sends[0])
            wait_bytes(from_core, recvs[0])
            ext[block, mine] += tab[tmp_base : tmp_base + size, cols]

            @pl.loop(0, owners)
            def _(k):
                q = lax.rem(chip + k, owners)

                @pl.when(q == chip)
                def _():
                    pltpu.make_async_copy(ext.at[piece(q), mine], slot, recvs[1]).start()

                @pl.when(q != chip)
                def _():
                    remote(ext.at[piece(q), mine], slot, sends[1], recvs[1], q * 2 + core).start()

        def middle():
            @pl.when(chip < owners)
            def _():
                wait_bytes(many(owners - 1), sends[1])
                wait_bytes(many(chips), recvs[1])
                out = tab[first : first + rows_each, cols]
                for d in range(1, chips):
                    at = first + rows_each * d
                    out = out + tab[at : at + rows_each, cols]
                own[batch, 0:rows_each, :] = out
                there = res.at[piece(chip), mine]
                pltpu.make_async_copy(summed, there, recvs[2]).start()

                @pl.loop(1, chips)
                def _(k):
                    to = lax.rem(chip + k, chips) * 2 + core
                    remote(summed, there, sends[2], recvs[2], to).start()

            @pl.when(chip >= owners)
            def _():
                wait_bytes(many(owners), sends[1])

        def join():
            wait_bytes(res.at[block, mine], recvs[2])

            @pl.when(chip < owners)
            def _():
                wait_bytes(many(chips - 1), sends[2])

            here = res.at[block, mine]
            remote(here, here, sends[3], recvs[3], across(0)).start()

        def finish():
            wait_bytes(res.at[block, other], sends[3])
            wait_bytes(res.at[block, other], recvs[3])

        return [start, spread, middle, join, finish]

    mid_batch = max(W, 8 * n)
    mids = hops * W // mid_batch
    DW, HB, GAP = 1.0, 2.1, 4.5
    PART = (4.2, 6.3, 6.3, 4.2)
    clock = [(t + 1) * DW for t in range(hops * blocks)]
    clock += [clock[-1] + (t + 1) * HB for t in range(hops * blocks)]
    spare = hops * rows
    part_rows = 208 + 16 * chips
    spots = [(x, W, x.shape[0] - W), (tab, spare + part_rows, tab.shape[0] - spare - part_rows)]

    def take(size):
        spot = next(i for i in range(2) if spots[i][2] >= size)
        ref, first, left = spots[spot]
        spots[spot] = (ref, first + size, left - size)
        return ref, first

    events = []
    for k in range(mids):
        stages = halving(k, k * mid_batch, mid_batch, take)
        when = clock[(k + 1) * mid_batch // W * blocks - 1]
        for j in range(len(stages) + 1):
            todo = []
            if j:
                todo.append(stages[j - 1][1])
            elif k == 0:
                todo.append(lambda: pl.semaphore_wait(credit, bits))
            if j < len(stages):
                todo.append(stages[j][0])
            else:
                todo.append(lambda k=k: mid_out(k).start())
            events.append((when, len(events), todo))
            when += GAP
    ends = [clock[hops * blocks + (h + 1) * blocks - 1] for h in range(hops)]
    for batch, (when, base, size, rows_each) in enumerate(
        (
            (clock[0], 0, HOPS_AT, 16),
            (ends[1], hop_row(0), 208, 16),
            (ends[2], hop_row(2), 104, 8),
            (ends[3], hop_row(3), 104, 8),
        )
    ):
        stages = direct(batch, base, size, rows_each, spare, batch % 2 * half_lanes)
        for j, stage in enumerate(stages):
            at = when + sum(PART[:j])
            if batch == 1:
                at = min(at, ends[3] - 1e-3)
            events.append((at, len(events), [stage]))

    ticks = {}
    for when, _, todo in sorted(events, key=lambda e: e[:2]):
        tick = next((t for t, c in enumerate(clock) if c >= when - 1e-6), len(clock))
        ticks.setdefault(tick, []).extend(todo)

    def mid_out(k):
        here = slice(k * mid_batch, (k + 1) * mid_batch)
        return pltpu.make_async_copy(dwm.at[here], mid_sum.at[here], table_sem.at[k])

    def act(tick):
        for todo in ticks.get(tick, []):
            todo()

    for h in range(hops):
        here = slice(h * W, (h + 1) * W)

        @pl.loop(0, blocks)
        def _(b):
            at = pl.ds(pl.multiple_of(b * W, W), W)
            slot = lax.rem(b, 4)
            for part in range(2):
                cat_load(h, b, slot, part).wait()
            part_sum = dot3(cath[slot], catl[slot], pgh[at, :], pgl[at, :], NT)
            if h + 1 < hops:
                for part in range(2):
                    cat_load(h + 1, b, slot, part).start()

            @pl.when(b == 0)
            def _():
                dwm[here, :] = part_sum

            @pl.when(b > 0)
            def _():
                dwm[here, :] += part_sum

            for t in range(blocks):
                if ticks.get(h * blocks + t):

                    @pl.when(b == t)
                    def _():
                        act(h * blocks + t)

    grads = (x.at[0:W], cg)

    def head_back(h, b, rs):
        at = pl.ds(b * W, W)
        here = pl.ds(pl.multiple_of(h * W + rs.start, 128), rs.stop - rs.start)
        return dot3(wmh[here, :], wml[here, :], pgh[at, :], pgl[at, :])

    def weight_back(h, b, rs):
        window = pl.ds(pl.multiple_of(jnp.maximum(h - 1, 0) * 128, 128), WIN)
        at = pl.ds(b * W, W)
        part_sum = dot3(
            cath[b % 2, rs, :], catl[b % 2, rs, :], xh[window, at], xl[window, at], NT
        )
        if b == 0:
            hop_grad[rs, :] = part_sum
        else:
            hop_grad[rs, :] += part_sum

    def act_back(h, b, c):
        sub = slice(c * 64, (c + 1) * 64)
        col = pl.ds(pl.multiple_of(h * W + c * 64, 64), 64)
        grad = grads[b % 2][sub, :]
        pre = tab[pl.ds(pl.multiple_of((h * blocks + b) * W + c * 64, 64), 64), :]
        keep1, keep2 = wide(par[2, col, :]), wide(par[3, col, :])
        u = pre * wide(par[0, col, :]) + wide(par[1, col, :])
        t1 = jnp.tanh(u)
        r1 = 1.0 - t1
        v = u * (t1 + keep1 * r1)
        t2 = jnp.tanh(v)
        q = v * (1.0 - t2)
        sum2 = fold(grad * q)
        m = t2 + q + q * t2
        grad = grad * (m + keep2 * (1.0 - m))
        q = u * r1
        sum1 = fold(grad * q)
        m = t1 + q + q * t1
        grad = grad * (m + keep1 * (1.0 - m))
        for j, value in enumerate((sum2, sum1, fold(grad))):
            if b == 0:
                acc[j, sub, :] = value
            else:
                acc[j, sub, :] += value
        high, low = split(grad)
        cath[b % 2, sub, :] = high
        catl[b % 2, sub, :] = low

    halves = (slice(0, W // 2), slice(W // 2, W))
    grads[0][...] = head_back(0, 0, slice(0, W))

    @pl.loop(0, hops)
    def _(h):
        for b in range(blocks):
            for m, rs in enumerate(halves):
                if b + 1 < blocks:
                    grads[(b + 1) % 2][rs, :] = head_back(h, b + 1, rs)
                else:
                    grads[(b + 1) % 2][rs, :] = head_back(jnp.minimum(h + 1, hops - 1), 0, rs)
                if b:
                    weight_back(h, b - 1, rs)
                for c in range(4 * m, 4 * m + 4):
                    act_back(h, b, c)
            if b + 1 < blocks:
                for t in range(hops):
                    if ticks.get(hops * blocks + t * blocks + b):

                        @pl.when(h == t)
                        def _():
                            act(hops * blocks + t * blocks + b)

        weight_back(h, blocks - 1, slice(0, W))
        for t in range(hops):

            @pl.when(h == t)
            def _():
                sums = lane_sum(acc[2])
                offset = delta[n : n + 1, win_start(t) : win_start(t) + WIN]
                tall = hop_grad[...] + jnp.concatenate([sums] * 2, axis=1) * offset
                first = hop_row(t)
                start = t * width - win_start(t)
                cg[0:WIN, :] = tall.T
                ext[first : first + width, :] = cg[start : start + width, :]
                for j in range(3):
                    row = first + width + j
                    ext[row : row + 1, :] = to_row(lane_sum(acc[j]))
                act(hops * blocks + t * blocks + blocks - 1)

    act(len(clock))
    rest_out = pltpu.make_async_copy(res, rest_sum, load_sem.at[0])
    rest_out.start()
    for k in range(mids):
        mid_out(k).wait()
    rest_out.wait()


GRAM, SMALL, HOPS_AT = 0, 104, 176


def hop_row(h):
    return HOPS_AT + h * 104


def final_kernel(
    mid_sum, rest_sum, stats_sum, weights_in, gain, loss, hop_w, hop_g, hop_s, hop_l, cat_l, mid_w,
    mid_g, mid_s, mid_l, out_w, out_b, buf, wide_w, rest, stats, weights, sem,
):
    parts = 4
    size = mid_sum.shape[0] // parts

    def load(k):
        here = slice(k * size, (k + 1) * size)
        return pltpu.make_async_copy(mid_sum.at[here], buf.at[here], sem.at[0, k])

    def store(k):
        here = slice(k * size, (k + 1) * size)
        return pltpu.make_async_copy(buf.at[here], mid_w.at[here], sem.at[1, k])

    loads = [
        pltpu.make_async_copy(src, dst, sem.at[2, k])
        for k, (src, dst) in enumerate(((rest_sum, rest), (stats_sum, stats), (weights_in, weights)))
    ]
    for copy in loads:
        copy.start()
    for k in range(parts):
        load(k).start()
    for copy in loads:
        copy.wait()
    total = stats[2:3, :]
    width, hops, _ = weights.shape
    wide_w[...] = jnp.zeros_like(wide_w)
    for h in range(hops):
        first = hop_row(h)
        raw = rest[first : first + width, :]
        weight = weights[:, h, :]
        inv = stats[3 + h : 4 + h, :]
        gain_grad = inv * jnp.sum(weight * raw, axis=0, keepdims=True)
        wide_w[0:width, :] = weight
        along = lax.dot_general(
            rest[GRAM : GRAM + 104, h * 128 : (h + 1) * 128], wide_w[...], NN,
            precision=lax.Precision.HIGHEST, preferred_element_type=F32,
        )[0:width, :]
        grad = raw - along * (inv * gain_grad / total)
        hop_w[:, h, :] = gain[h : h + 1, :] * inv * grad
        hop_g[h : h + 1, :] = gain_grad
        cat_l[0:1, h * W : (h + 1) * W] = rest[first + width : first + width + 1, :]
        hop_l[h : h + 1, :] = rest[first + width + 1 : first + width + 2, :]
        hop_s[h : h + 1, :] = rest[first + width + 2 : first + width + 3, :]
        load(h).wait()
        store(h).start()
    mid_s[...] = stats[0:1, :]
    mid_g[...] = stats[1:2, :]
    mid_l[...] = rest[SMALL + 48 : SMALL + 49, :]
    out_w[...] = rest[SMALL : SMALL + out_w.shape[0], :]
    out_b[...] = rest[SMALL + 50 : SMALL + 51, 0 : out_b.shape[1]]
    loss[...] = jnp.sum(rest[SMALL + 49 : SMALL + 50, :], axis=1, keepdims=True) / total[:, 0:1]
    for k in range(parts):
        store(k).wait()


def on_device(
    node_table, batch_nodes, send_counts, labels, hop_weight, hop_gain, hop_shift, hop_slope,
    cat_slope, mid_weight, mid_gain, mid_shift, mid_slope, out_weight, out_bias,
):
    n = lax.axis_size("nodes")
    node_rows, feats = node_table.shape
    rows = batch_nodes.shape[0]
    slots = rows // n
    hops, width, units = hop_weight.shape
    blocks = rows // W
    classes = out_weight.shape[1]
    vmem = pl.BlockSpec(memory_space=pltpu.VMEM)
    hbm = pl.BlockSpec(memory_space=pl.ANY)
    shape = jax.ShapeDtypeStruct
    bits = n.bit_length() - 1
    mid_batch = max(W, 8 * n)
    sums = hops * W // mid_batch
    small_rows = HOPS_AT + 104 * hops
    halves = 2 * sums - (hops * W - W) // (mid_batch // 2)
    spill = 208 + 8 * n + halves * mid_batch // 2
    tab_rows = max(node_rows, hops * rows + spill)
    weights = hop_weight.transpose(1, 0, 2)
    mid_sum, rest_sum, stats, _ = pl.pallas_call(
        functools.partial(main_kernel, n, slots),
        out_shape=(
            shape((hops * units, W), F32),
            shape((small_rows, W), F32),
            shape((8, W), F32),
            shape((2, hops, blocks, W, W), BF16),
        ),
        in_specs=[hbm, vmem, vmem, pl.BlockSpec(memory_space=pltpu.SMEM), vmem, hbm] + [vmem] * 9,
        out_specs=(hbm, hbm, vmem, hbm),
        scratch_shapes=[
            pltpu.VMEM((tab_rows, 512), F32),
            pltpu.VMEM((max(rows, hops * W), W), F32),
            pltpu.VMEM((max(rows, hops * W), W), F32),
            pltpu.VMEM((512, rows), BF16),
            pltpu.VMEM((512, rows), BF16),
            pltpu.VMEM((hops * W, W), BF16),
            pltpu.VMEM((hops * W, W), BF16),
            pltpu.VMEM((max(rows, hops * W), W), BF16),
            pltpu.VMEM((max(rows, hops * W), W), BF16),
            pltpu.VMEM((4, W, W), BF16),
            pltpu.VMEM((4, W, W), BF16),
            pltpu.VMEM((4, hops * W, 128), F32),
            pltpu.VMEM((5, W, 128), F32),
            pltpu.VMEM((4, W, 128), F32),
            pltpu.VMEM((8, W), F32),
            pltpu.VMEM((1, rows), F32),
            pltpu.VMEM((1, rows), jnp.int32),
            pltpu.VMEM((n + 8, W), F32),
            pltpu.VMEM((small_rows, W), F32),
            pltpu.VMEM((small_rows, W), F32),
            pltpu.VMEM((4, 16, W // 2), F32),
            pltpu.VMEM((W, WIN), F32),
            pltpu.VMEM((W, W), F32),
            pltpu.SMEM((n, 2, 128), jnp.int32),
            pltpu.VMEM((n, 2, 128), jnp.int32),
            pltpu.VMEM((n, 2, 128), jnp.int32),
            pltpu.VMEM((n, 2, 3 * W), F32),
            pltpu.VMEM((n, 2, W), F32),
            pltpu.VMEM((n, 2, W), F32),
            pltpu.SemaphoreType.DMA((4,)),
            pltpu.SemaphoreType.DMA((4,)),
            pltpu.SemaphoreType.DMA((sums, 2 * bits)),
            pltpu.SemaphoreType.DMA((sums, 2 * bits)),
            pltpu.SemaphoreType.DMA((4, 4)),
            pltpu.SemaphoreType.DMA((4, 4)),
            pltpu.SemaphoreType.REGULAR,
            pltpu.SemaphoreType.REGULAR((sums, bits)),
            pltpu.SemaphoreType.DMA((8,)),
            pltpu.SemaphoreType.DMA((2,)),
            pltpu.SemaphoreType.DMA((2, 4)),
        ],
        compiler_params=pltpu.CompilerParams(
            collective_id=0, has_side_effects=True, vmem_limit_bytes=66_900_000
        ),
    )(
        node_table.T, batch_nodes.reshape(rows // 128, 128), labels.reshape(rows // 128, 128),
        send_counts, weights, mid_weight, hop_gain, hop_shift, hop_slope,
        cat_slope.reshape(1, hops * units), mid_gain.reshape(1, W), mid_shift.reshape(1, W),
        mid_slope.reshape(1, W), out_weight.T, out_bias.reshape(1, classes),
    )
    (
        loss, hop_w, hop_g, hop_s, hop_l, cat_l, mid_w, mid_g, mid_s, mid_l, out_w, out_b,
    ) = pl.pallas_call(
        final_kernel,
        out_shape=(
            shape((1, 1), F32), shape((width, hops, units), F32), shape((hops, units), F32),
            shape((hops, units), F32), shape((hops, units), F32), shape((1, hops * units), F32),
            shape((hops * units, W), F32), shape((1, W), F32), shape((1, W), F32),
            shape((1, W), F32), shape((classes, W), F32), shape((1, classes), F32),
        ),
        in_specs=[hbm] * 4 + [vmem],
        out_specs=(vmem,) * 6 + (hbm,) + (vmem,) * 5,
        scratch_shapes=[
            pltpu.VMEM((hops * units, W), F32),
            pltpu.VMEM((128, W), F32),
            pltpu.VMEM((small_rows, W), F32),
            pltpu.VMEM((8, W), F32),
            pltpu.VMEM((width, hops, units), F32),
            pltpu.SemaphoreType.DMA((3, 4)),
        ],
        compiler_params=pltpu.CompilerParams(vmem_limit_bytes=62 * 2**20),
    )(mid_sum, rest_sum, stats, weights, hop_gain)
    return (
        loss.reshape(()), hop_w.transpose(1, 0, 2), hop_g, hop_s, hop_l, cat_l.reshape(-1),
        mid_w, mid_g.reshape(-1), mid_s.reshape(-1), mid_l.reshape(-1), out_w.T,
        out_b.reshape(-1),
    )


def solution(mesh):
    placed = (P("nodes", None), P("nodes"), P("nodes", None), P("nodes")) + (P(),) * 11
    return jax.shard_map(
        on_device, mesh=mesh, in_specs=placed, out_specs=(P(),) * 12, check_vma=False
    )
```
